32 devices in a mesh: member: 2 (over core), comp: 2 (over y), tile: 8 (over z, x).
Axes of the slice: x: 2, y: 2, z: 4, core: 2. Of those that a mesh axis runs over, the one named last changes fastest.
Arguments:
- member_state: float32 [4, 2, 4, 4, 384, 768], P('member', 'comp', None, None, 'tile'), may hold values from -6 to 6
- layer_blend_operator: float32 [2, 4, 4], P('comp'), may hold values from -3 to 3
- coefficient: float32 [2, 4], P('comp'), may hold values from 0.05 to 0.24
- interpolation_donor_meridians: int32 [2, 384, 768], P('comp', 'tile'), may hold values from 0 to 767, as said below
- land_sea: int32 [384, 768], P('tile'), may hold values 0 or 1
- ancestry: int32 [4], replicated, may hold values from 0 to 3, as said below
Outputs:
- cloned: float32 [4, 2, 4, 4, 384, 768], P('member', 'comp', None, None, 'tile')
- region_score: float32 [4, 2], P('member', 'comp')
The draws below stay inside these ranges and needn't reach their ends.
Inputs may be any that keep to these rules, and one draw needn't show every extreme that they name: interpolation_donor_meridians[c, j, x] is a longitude from one cell west to four cells east of x, cyclically. `ancestry`: slot 0 has a parent among slots 2 and above, slot 2 one below 2.
All inputs are finite; a program needn't handle non-finite values. No bound on the sum of `land_sea` on one device may be relied on, other than what follows from the above.
Results may differ from the reference program's by a relative error of at most 0.00014.
Values sent between devices are 32-bit elements; how exact they have to be, the bound alone decides.
A program may use at most 128 MiB of HBM per device.

```python
import math
import jax
import jax.numpy as jnp
from jax import lax

F = 4
LEV = 4
LAT = 384
LON = 768
MODES = 256
STEPS = 2
SLOTS_DEV = 2
MEMBERS = 4


def draw_interpolation_donor_meridians(key, part):
    first_key, second_key = jax.random.split(jax.random.fold_in(key, 11))
    offset = jax.random.randint(first_key, (2, LAT, 1), 0, 4)
    jitter = jax.random.randint(second_key, (2, LAT, LON), -1, 2)
    cells = jnp.arange(LON, dtype=jnp.int32)[None, None, :]
    return jnp.mod(cells + offset + jitter, LON).astype(jnp.int32)


def draw_ancestry(key, part):
    base_key, upper_key, lower_key = jax.random.split(jax.random.fold_in(key, 23), 3)
    parents = jax.random.randint(base_key, (MEMBERS,), 0, MEMBERS)
    upper = jax.random.randint(upper_key, (), SLOTS_DEV, MEMBERS)
    lower = jax.random.randint(lower_key, (), 0, SLOTS_DEV)
    parents = parents.at[0].set(upper).at[SLOTS_DEV].set(lower)
    return parents.astype(jnp.int32)


def set_ends(result, rng, low, largest):
    longest = result.shape.index(max(result.shape))
    spots = []
    for shift in (0, 1):
        where = [jax.random.randint(jax.random.fold_in(rng, axis), (), 0, length) for axis, length in enumerate(result.shape)]
        where[longest] = (where[longest] + shift) % result.shape[longest]
        spots.append(tuple(where))
    return result.at[spots[0]].set(low).at[spots[1]].set(largest)


def steps_of(stream_key, extent, cuts, least, high):
    def one(axis_at, parts):
        heights = jax.random.uniform(jax.random.fold_in(jax.random.fold_in(stream_key, 6), axis_at), (parts,), jnp.float32, least / len(cuts), high / len(cuts))
        return jnp.repeat(jnp.exp(heights), extent[axis_at] // parts).reshape((-1,) + (1,) * (len(extent) - axis_at - 1))

    loudness = one(*cuts[0])
    for cut in cuts[1:]:
        loudness = loudness * one(*cut)
    return loudness


def centred(own_key, shape, width, reach, cuts=(), held_as=jnp.bfloat16):
    result = jax.random.normal(own_key, shape, jnp.float32) * width
    if len(cuts) > 0:
        result = steps_of(own_key, shape, cuts, -0.22, 0.18) * result
    return jnp.clip(result, min=-reach, max=reach).astype(held_as)


def setup_inputs(seed: int = 0) -> dict:
    streams_of = jax.random.split(jax.random.key(seed), 7)
    member_state = centred(streams_of[0], (MEMBERS, 2, F, LEV, LAT, LON), 1.0, 6.0, ((0, 2), (1, 2), (4, 8)), jnp.float32)
    layer_blend_operator = centred(streams_of[1], (2, LEV, LEV), LEV ** -0.5, 3.0, ((0, 2),), jnp.float32)
    coefficient = jnp.clip(jnp.exp(math.log(0.24) - 1.5686159 * jax.random.uniform(streams_of[2], (2, F), jnp.float32) ** steps_of(streams_of[2], (2, F), ((0, 2),), -0.2, 0.2)), 0.05, 0.24)
    interpolation_donor_meridians = draw_interpolation_donor_meridians(jax.random.fold_in(streams_of[6], 71), 0)
    land_sea = set_ends((jax.random.randint(streams_of[4], (LAT, LON), 0, 4) < 3).astype(jnp.int32), jax.random.fold_in(streams_of[4], 1), 0, 1)
    ancestry = draw_ancestry(jax.random.fold_in(streams_of[6], 71), 0)
    return {"member_state": member_state, "layer_blend_operator": layer_blend_operator, "coefficient": coefficient, "interpolation_donor_meridians": interpolation_donor_meridians, "land_sea": land_sea, "ancestry": ancestry}


coupling_rate = 0.5
forcing_rate = 0.5

def kept_lon_basis():
    wave = jnp.arange(2 * MODES, dtype=jnp.int32)
    is_cosine = wave < MODES
    number = jnp.where(is_cosine, wave, wave - MODES + 1).astype(jnp.float32)
    cells = jnp.arange(LON, dtype=jnp.int32).astype(jnp.float32)
    angle = 2.0 * math.pi * number[:, None] * cells[None, :] / LON
    scale = jnp.where(number == 0.0, math.sqrt(1.0 / LON), math.sqrt(2.0 / LON)).astype(jnp.float32)
    table = jnp.where(is_cosine[:, None], jnp.cos(angle), jnp.sin(angle)) * scale[:, None]
    return (table, number)

def lat_table():
    order = jnp.arange(MODES, dtype=jnp.int32).astype(jnp.float32)
    cells = jnp.arange(LAT, dtype=jnp.int32).astype(jnp.float32)
    scale = jnp.where(order == 0.0, math.sqrt(1.0 / LAT), math.sqrt(2.0 / LAT)).astype(jnp.float32)
    return jnp.cos(math.pi * (cells[None, :] + 0.5) * order[:, None] / LAT) * scale[:, None]

def boundary_tendency_input(field, mixing_matrix, received):
    mixing = jnp.einsum('uv,fvjx->fujx', mixing_matrix, field, precision=lax.Precision.HIGHEST)
    forced = field + forcing_rate * jnp.tanh(mixing)
    return forced.at[0, 0].add(coupling_rate * (received - field[0, 0]))

def laplacian(field):
    padded = jnp.pad(field, ((0, 0), (0, 0), (1, 1), (0, 0)))
    return padded[:, :, 2:] + padded[:, :, :-2] + jnp.roll(field, 1, axis=3) + jnp.roll(field, -1, axis=3) - 4.0 * field

def reference(member_state, layer_blend_operator, coefficient, interpolation_donor_meridians, land_sea, ancestry):
    highest = lax.Precision.HIGHEST
    lon_basis, number = kept_lon_basis()
    lat_basis = lat_table()
    order = jnp.arange(MODES, dtype=jnp.int32).astype(jnp.float32)
    spectral_gain = 1.0 / (1.0 + coefficient[0][:, None, None] * (order[None, None, :] ** 2 + number[None, :, None] ** 2) / (MODES * MODES))
    rows = jnp.arange(LAT, dtype=jnp.int32).astype(jnp.float32)
    weights = jnp.cos(math.pi * ((rows + 0.5) / LAT - 0.5))
    stepped_slots = []
    scores = []
    for slot in range(MEMBERS):
        air_model_snapshot = member_state[slot, 0]
        ocean = member_state[slot, 1]
        for step_index in range(STEPS):
            surface_atm = air_model_snapshot[0, 0]
            marine_top_layer = ocean[0, 0]
            marine_heat_upon_air_grid = jnp.take_along_axis(marine_top_layer, interpolation_donor_meridians[0], axis=1)
            flux_on_ocn = jnp.take_along_axis(surface_atm, interpolation_donor_meridians[1], axis=1)
            driven_air_model = boundary_tendency_input(air_model_snapshot, layer_blend_operator[0], marine_heat_upon_air_grid)
            forced_ocn = boundary_tendency_input(ocean, layer_blend_operator[1], flux_on_ocn)
            fourier = jnp.einsum('fvjx,qx->fvjq', driven_air_model, lon_basis, precision=highest)
            spectrum = jnp.einsum('lj,fvjq->fvql', lat_basis, fourier, precision=highest)
            spectrum = spectrum * spectral_gain[:, None]
            fourier = jnp.einsum('lj,fvql->fvjq', lat_basis, spectrum, precision=highest)
            new_atm = jnp.einsum('fvjq,qx->fvjx', fourier, lon_basis, precision=highest)
            diffused = forced_ocn + coefficient[1][:, None, None, None] * laplacian(ocean)
            ocean = jnp.where(land_sea[None, None] == 1, diffused, ocean)
            air_model_snapshot = new_atm
        pair = jnp.stack([air_model_snapshot, ocean])
        stepped_slots.append(pair)
        surfaces = pair[:, 0, 0]
        row_means = lax.optimization_barrier(jnp.mean(surfaces, axis=2))
        scores.append(lax.optimization_barrier(jnp.sum(row_means * weights[None, :], axis=1)) / jnp.sum(weights))
    stepped = jnp.stack(stepped_slots)
    cloned = jnp.take(stepped, ancestry, axis=0)
    return (cloned, jnp.stack(scores))
```

```python
import functools
import math

import jax
import jax.numpy as jnp
import numpy as np
from jax import lax
from jax.experimental import pallas as pl
from jax.experimental.pallas import tpu as pltpu
from jax.sharding import PartitionSpec as P

LAT = 384
MODES = 256
STEPS = 2
MESH = pl.DeviceIdType.MESH


coupling_rate = 0.5
forcing_rate = 0.5
precise = lax.Precision.HIGH


def partner_2(value, axis, distance):
    mask = 2**distance
    pairs = [(source, source ^ mask) for source in range(lax.axis_size(axis))]
    return lax.ppermute(value, axis, pairs)


def padded_2(block, sides, width):
    for axis, dim in sides:
        count = lax.axis_size(axis)
        forward = [(i, i + 1) for i in range(count - 1)]
        backward = [(target, source) for source, target in forward]
        low = lax.ppermute(
            lax.slice_in_dim(block, block.shape[dim] - width, None, axis=dim), axis, forward
        )
        high = lax.ppermute(lax.slice_in_dim(block, 0, width, axis=dim), axis, backward)
        block = jnp.concatenate([low, block, high], axis=dim)
    return block


def kept_lon_basis(lon_count):
    wave = np.arange(2 * MODES)
    is_cosine = wave < MODES
    number = np.where(is_cosine, wave, wave - MODES + 1).astype(np.float32)
    cells = np.arange(lon_count).astype(np.float32)
    angle = np.float32(2.0 * math.pi) * number[:, None] * cells[None, :] / np.float32(lon_count)
    scale = np.where(number == 0.0, math.sqrt(1.0 / lon_count), math.sqrt(2.0 / lon_count)).astype(
        np.float32
    )
    table = np.where(is_cosine[:, None], np.cos(angle), np.sin(angle)) * scale[:, None]
    return table.astype(np.float32), number


def lat_table():
    order = np.arange(MODES).astype(np.float32)
    cells = np.arange(LAT).astype(np.float32)
    scale = np.where(order == 0.0, math.sqrt(1.0 / LAT), math.sqrt(2.0 / LAT)).astype(np.float32)
    angle = np.float32(math.pi) * (cells[None, :] + np.float32(0.5)) * order[:, None]
    return (np.cos(angle / np.float32(LAT)) * scale[:, None]).astype(np.float32)


def row_weights():
    rows = np.arange(LAT).astype(np.float32)
    return np.cos(
        np.float32(math.pi) * ((rows + np.float32(0.5)) / np.float32(LAT) - np.float32(0.5))
    ).astype(np.float32)


def donor_lookup(partner, donors):
    lon_count = partner.shape[-1]
    cells = jnp.arange(lon_count, dtype=jnp.int32)[None, :]
    offsets = jnp.mod(donors - cells, lon_count)
    result = jnp.zeros_like(partner)
    for shift_by in (-1, 0, 1, 2, 3, 4):
        moved = jnp.roll(partner, -shift_by, axis=-1)
        result = result + jnp.where(offsets == shift_by % lon_count, moved, 0.0)
    return result


def remote(src, dst, send_sem, recv_sem, device):
    return pltpu.make_async_remote_copy(
        src_ref=src,
        dst_ref=dst,
        send_sem=send_sem,
        recv_sem=recv_sem,
        device_id=device,
        device_id_type=MESH,
    )


def here():
    return lax.axis_index("member"), lax.axis_index("comp"), lax.axis_index("tile")


def greet(targets, count):
    barrier = pltpu.get_barrier_semaphore()
    for condition, device in targets:

        @pl.when(condition)
        def _():
            pl.semaphore_signal(barrier, inc=1, device_id=device, device_id_type=MESH)

    @pl.when(count > 0)
    def _():
        pl.semaphore_wait(barrier, count)


def differs(a, b):
    return jnp.logical_or(a[0] != b[0], jnp.logical_or(a[1] != b[1], a[2] != b[2]))


def spread_kernel(sizes, c_ref, r_ref, u_ref, ru_ref, send, rsend, recv, rrecv, loc):
    members, comps, fields, tiles, rows = sizes
    me = m, y, t = here()
    per = c_ref.shape[2] // members
    unit_m, unit_f = t // fields, t % fields
    has_surface = jnp.logical_and(m == 0, unit_f == 0)
    targets = []
    for j in range(tiles):
        source = (unit_m, 0, j)
        targets.append((differs(source, me), source))
    for j in range(tiles):
        source = (unit_m, 1, j)
        targets.append((jnp.logical_and(has_surface, differs(source, me)), source))
    self_unit = (unit_m == m).astype(jnp.int32)
    self_surface = jnp.logical_and(has_surface, unit_m == m).astype(jnp.int32)
    count = jnp.where(
        y == 0,
        members * comps * fields - self_unit,
        comps - self_surface,
    )
    greet(targets, count)

    def rows_of(j):
        return pl.ds(pl.multiple_of(j * rows, 8), rows)

    pieces = [(s, f, c) for s in range(comps) for f in range(fields) for c in range(members)]

    def piece(k):
        s, f, c = pieces[k]
        device = (c, s, m * fields + f)
        copy = remote(
            c_ref.at[s, f, pl.ds(c * per, per)],
            u_ref.at[:, rows_of(t), :],
            send.at[k],
            recv.at[t],
            device,
        )
        local = pltpu.make_async_copy(
            c_ref.at[s, f, pl.ds(c * per, per)], u_ref.at[:, rows_of(t), :], loc.at[0]
        )
        return device, copy, local

    def surface(s):
        device = (0, s, m * fields)
        copy = remote(r_ref.at[s], ru_ref.at[rows_of(t), :], rsend.at[s], rrecv.at[t], device)
        local = pltpu.make_async_copy(r_ref.at[s], ru_ref.at[rows_of(t), :], loc.at[1])
        return device, copy, local

    @pl.when(y == 0)
    def _():
        for k in range(len(pieces)):
            device, copy, local = piece(k)
            away = differs(device, me)
            pl.when(away)(copy.start)
            pl.when(jnp.logical_not(away))(local.start)

    @pl.when(y == 1)
    def _():
        for s in range(comps):
            device, copy, local = surface(s)
            away = differs(device, me)
            pl.when(away)(copy.start)
            pl.when(jnp.logical_not(away))(local.start)

    for j in range(tiles):
        away = differs((unit_m, 0, j), me)
        arrival = remote(
            u_ref.at[:, rows_of(j), :], u_ref.at[:, rows_of(j), :], send.at[0], recv.at[j], me
        )
        pl.when(away)(arrival.wait_recv)
        late = remote(
            ru_ref.at[rows_of(j), :], ru_ref.at[rows_of(j), :], rsend.at[0], rrecv.at[j], me
        )
        away = jnp.logical_and(has_surface, differs((unit_m, 1, j), me))
        pl.when(away)(late.wait_recv)

    @pl.when(y == 0)
    def _():
        for k in range(len(pieces)):
            device, copy, local = piece(k)
            away = differs(device, me)
            pl.when(away)(copy.wait_send)
            pl.when(jnp.logical_not(away))(local.wait)

    @pl.when(y == 1)
    def _():
        for s in range(comps):
            device, copy, local = surface(s)
            away = differs(device, me)
            pl.when(away)(copy.wait_send)
            pl.when(jnp.logical_not(away))(local.wait)


def swap_kernel(sizes, x_ref, xo_ref, sa_ref, send, recv, ssend, srecv, loc):
    members, comps, fields, tiles, rows = sizes
    me = m, y, t = here()
    unit_m, unit_f = t // fields, t % fields
    has_surface = jnp.logical_and(m == 0, unit_f == 0)
    other = (1 - m, y, t)
    targets = [(m >= 0, other)]
    for s in range(comps):
        source = (0, s, m * fields)
        targets.append((jnp.logical_and(y == 1, differs(source, me)), source))
    own_surface = jnp.logical_and(has_surface, jnp.logical_and(y == 1, unit_m == m))
    count = 1 + jnp.where(has_surface, tiles - own_surface.astype(jnp.int32), 0)
    greet(targets, count)

    def surface(j):
        device = (unit_m, 1, j)
        part = x_ref.at[0, pl.ds(j * rows, rows), :]
        copy = remote(part, sa_ref.at[y], ssend.at[j], srecv.at[y], device)
        return device, copy, pltpu.make_async_copy(part, sa_ref.at[y], loc.at[0])

    @pl.when(has_surface)
    def _():
        for j in range(tiles):
            device, copy, local = surface(j)
            away = differs(device, me)
            pl.when(away)(copy.start)
            pl.when(jnp.logical_not(away))(local.start)

    across = remote(x_ref, xo_ref, send.at[0], recv.at[0], other)
    across.start()
    across.wait()

    @pl.when(has_surface)
    def _():
        for j in range(tiles):
            device, copy, local = surface(j)
            away = differs(device, me)
            pl.when(away)(copy.wait_send)
            pl.when(jnp.logical_not(away))(local.wait)

    for s in range(comps):
        away = jnp.logical_and(y == 1, differs((0, s, m * fields), me))
        arrival = remote(sa_ref.at[s], sa_ref.at[s], ssend.at[0], srecv.at[s], me)
        pl.when(away)(arrival.wait_recv)


def return_kernel(
    sizes, f_ref, p_ref, own_ref, far_ref, score_ref, send, recv, fsend, frecv, psend, precv, loc
):
    members, comps, fields, tiles, rows = sizes
    me = m, y, t = here()
    per = f_ref.shape[0]
    unit_m, unit_f = t // fields, t % fields
    has_surface = jnp.logical_and(m == 0, unit_f == 0)
    other = (1 - m, y, t)
    pieces = [(s, f, c) for s in range(comps) for f in range(fields) for c in range(members)]
    targets = [(y == 0, other)]
    for s, f, c in pieces:
        source = (c, s, m * fields + f)
        targets.append((jnp.logical_and(y == 0, differs(source, me)), source))
    own_unit = jnp.logical_and(y == 0, unit_m == m).astype(jnp.int32)
    greet(targets, tiles - own_unit + jnp.where(y == 0, 1, 0))

    def band(j):
        device = (unit_m, 0, j)
        src = f_ref.at[:, pl.ds(j * rows, rows), :]
        dst = own_ref.at[y, unit_f, pl.ds(m * per, per)]
        slot = (y * fields + unit_f) * members + m
        return (
            device,
            remote(src, dst, send.at[j], recv.at[slot], device),
            pltpu.make_async_copy(src, dst, loc.at[0]),
            remote(p_ref, score_ref.at[y], psend.at[j], precv.at[y], device),
            pltpu.make_async_copy(p_ref, score_ref.at[y], loc.at[1]),
        )

    for j in range(tiles):
        device, copy, local, point, local_point = band(j)
        away = differs(device, me)
        pl.when(away)(copy.start)
        pl.when(jnp.logical_not(away))(local.start)
        pl.when(jnp.logical_and(has_surface, away))(point.start)
        pl.when(jnp.logical_and(has_surface, jnp.logical_not(away)))(local_point.start)

    def forward(k):
        s, f, c = pieces[k]
        part = (s, f, pl.ds(c * per, per))
        return remote(own_ref.at[part], far_ref.at[part], fsend.at[k], frecv.at[k], other)

    @pl.when(y == 0)
    def _():
        for k, (s, f, c) in enumerate(pieces):
            part = own_ref.at[s, f, pl.ds(c * per, per)]
            away = differs((c, s, m * fields + f), me)
            arrival = remote(part, part, send.at[0], recv.at[k], me)
            pl.when(away)(arrival.wait_recv)
            own = pltpu.make_async_copy(part, part, loc.at[0])
            pl.when(jnp.logical_not(away))(own.wait)
            forward(k).start()
        for s in range(comps):
            away = differs((0, s, m * fields), me)
            arrival = remote(score_ref.at[s], score_ref.at[s], psend.at[0], precv.at[s], me)
            pl.when(away)(arrival.wait_recv)
            own = pltpu.make_async_copy(p_ref, score_ref.at[s], loc.at[1])
            pl.when(jnp.logical_not(away))(own.wait)
        for k in range(len(pieces)):
            forward(k).wait()

    for j in range(tiles):
        device, copy, local, point, local_point = band(j)
        away = differs(device, me)
        pl.when(away)(copy.wait_send)
        pl.when(jnp.logical_and(has_surface, away))(point.wait_send)


def ocean_kernel(sizes, o_ref, p_ref, far_ref, score_ref, send, recv, psend, precv, loc):
    members, comps, fields, tiles, rows = sizes
    me = m, y, t = here()
    other = (1 - m, y, t)
    targets = [(y == 1, other)]
    for j in range(tiles):
        targets.append((jnp.logical_and(y == 1, j != t), (m, y, j)))
    greet(targets, jnp.where(y == 1, tiles, 0))

    @pl.when(y == 1)
    def _():
        across = remote(o_ref, far_ref, send.at[0], recv.at[0], other)
        across.start()
        local = pltpu.make_async_copy(p_ref, score_ref.at[t], loc.at[0])
        local.start()

        def point(j):
            return remote(p_ref, score_ref.at[t], psend.at[j], precv.at[t], (m, y, j))

        for j in range(tiles):
            pl.when(j != t)(point(j).start)
        for j in range(tiles):
            arrival = remote(score_ref.at[j], score_ref.at[j], psend.at[0], precv.at[j], me)
            pl.when(j != t)(arrival.wait_recv)
            pl.when(j != t)(point(j).wait_send)
        local.wait()
        across.wait()


def call(kernel, collective_id, outs, sems, *args):
    return pl.pallas_call(
        kernel,
        out_shape=[jax.ShapeDtypeStruct(shape, jnp.float32) for shape in outs],
        in_specs=[pl.BlockSpec(memory_space=pl.ANY)] * len(args),
        out_specs=[pl.BlockSpec(memory_space=pl.ANY)] * len(outs),
        scratch_shapes=[pltpu.SemaphoreType.DMA((n,)) for n in sems],
        compiler_params=pltpu.CompilerParams(collective_id=collective_id, has_side_effects=True),
    )(*args)


def matmul(a, b):
    return jnp.dot(a, b, precision=precise, preferred_element_type=jnp.float32)


def forced_of(field, blend, received):
    levels = field.shape[2]
    mixed = []
    for u in range(levels):
        total = blend[u, 0] * field[:, :, 0]
        for v in range(1, levels):
            total = total + blend[u, v] * field[:, :, v]
        mixed.append(total)
    forced = field + forcing_rate * jnp.tanh(jnp.stack(mixed, axis=2))
    extra = coupling_rate * (received - field[:, 0, 0])
    where_added = np.zeros(field.shape[1:3] + (1, 1), np.float32)
    where_added[0, 0] = 1.0
    return forced + where_added * extra[:, None, None]


def ocean_step(field, blend, received, diffusivity, land_sea, low, high):
    forced = forced_of(field, blend, received)
    above = jnp.concatenate([field[:, :, :, 1:], high], axis=3)
    below = jnp.concatenate([low, field[:, :, :, :-1]], axis=3)
    laplacian = (
        above
        + below
        + jnp.roll(field, 1, axis=4)
        + jnp.roll(field, -1, axis=4)
        - 4.0 * field
    )
    sea = land_sea[None, None, None] == 1
    return jnp.where(sea, forced + diffusivity[:, None, None, None] * laplacian, field)


def edges(field):
    count = lax.axis_size("tile")
    forward = [(i, i + 1) for i in range(count - 1)]
    backward = [(target, source) for source, target in forward]
    low = lax.ppermute(field[:, :, :, -1:], "tile", forward)
    high = lax.ppermute(field[:, :, :, :1], "tile", backward)
    return low, high


def by_units(
    member_state,
    layer_blend_operator,
    coefficient,
    interpolation_donor_meridians,
    land_sea,
    ancestry,
):
    member, component, tile = here()
    members, comps, tiles = (lax.axis_size(name) for name in ("member", "comp", "tile"))
    field = member_state[:, 0]
    slots, fields, levels, rows, lon_count = field.shape
    per = levels // members
    sizes = (members, comps, fields, tiles, rows)
    lon_basis, number = kept_lon_basis(lon_count)
    waves = lon_basis.shape[0]
    lon_forward = jnp.asarray(np.ascontiguousarray(lon_basis.T))
    lon_inverse = jnp.asarray(lon_basis)
    lat_basis = lat_table()
    lat_forward = jnp.asarray(lat_basis)
    lat_inverse = jnp.asarray(np.ascontiguousarray(lat_basis.T))
    weights = row_weights()
    weight_total = float(weights.sum())
    order = np.arange(MODES).astype(np.float32)
    squares = jnp.asarray(order[:, None] ** 2 + number[None, :] ** 2)

    is_air = component == 0
    small = jnp.concatenate([layer_blend_operator[0].reshape(-1), coefficient[0]])
    other_small = partner_2(small, "comp", 0)
    air_small = jnp.where(is_air, small, other_small)
    air_blend = air_small[: levels * levels].reshape(levels, levels)
    air_coefficient = air_small[levels * levels :]
    donors = interpolation_donor_meridians[0]
    other_donors = partner_2(donors, "comp", 0)
    partner = partner_2(field[:, 0, 0], "comp", 0)
    low, high = edges(field)

    def air_first(_):
        received = donor_lookup(partner, donors)
        forced = forced_of(field, layer_blend_operator[0], received)
        fourier = matmul(forced.reshape(-1, lon_count), lon_forward)
        return (
            fourier.reshape(slots, fields, levels, rows, waves),
            jnp.zeros((slots, rows, lon_count), jnp.float32),
            field,
        )

    def sea_first(_):
        received = donor_lookup(partner, donors)
        new = ocean_step(
            field, layer_blend_operator[0], received, coefficient[0], land_sea, low, high
        )
        return (
            jnp.zeros((slots, fields, levels, rows, waves), jnp.float32),
            donor_lookup(new[:, 0, 0], other_donors),
            new,
        )

    fourier, lookup, ocean = lax.cond(is_air, air_first, sea_first, 0)
    low, high = edges(ocean)
    gathered, sst = call(
        functools.partial(spread_kernel, sizes),
        0,
        [(per, LAT, waves), (LAT, lon_count)],
        (members * comps * fields, comps, tiles, tiles, 2),
        fourier,
        lookup,
    )
    unit_field = tile % fields
    rate = lax.dynamic_index_in_dim(air_coefficient, unit_field, keepdims=False)
    gain = 1.0 / (1.0 + rate * squares / (MODES * MODES))

    def filtered(level):
        return matmul(lat_inverse, matmul(lat_forward, level) * gain)

    coefs = jnp.concatenate([filtered(gathered[v]) for v in range(per)])
    state = matmul(coefs, lon_inverse).reshape(per, LAT, lon_count)
    other_state, flux = call(
        functools.partial(swap_kernel, sizes),
        1,
        [(per, LAT, lon_count), (slots, rows, lon_count)],
        (1, 1, tiles, comps, 1),
        state,
    )
    mine = lax.dynamic_slice_in_dim(air_blend, member * per, per)
    mine_own = lax.dynamic_slice_in_dim(mine, member * per, per, axis=1)
    mine_other = lax.dynamic_slice_in_dim(mine, (1 - member) * per, per, axis=1)
    has_surface = jnp.logical_and(member == 0, unit_field == 0)
    forced = []
    for u in range(per):
        mixing = mine_own[u, 0] * state[0] + mine_other[u, 0] * other_state[0]
        for v in range(1, per):
            mixing = mixing + mine_own[u, v] * state[v] + mine_other[u, v] * other_state[v]
        level = state[u] + forcing_rate * jnp.tanh(mixing)
        if u == 0:
            level = level + jnp.where(has_surface, coupling_rate * (sst - state[0]), 0.0)
        forced.append(level)
    fourier = matmul(jnp.concatenate(forced), lon_forward).reshape(per, LAT, waves)
    back = jnp.stack([filtered(fourier[v]) for v in range(per)])
    zonal_mean = back[0, :, 0] * lon_basis[0, 0]
    air_score = jnp.sum(zonal_mean * weights) / weight_total
    air_point = jnp.full((8, 128), air_score)
    own, far, air_scores = call(
        functools.partial(return_kernel, sizes),
        2,
        [(slots, fields, levels, rows, waves)] * 2 + [(slots, 8, 128)],
        (tiles, slots * fields * members, slots * fields * members)
        + (slots * fields * members, tiles, comps, 2),
        back,
        air_point,
    )

    def sea_second(_):
        received = donor_lookup(flux, donors)
        new = ocean_step(
            ocean, layer_blend_operator[0], received, coefficient[0], land_sea, low, high
        )
        my_weights = lax.dynamic_slice_in_dim(jnp.asarray(weights), tile * rows, rows)
        sums = jnp.sum(jnp.mean(new[:, 0, 0], axis=2) * my_weights, axis=1)
        return new, jnp.broadcast_to(jnp.pad(sums, (0, 8 - slots))[:, None], (8, 128))

    def air_second(_):
        return ocean, jnp.zeros((8, 128), jnp.float32)

    ocean, partial = lax.cond(is_air, air_second, sea_second, 0)
    far_ocean, sea_parts = call(
        functools.partial(ocean_kernel, sizes),
        3,
        [(slots, fields, levels, rows, lon_count), (tiles, 8, 128)],
        (1, 1, tiles, tiles, 1),
        ocean,
        partial,
    )
    parents = lax.dynamic_slice_in_dim(ancestry, member * slots, slots)

    def chosen(own, far):
        picked = []
        for slot in range(slots):
            parent = parents[slot]
            inside = parent % slots
            picked.append(
                jnp.where(
                    parent // slots == member,
                    lax.dynamic_index_in_dim(own, inside, keepdims=False),
                    lax.dynamic_index_in_dim(far, inside, keepdims=False),
                )
            )
        return jnp.stack(picked)

    def air_last(_):
        coefs = chosen(own, far).reshape(-1, waves)
        grid = matmul(coefs, lon_inverse)
        return grid.reshape(member_state.shape), air_scores[:, 0, :1]

    def sea_last(_):
        score = jnp.sum(sea_parts[:, :slots, :1], axis=0) / weight_total
        return chosen(ocean, far_ocean)[:, None], score

    return lax.cond(is_air, air_last, sea_last, 0)


def by_bands(
    member_state,
    layer_blend_operator,
    coefficient,
    interpolation_donor_meridians,
    land_sea,
    ancestry,
):
    slot_count = member_state.shape[0]
    component = lax.axis_index("comp")
    tile_index = lax.axis_index("tile")
    tile_count = lax.axis_size("tile")
    row_count = member_state.shape[4]
    lon_count = member_state.shape[5]
    lon_table, number = kept_lon_basis(lon_count)
    lon_basis = jnp.asarray(lon_table)
    local_modes = lon_table.shape[0] // tile_count
    my_numbers = lax.dynamic_slice_in_dim(jnp.asarray(number), tile_index * local_modes, local_modes)
    lat_basis = jnp.asarray(lat_table())
    order = jnp.arange(MODES, dtype=jnp.int32).astype(jnp.float32)
    sea_cells = land_sea[None, None] == 1
    diffusivity = coefficient[0][:, None, None, None]
    weights = row_weights()
    my_weights = lax.dynamic_slice_in_dim(jnp.asarray(weights), tile_index * row_count, row_count)
    weight_total = float(weights.sum())
    stepped_list = []
    partial_list = []
    for slot in range(slot_count):
        field = member_state[slot, 0]
        for _ in range(STEPS):
            surface = field[0, 0]
            partner = partner_2(surface, "comp", 0)
            received = donor_lookup(partner, interpolation_donor_meridians[0])
            mixing = jnp.einsum("uv,fvjx->fujx", layer_blend_operator[0], field, precision=precise)
            forced = field + forcing_rate * jnp.tanh(mixing)
            forced = forced.at[0, 0].add(coupling_rate * (received - surface))
            spectral_gain = 1.0 / (
                1.0
                + coefficient[0][:, None, None]
                * (order[None, None, :] ** 2 + my_numbers[None, :, None] ** 2)
                / (MODES * MODES)
            )
            fourier = jnp.einsum("fvjx,qx->fvjq", forced, lon_basis, precision=precise)
            spectrum = jnp.einsum(
                "lj,fkjq->fkql",
                lat_basis,
                lax.all_to_all(fourier, "tile", split_axis=3, concat_axis=2, tiled=True),
                precision=precise,
            )
            spectrum = spectrum * spectral_gain[:, None]
            returned = jnp.einsum("lj,fkql->fkjq", lat_basis, spectrum, precision=precise)
            filtered = lax.all_to_all(returned, "tile", split_axis=2, concat_axis=3, tiled=True)
            block_atm = jnp.einsum("fvjq,qx->fvjx", filtered, lon_basis, precision=precise)
            padded = padded_2(field, (("tile", 2),), 1)
            laplacian = (
                padded[:, :, 2:]
                + padded[:, :, :-2]
                + jnp.roll(field, 1, axis=3)
                + jnp.roll(field, -1, axis=3)
                - 4.0 * field
            )
            new_ocn = jnp.where(sea_cells, forced + diffusivity * laplacian, field)
            field = jnp.where(component == 0, block_atm, new_ocn)
        stepped_list.append(field)
        partial_list.append(jnp.sum(jnp.mean(field[0, 0], axis=1) * my_weights))
    local_states = jnp.stack(stepped_list)
    region_sums = lax.psum(jnp.stack(partial_list), "tile")
    region_score = (region_sums / weight_total).reshape(slot_count, 1)
    member_index = lax.axis_index("member")
    my_parents = lax.dynamic_slice_in_dim(ancestry, member_index * slot_count, slot_count)
    gathered = lax.all_gather(local_states, "member", axis=0, tiled=True)
    chosen = jnp.take(gathered, my_parents, axis=0)
    return (chosen[:, None], region_score)


def local(member_state, *others):
    members, comps, tiles = (lax.axis_size(name) for name in ("member", "comp", "tile"))
    slots, _, fields, levels, rows, _ = member_state.shape
    fits = members == 2 and comps == 2 and slots == comps and tiles == members * fields
    if fits and levels % members == 0 and rows % 8 == 0:
        return by_units(member_state, *others)
    return by_bands(member_state, *others)


def solution(mesh):
    return jax.shard_map(
        local,
        mesh=mesh,
        in_specs=(
            P("member", "comp", None, None, "tile", None),
            P("comp", None, None),
            P("comp", None),
            P("comp", "tile", None),
            P("tile", None),
            P(),
        ),
        out_specs=(P("member", "comp", None, None, "tile", None), P("member", "comp")),
        check_vma=False,
    )
```

```python
import functools
import math

import jax
import jax.numpy as jnp
import numpy as np
from jax import lax
from jax.experimental import pallas as pl
from jax.experimental.pallas import tpu as pltpu
from jax.sharding import PartitionSpec as P

LAT = 384
MODES = 256
STEPS = 2
MESH = pl.DeviceIdType.MESH


coupling_rate = 0.5
forcing_rate = 0.5
precise = lax.Precision.HIGH


def partner_2(value, axis, distance):
    mask = 2**distance
    pairs = [(source, source ^ mask) for source in range(lax.axis_size(axis))]
    return lax.ppermute(value, axis, pairs)


def padded_2(block, sides, width):
    for axis, dim in sides:
        count = lax.axis_size(axis)
        forward = [(i, i + 1) for i in range(count - 1)]
        backward = [(target, source) for source, target in forward]
        low = lax.ppermute(
            lax.slice_in_dim(block, block.shape[dim] - width, None, axis=dim), axis, forward
        )
        high = lax.ppermute(lax.slice_in_dim(block, 0, width, axis=dim), axis, backward)
        block = jnp.concatenate([low, block, high], axis=dim)
    return block


def kept_lon_basis(lon_count):
    wave = np.arange(2 * MODES)
    is_cosine = wave < MODES
    number = np.where(is_cosine, wave, wave - MODES + 1).astype(np.float32)
    cells = np.arange(lon_count).astype(np.float32)
    angle = np.float32(2.0 * math.pi) * number[:, None] * cells[None, :] / np.float32(lon_count)
    scale = np.where(number == 0.0, math.sqrt(1.0 / lon_count), math.sqrt(2.0 / lon_count)).astype(
        np.float32
    )
    table = np.where(is_cosine[:, None], np.cos(angle), np.sin(angle)) * scale[:, None]
    return table.astype(np.float32), number


def lat_table():
    order = np.arange(MODES).astype(np.float32)
    cells = np.arange(LAT).astype(np.float32)
    scale = np.where(order == 0.0, math.sqrt(1.0 / LAT), math.sqrt(2.0 / LAT)).astype(np.float32)
    angle = np.float32(math.pi) * (cells[None, :] + np.float32(0.5)) * order[:, None]
    return (np.cos(angle / np.float32(LAT)) * scale[:, None]).astype(np.float32)


def row_weights():
    rows = np.arange(LAT).astype(np.float32)
    return np.cos(
        np.float32(math.pi) * ((rows + np.float32(0.5)) / np.float32(LAT) - np.float32(0.5))
    ).astype(np.float32)


def donor_lookup(partner, donors):
    lon_count = partner.shape[-1]
    cells = jnp.arange(lon_count, dtype=jnp.int32)[None, :]
    offsets = jnp.mod(donors - cells, lon_count)
    result = jnp.zeros_like(partner)
    for shift_by in (-1, 0, 1, 2, 3, 4):
        moved = jnp.roll(partner, -shift_by, axis=-1)
        result = result + jnp.where(offsets == shift_by % lon_count, moved, 0.0)
    return result


def remote(src, dst, send_sem, recv_sem, device):
    return pltpu.make_async_remote_copy(
        src_ref=src,
        dst_ref=dst,
        send_sem=send_sem,
        recv_sem=recv_sem,
        device_id=device,
        device_id_type=MESH,
    )


def here():
    return lax.axis_index("member"), lax.axis_index("comp"), lax.axis_index("tile")


def greet(targets, count):
    barrier = pltpu.get_barrier_semaphore()
    for condition, device in targets:

        @pl.when(condition)
        def _():
            pl.semaphore_signal(barrier, inc=1, device_id=device, device_id_type=MESH)

    @pl.when(count > 0)
    def _():
        pl.semaphore_wait(barrier, count)


def differs(a, b):
    return jnp.logical_or(a[0] != b[0], jnp.logical_or(a[1] != b[1], a[2] != b[2]))


def spread_kernel(
    sizes, c_ref, r_ref, u_ref, ru_ref, h_ref, send, hsend, hrecv, rsend, recv, rrecv, loc
):
    members, comps, fields, tiles, rows = sizes
    me = m, y, t = here()
    per = c_ref.shape[2] // members
    unit_m, unit_f = t // fields, t % fields
    has_surface = jnp.logical_and(m == 0, unit_f == 0)
    targets = [(y == 1, (m, 0, t))]
    for j in range(tiles):
        source = (unit_m, y, j)
        targets.append((differs(source, me), source))
    for j in range(tiles):
        source = (unit_m, 1, j)
        targets.append((jnp.logical_and(has_surface, differs(source, me)), source))
    self_unit = (unit_m == m).astype(jnp.int32)
    self_surface = jnp.logical_and(has_surface, unit_m == m).astype(jnp.int32)
    count = members * fields - self_unit + jnp.where(y == 0, 1, comps - self_surface)
    greet(targets, count)

    def rows_of(j):
        return pl.ds(pl.multiple_of(j * rows, 8), rows)

    pieces = [(f, c) for f in range(fields) for c in range(members)]

    def place(k):
        f, c = pieces[k]
        return lax.rem(f + t, fields), c

    def piece(k, ref):
        f, c = place(k)
        device = (c, y, m * fields + f)
        src = ref.at[f, pl.ds(c * per, per)]
        dst = u_ref.at[:, rows_of(t), :]
        copy = remote(src, dst, send.at[k], recv.at[t], device)
        return differs(device, me), copy, pltpu.make_async_copy(src, dst, loc.at[0])

    def hop(k):
        f, c = place(k)
        part = (f, pl.ds(c * per, per))
        return remote(
            c_ref.at[(1,) + part], h_ref.at[part], hsend.at[k], hrecv.at[k], (m, 1 - y, t)
        )

    def surface(s):
        device = (0, s, m * fields)
        dst = ru_ref.at[rows_of(t), :]
        copy = remote(r_ref.at[s], dst, rsend.at[s], rrecv.at[t], device)
        return differs(device, me), copy, pltpu.make_async_copy(r_ref.at[s], dst, loc.at[1])

    def begin(parts):
        away, copy, local = parts
        pl.when(away)(copy.start)
        pl.when(jnp.logical_not(away))(local.start)

    def end(parts):
        away, copy, local = parts
        pl.when(away)(copy.wait_send)
        pl.when(jnp.logical_not(away))(local.wait)

    @pl.when(y == 0)
    def _():
        for k in range(len(pieces)):
            hop(k).start()
            begin(piece(k, c_ref.at[0]))

    @pl.when(y == 1)
    def _():
        for s in range(comps):
            begin(surface(s))
        for k in range(len(pieces)):
            hop(k).wait_recv()
            begin(piece(k, h_ref))

    for j in range(tiles):
        away = differs((unit_m, y, j), me)
        part = u_ref.at[:, rows_of(j), :]
        arrival = remote(part, part, send.at[0], recv.at[j], me)
        pl.when(away)(arrival.wait_recv)
        late = remote(
            ru_ref.at[rows_of(j), :], ru_ref.at[rows_of(j), :], rsend.at[0], rrecv.at[j], me
        )
        away = jnp.logical_and(has_surface, differs((unit_m, 1, j), me))
        pl.when(away)(late.wait_recv)

    @pl.when(y == 0)
    def _():
        for k in range(len(pieces)):
            hop(k).wait_send()
            end(piece(k, c_ref.at[0]))

    @pl.when(y == 1)
    def _():
        for s in range(comps):
            end(surface(s))
        for k in range(len(pieces)):
            end(piece(k, h_ref))


def swap_kernel(sizes, x_ref, xo_ref, sa_ref, send, recv, ssend, srecv, loc):
    members, comps, fields, tiles, rows = sizes
    me = m, y, t = here()
    unit_m, unit_f = t // fields, t % fields
    has_surface = jnp.logical_and(m == 0, unit_f == 0)
    other = (1 - m, y, t)
    targets = [(m >= 0, other)]
    for s in range(comps):
        source = (0, s, m * fields)
        targets.append((jnp.logical_and(y == 1, differs(source, me)), source))
    own_surface = jnp.logical_and(has_surface, jnp.logical_and(y == 1, unit_m == m))
    count = 1 + jnp.where(has_surface, tiles - own_surface.astype(jnp.int32), 0)
    greet(targets, count)

    def surface(j):
        device = (unit_m, 1, j)
        part = x_ref.at[0, pl.ds(j * rows, rows), :]
        copy = remote(part, sa_ref.at[y], ssend.at[j], srecv.at[y], device)
        return device, copy, pltpu.make_async_copy(part, sa_ref.at[y], loc.at[0])

    @pl.when(has_surface)
    def _():
        for j in range(tiles):
            device, copy, local = surface(j)
            away = differs(device, me)
            pl.when(away)(copy.start)
            pl.when(jnp.logical_not(away))(local.start)

    across = remote(x_ref, xo_ref, send.at[0], recv.at[0], other)
    across.start()
    across.wait()

    @pl.when(has_surface)
    def _():
        for j in range(tiles):
            device, copy, local = surface(j)
            away = differs(device, me)
            pl.when(away)(copy.wait_send)
            pl.when(jnp.logical_not(away))(local.wait)

    for s in range(comps):
        away = jnp.logical_and(y == 1, differs((0, s, m * fields), me))
        arrival = remote(sa_ref.at[s], sa_ref.at[s], ssend.at[0], srecv.at[s], me)
        pl.when(away)(arrival.wait_recv)


def return_kernel(
    sizes, f_ref, p_ref, own_ref, far_ref, score_ref, send, recv, fsend, frecv, psend, precv, loc
):
    members, comps, fields, tiles, rows = sizes
    me = m, y, t = here()
    per = f_ref.shape[0]
    unit_m, unit_f = t // fields, t % fields
    has_surface = jnp.logical_and(m == 0, unit_f == 0)
    other = (1 - m, y, t)
    pieces = [(s, f, c) for s in range(comps) for f in range(fields) for c in range(members)]
    targets = [(y == 0, other)]
    for s, f, c in pieces:
        source = (c, s, m * fields + f)
        targets.append((jnp.logical_and(y == 0, differs(source, me)), source))
    own_unit = jnp.logical_and(y == 0, unit_m == m).astype(jnp.int32)
    greet(targets, tiles - own_unit + jnp.where(y == 0, 1, 0))

    def band(j):
        device = (unit_m, 0, j)
        src = f_ref.at[:, pl.ds(j * rows, rows), :]
        dst = own_ref.at[y, unit_f, pl.ds(m * per, per)]
        slot = (y * fields + unit_f) * members + m
        return (
            device,
            remote(src, dst, send.at[j], recv.at[slot], device),
            pltpu.make_async_copy(src, dst, loc.at[0]),
            remote(p_ref, score_ref.at[y], psend.at[j], precv.at[y], device),
            pltpu.make_async_copy(p_ref, score_ref.at[y], loc.at[1]),
        )

    for j in range(tiles):
        device, copy, local, point, local_point = band(j)
        away = differs(device, me)
        pl.when(away)(copy.start)
        pl.when(jnp.logical_not(away))(local.start)
        pl.when(jnp.logical_and(has_surface, away))(point.start)
        pl.when(jnp.logical_and(has_surface, jnp.logical_not(away)))(local_point.start)

    def forward(k):
        s, f, c = pieces[k]
        part = (s, f, pl.ds(c * per, per))
        return remote(own_ref.at[part], far_ref.at[part], fsend.at[k], frecv.at[k], other)

    @pl.when(y == 0)
    def _():
        for k, (s, f, c) in enumerate(pieces):
            part = own_ref.at[s, f, pl.ds(c * per, per)]
            away = differs((c, s, m * fields + f), me)
            arrival = remote(part, part, send.at[0], recv.at[k], me)
            pl.when(away)(arrival.wait_recv)
            own = pltpu.make_async_copy(part, part, loc.at[0])
            pl.when(jnp.logical_not(away))(own.wait)
            forward(k).start()
        for s in range(comps):
            away = differs((0, s, m * fields), me)
            arrival = remote(score_ref.at[s], score_ref.at[s], psend.at[0], precv.at[s], me)
            pl.when(away)(arrival.wait_recv)
            own = pltpu.make_async_copy(p_ref, score_ref.at[s], loc.at[1])
            pl.when(jnp.logical_not(away))(own.wait)
        for k in range(len(pieces)):
            forward(k).wait()

    for j in range(tiles):
        device, copy, local, point, local_point = band(j)
        away = differs(device, me)
        pl.when(away)(copy.wait_send)
        pl.when(jnp.logical_and(has_surface, away))(point.wait_send)


def ocean_kernel(sizes, o_ref, p_ref, far_ref, score_ref, send, recv, psend, precv, loc):
    members, comps, fields, tiles, rows = sizes
    me = m, y, t = here()
    other = (1 - m, y, t)
    targets = [(y == 1, other)]
    for j in range(tiles):
        targets.append((jnp.logical_and(y == 1, j != t), (m, y, j)))
    greet(targets, jnp.where(y == 1, tiles, 0))

    @pl.when(y == 1)
    def _():
        across = remote(o_ref, far_ref, send.at[0], recv.at[0], other)
        across.start()
        local = pltpu.make_async_copy(p_ref, score_ref.at[t], loc.at[0])
        local.start()

        def point(j):
            return remote(p_ref, score_ref.at[t], psend.at[j], precv.at[t], (m, y, j))

        for j in range(tiles):
            pl.when(j != t)(point(j).start)
        for j in range(tiles):
            arrival = remote(score_ref.at[j], score_ref.at[j], psend.at[0], precv.at[j], me)
            pl.when(j != t)(arrival.wait_recv)
            pl.when(j != t)(point(j).wait_send)
        local.wait()
        across.wait()


def call(kernel, collective_id, outs, sems, *args):
    return pl.pallas_call(
        kernel,
        out_shape=[jax.ShapeDtypeStruct(shape, jnp.float32) for shape in outs],
        in_specs=[pl.BlockSpec(memory_space=pl.ANY)] * len(args),
        out_specs=[pl.BlockSpec(memory_space=pl.ANY)] * len(outs),
        scratch_shapes=[pltpu.SemaphoreType.DMA((n,)) for n in sems],
        compiler_params=pltpu.CompilerParams(collective_id=collective_id, has_side_effects=True),
    )(*args)


def matmul(a, b):
    return jnp.dot(a, b, precision=precise, preferred_element_type=jnp.float32)


def split(value):
    high = value.astype(jnp.bfloat16)
    return high, (value - high.astype(jnp.float32)).astype(jnp.bfloat16)


def split_table(table):
    high = table.astype(jnp.bfloat16)
    low = (table - high.astype(np.float32)).astype(jnp.bfloat16)
    return jnp.asarray(high), jnp.asarray(low)


def dot3(value, high_ref, low_ref):
    high, low = split(value)
    total = jnp.dot(high, low_ref[...], preferred_element_type=jnp.float32)
    total = total + jnp.dot(low, high_ref[...], preferred_element_type=jnp.float32)
    return total + jnp.dot(high, high_ref[...], preferred_element_type=jnp.float32)


def lookup(surface, donors):
    lon_count = surface.shape[-1]
    offset = donors - lax.broadcasted_iota(jnp.int32, donors.shape, 1)
    offset = jnp.where(offset > lon_count // 2, offset - lon_count, offset)
    offset = jnp.where(offset < -(lon_count // 2), offset + lon_count, offset)
    result = surface
    for shift in (-1, 1, 2, 3, 4):
        moved = pltpu.roll(surface, (-shift) % lon_count, 1)
        result = jnp.where(offset == shift, moved, result)
    return result


def mixed_level(blend_ref, field_ref, u):
    levels = field_ref.shape[2]
    total = blend_ref[u, 0] * field_ref[0, 0, 0]
    for v in range(1, levels):
        total = total + blend_ref[u, v] * field_ref[0, 0, v]
    return forcing_rate * jnp.tanh(total)


def air_kernel(field_ref, partner_ref, donors_ref, blend_ref, high_ref, low_ref, out_ref, forced):
    levels, rows = field_ref.shape[2:4]
    for u in range(levels):
        forced[u * rows : (u + 1) * rows] = field_ref[0, 0, u] + mixed_level(blend_ref, field_ref, u)

    @pl.when(pl.program_id(1) == 0)
    def _():
        received = lookup(partner_ref[0], donors_ref[...])
        forced[:rows] += coupling_rate * (received - field_ref[0, 0, 0])

    out_ref[0, 0] = dot3(forced[...], high_ref, low_ref).reshape(out_ref.shape[2:])


def sea_kernel(
    field_ref,
    low_ref,
    high_ref,
    partner_ref,
    donors_ref,
    next_ref,
    land_ref,
    blend_ref,
    rate_ref,
    out_ref,
    look_ref,
):
    levels, rows, lon_count = field_ref.shape[2:]
    rate = rate_ref[pl.program_id(1)]
    sea = land_ref[...] == 1
    first = pl.program_id(1) == 0
    row = lax.broadcasted_iota(jnp.int32, (rows, lon_count), 0)
    for u in range(levels):
        value = field_ref[0, 0, u]
        forced = value + mixed_level(blend_ref, field_ref, u)
        north = jnp.where(row == 0, low_ref[0, 0, u], pltpu.roll(value, 1, 0))
        south = jnp.where(row == rows - 1, high_ref[0, 0, u], pltpu.roll(value, rows - 1, 0))
        laplacian = (
            south
            + north
            + pltpu.roll(value, 1, 1)
            + pltpu.roll(value, lon_count - 1, 1)
            - 4.0 * value
        )
        if u == 0:
            received = lookup(partner_ref[0], donors_ref[...])
            extra = coupling_rate * (received - value)
            forced = forced + jnp.where(first, extra, 0.0)
        out_ref[0, 0, u] = jnp.where(sea, forced + rate * laplacian, value)

    @pl.when(first)
    def _():
        look_ref[0] = lookup(out_ref[0, 0, 0], next_ref[...])


def whole_spec(array):
    zeros = (0,) * array.ndim
    return pl.BlockSpec(array.shape, lambda *_: zeros)


def scalar_spec():
    return pl.BlockSpec(memory_space=pltpu.SMEM)


def state_spec(shape):
    return pl.BlockSpec((1, 1) + tuple(shape[2:]), lambda s, f, *_: (s, f, 0, 0, 0))


def surface_spec(shape):
    return pl.BlockSpec((1,) + tuple(shape[1:]), lambda s, f, *_: (s, 0, 0))


large = pltpu.CompilerParams(vmem_limit_bytes=40 * 1024 * 1024)


def air_forward(field, partner, donors, blend, table):
    slots, fields, levels, rows, lon_count = field.shape
    high, low = split_table(table)
    shape = field.shape[:-1] + (table.shape[1],)
    return pl.pallas_call(
        air_kernel,
        grid=(slots, fields),
        out_shape=jax.ShapeDtypeStruct(shape, jnp.float32),
        in_specs=[
            state_spec(field.shape),
            surface_spec(partner.shape),
            whole_spec(donors),
            scalar_spec(),
            whole_spec(high),
            whole_spec(low),
        ],
        out_specs=state_spec(shape),
        scratch_shapes=[pltpu.VMEM((levels * rows, lon_count), jnp.float32)],
        compiler_params=large,
    )(field, partner, donors, blend, high, low)


def sea_step(field, low, high, partner, donors, following, land_sea, blend, rate):
    return pl.pallas_call(
        sea_kernel,
        grid=field.shape[:2],
        out_shape=[
            jax.ShapeDtypeStruct(field.shape, jnp.float32),
            jax.ShapeDtypeStruct(partner.shape, jnp.float32),
        ],
        in_specs=[
            state_spec(field.shape),
            state_spec(low.shape),
            state_spec(high.shape),
            surface_spec(partner.shape),
            whole_spec(donors),
            whole_spec(following),
            whole_spec(land_sea),
            scalar_spec(),
            scalar_spec(),
        ],
        out_specs=[state_spec(field.shape), surface_spec(partner.shape)],
        compiler_params=large,
    )(field, low, high, partner, donors, following, land_sea, blend, rate)


def air_last_kernel(inside_ref, near_ref, own_ref, far_ref, high_ref, low_ref, out_ref):
    near = near_ref[pl.program_id(0)] == 1
    levels, rows, waves = own_ref.shape[2:]
    coefs = jnp.where(near, own_ref[0, 0], far_ref[0, 0]).reshape(levels * rows, waves)
    out_ref[0, 0] = dot3(coefs, high_ref, low_ref).reshape(out_ref.shape[2:])


def sea_last_kernel(inside_ref, near_ref, own_ref, far_ref, out_ref):
    near = near_ref[pl.program_id(0)] == 1
    out_ref[0, 0] = jnp.where(near, own_ref[0, 0], far_ref[0, 0])


def resampled(kernel, inside, near, own, far, tables, lon_count):
    shape = own.shape[:-1] + (lon_count,)

    def parent(s, f, inside_ref, near_ref):
        return (inside_ref[s], f, 0, 0, 0)

    parent_spec = pl.BlockSpec((1, 1) + own.shape[2:], parent)
    return pl.pallas_call(
        kernel,
        grid_spec=pltpu.PrefetchScalarGridSpec(
            num_scalar_prefetch=2,
            grid=own.shape[:2],
            in_specs=[parent_spec, parent_spec] + [whole_spec(table) for table in tables],
            out_specs=state_spec(shape),
        ),
        out_shape=jax.ShapeDtypeStruct(shape, jnp.float32),
        compiler_params=large,
    )(inside, near, own, far, *tables)


def edges(field):
    count = lax.axis_size("tile")
    forward = [(i, i + 1) for i in range(count - 1)]
    backward = [(target, source) for source, target in forward]
    low = lax.ppermute(field[:, :, :, -1:], "tile", forward)
    high = lax.ppermute(field[:, :, :, :1], "tile", backward)
    return low, high


def by_units(
    member_state,
    layer_blend_operator,
    coefficient,
    interpolation_donor_meridians,
    land_sea,
    ancestry,
):
    member, component, tile = here()
    members, comps, tiles = (lax.axis_size(name) for name in ("member", "comp", "tile"))
    field = member_state[:, 0]
    slots, fields, levels, rows, lon_count = field.shape
    per = levels // members
    sizes = (members, comps, fields, tiles, rows)
    lon_basis, number = kept_lon_basis(lon_count)
    waves = lon_basis.shape[0]
    lon_forward = jnp.asarray(np.ascontiguousarray(lon_basis.T))
    lon_inverse = jnp.asarray(lon_basis)
    lat_basis = lat_table()
    lat_forward = jnp.asarray(lat_basis)
    lat_inverse = jnp.asarray(np.ascontiguousarray(lat_basis.T))
    weights = row_weights()
    weight_total = float(weights.sum())
    order = np.arange(MODES).astype(np.float32)
    squares = jnp.asarray(order[:, None] ** 2 + number[None, :] ** 2)

    is_air = component == 0
    small = jnp.concatenate([layer_blend_operator[0].reshape(-1), coefficient[0]])
    other_small = partner_2(small, "comp", 0)
    air_small = jnp.where(is_air, small, other_small)
    air_blend = air_small[: levels * levels].reshape(levels, levels)
    air_coefficient = air_small[levels * levels :]
    donors = interpolation_donor_meridians[0]
    other_donors = partner_2(donors, "comp", 0)
    partner = partner_2(field[:, 0, 0], "comp", 0)
    low, high = edges(field)

    blend = layer_blend_operator[0]
    rate = coefficient[0]

    def air_first(_):
        fourier = air_forward(field, partner, donors, blend, np.ascontiguousarray(lon_basis.T))
        return fourier, jnp.zeros((slots, rows, lon_count), jnp.float32), field

    def sea_first(_):
        new, looked = sea_step(
            field, low, high, partner, donors, other_donors, land_sea, blend, rate
        )
        return jnp.zeros((slots, fields, levels, rows, waves), jnp.float32), looked, new

    fourier, looked, ocean = lax.cond(is_air, air_first, sea_first, 0)
    low, high = edges(ocean)
    gathered, sst, _ = call(
        functools.partial(spread_kernel, sizes),
        0,
        [(per, LAT, waves), (LAT, lon_count), (fields, levels, rows, waves)],
        (members * fields,) * 3 + (comps, tiles, tiles, 2),
        fourier,
        looked,
    )
    unit_field = tile % fields
    unit_rate = lax.dynamic_index_in_dim(air_coefficient, unit_field, keepdims=False)
    gain = 1.0 / (1.0 + unit_rate * squares / (MODES * MODES))

    def filtered(level):
        return matmul(lat_inverse, matmul(lat_forward, level) * gain)

    coefs = jnp.concatenate([filtered(gathered[v]) for v in range(per)])
    state = matmul(coefs, lon_inverse).reshape(per, LAT, lon_count)
    other_state, flux = call(
        functools.partial(swap_kernel, sizes),
        1,
        [(per, LAT, lon_count), (slots, rows, lon_count)],
        (1, 1, tiles, comps, 1),
        state,
    )
    mine = lax.dynamic_slice_in_dim(air_blend, member * per, per)
    mine_own = lax.dynamic_slice_in_dim(mine, member * per, per, axis=1)
    mine_other = lax.dynamic_slice_in_dim(mine, (1 - member) * per, per, axis=1)
    has_surface = jnp.logical_and(member == 0, unit_field == 0)
    forced = []
    for u in range(per):
        mixing = mine_own[u, 0] * state[0] + mine_other[u, 0] * other_state[0]
        for v in range(1, per):
            mixing = mixing + mine_own[u, v] * state[v] + mine_other[u, v] * other_state[v]
        level = state[u] + forcing_rate * jnp.tanh(mixing)
        if u == 0:
            level = level + jnp.where(has_surface, coupling_rate * (sst - state[0]), 0.0)
        forced.append(level)
    fourier = matmul(jnp.concatenate(forced), lon_forward).reshape(per, LAT, waves)
    back = jnp.stack([filtered(fourier[v]) for v in range(per)])
    zonal_mean = back[0, :, 0] * lon_basis[0, 0]
    air_score = jnp.sum(zonal_mean * weights) / weight_total
    air_point = jnp.full((8, 128), air_score)
    own, far, air_scores = call(
        functools.partial(return_kernel, sizes),
        2,
        [(slots, fields, levels, rows, waves)] * 2 + [(slots, 8, 128)],
        (tiles, slots * fields * members, slots * fields * members)
        + (slots * fields * members, tiles, comps, 2),
        back,
        air_point,
    )

    def sea_second(_):
        new, _ = sea_step(ocean, low, high, flux, donors, donors, land_sea, blend, rate)
        my_weights = lax.dynamic_slice_in_dim(jnp.asarray(weights), tile * rows, rows)
        sums = jnp.sum(jnp.mean(new[:, 0, 0], axis=2) * my_weights, axis=1)
        return new, jnp.broadcast_to(jnp.pad(sums, (0, 8 - slots))[:, None], (8, 128))

    def air_second(_):
        return ocean, jnp.zeros((8, 128), jnp.float32)

    ocean, partial = lax.cond(is_air, air_second, sea_second, 0)
    far_ocean, sea_parts = call(
        functools.partial(ocean_kernel, sizes),
        3,
        [(slots, fields, levels, rows, lon_count), (tiles, 8, 128)],
        (1, 1, tiles, tiles, 1),
        ocean,
        partial,
    )
    parents = lax.dynamic_slice_in_dim(ancestry, member * slots, slots)

    inside = parents % slots
    near = (parents // slots == member).astype(jnp.int32)

    def air_last(_):
        grid = resampled(
            air_last_kernel, inside, near, own, far, split_table(lon_basis), lon_count
        )
        return grid.reshape(member_state.shape), air_scores[:, 0, :1]

    def sea_last(_):
        score = jnp.sum(sea_parts[:, :slots, :1], axis=0) / weight_total
        states = resampled(sea_last_kernel, inside, near, ocean, far_ocean, (), lon_count)
        return states.reshape(member_state.shape), score

    return lax.cond(is_air, air_last, sea_last, 0)


def by_bands(
    member_state,
    layer_blend_operator,
    coefficient,
    interpolation_donor_meridians,
    land_sea,
    ancestry,
):
    slot_count = member_state.shape[0]
    component = lax.axis_index("comp")
    tile_index = lax.axis_index("tile")
    tile_count = lax.axis_size("tile")
    row_count = member_state.shape[4]
    lon_count = member_state.shape[5]
    lon_table, number = kept_lon_basis(lon_count)
    lon_basis = jnp.asarray(lon_table)
    local_modes = lon_table.shape[0] // tile_count
    my_numbers = lax.dynamic_slice_in_dim(jnp.asarray(number), tile_index * local_modes, local_modes)
    lat_basis = jnp.asarray(lat_table())
    order = jnp.arange(MODES, dtype=jnp.int32).astype(jnp.float32)
    sea_cells = land_sea[None, None] == 1
    diffusivity = coefficient[0][:, None, None, None]
    weights = row_weights()
    my_weights = lax.dynamic_slice_in_dim(jnp.asarray(weights), tile_index * row_count, row_count)
    weight_total = float(weights.sum())
    stepped_list = []
    partial_list = []
    for slot in range(slot_count):
        field = member_state[slot, 0]
        for _ in range(STEPS):
            surface = field[0, 0]
            partner = partner_2(surface, "comp", 0)
            received = donor_lookup(partner, interpolation_donor_meridians[0])
            mixing = jnp.einsum("uv,fvjx->fujx", layer_blend_operator[0], field, precision=precise)
            forced = field + forcing_rate * jnp.tanh(mixing)
            forced = forced.at[0, 0].add(coupling_rate * (received - surface))
            spectral_gain = 1.0 / (
                1.0
                + coefficient[0][:, None, None]
                * (order[None, None, :] ** 2 + my_numbers[None, :, None] ** 2)
                / (MODES * MODES)
            )
            fourier = jnp.einsum("fvjx,qx->fvjq", forced, lon_basis, precision=precise)
            spectrum = jnp.einsum(
                "lj,fkjq->fkql",
                lat_basis,
                lax.all_to_all(fourier, "tile", split_axis=3, concat_axis=2, tiled=True),
                precision=precise,
            )
            spectrum = spectrum * spectral_gain[:, None]
            returned = jnp.einsum("lj,fkql->fkjq", lat_basis, spectrum, precision=precise)
            filtered = lax.all_to_all(returned, "tile", split_axis=2, concat_axis=3, tiled=True)
            block_atm = jnp.einsum("fvjq,qx->fvjx", filtered, lon_basis, precision=precise)
            padded = padded_2(field, (("tile", 2),), 1)
            laplacian = (
                padded[:, :, 2:]
                + padded[:, :, :-2]
                + jnp.roll(field, 1, axis=3)
                + jnp.roll(field, -1, axis=3)
                - 4.0 * field
            )
            new_ocn = jnp.where(sea_cells, forced + diffusivity * laplacian, field)
            field = jnp.where(component == 0, block_atm, new_ocn)
        stepped_list.append(field)
        partial_list.append(jnp.sum(jnp.mean(field[0, 0], axis=1) * my_weights))
    local_states = jnp.stack(stepped_list)
    region_sums = lax.psum(jnp.stack(partial_list), "tile")
    region_score = (region_sums / weight_total).reshape(slot_count, 1)
    member_index = lax.axis_index("member")
    my_parents = lax.dynamic_slice_in_dim(ancestry, member_index * slot_count, slot_count)
    gathered = lax.all_gather(local_states, "member", axis=0, tiled=True)
    chosen = jnp.take(gathered, my_parents, axis=0)
    return (chosen[:, None], region_score)


def local(member_state, *others):
    members, comps, tiles = (lax.axis_size(name) for name in ("member", "comp", "tile"))
    slots, _, fields, levels, rows, _ = member_state.shape
    fits = members == 2 and comps == 2 and slots == comps and tiles == members * fields
    if fits and levels % members == 0 and rows % 8 == 0:
        return by_units(member_state, *others)
    return by_bands(member_state, *others)


def solution(mesh):
    return jax.shard_map(
        local,
        mesh=mesh,
        in_specs=(
            P("member", "comp", None, None, "tile", None),
            P("comp", None, None),
            P("comp", None),
            P("comp", "tile", None),
            P("tile", None),
            P(),
        ),
        out_specs=(P("member", "comp", None, None, "tile", None), P("member", "comp")),
        check_vma=False,
    )
```

```python
import functools
import math

import jax
import jax.numpy as jnp
import numpy as np
from jax import lax
from jax.experimental import pallas as pl
from jax.experimental.pallas import tpu as pltpu
from jax.sharding import PartitionSpec as P

LAT = 384
MODES = 256
STEPS = 2
MESH = pl.DeviceIdType.MESH


coupling_rate = 0.5
forcing_rate = 0.5
precise = lax.Precision.HIGH


def partner_2(value, axis, distance):
    mask = 2**distance
    pairs = [(source, source ^ mask) for source in range(lax.axis_size(axis))]
    return lax.ppermute(value, axis, pairs)


def padded_2(block, sides, width):
    for axis, dim in sides:
        count = lax.axis_size(axis)
        forward = [(i, i + 1) for i in range(count - 1)]
        backward = [(target, source) for source, target in forward]
        low = lax.ppermute(
            lax.slice_in_dim(block, block.shape[dim] - width, None, axis=dim), axis, forward
        )
        high = lax.ppermute(lax.slice_in_dim(block, 0, width, axis=dim), axis, backward)
        block = jnp.concatenate([low, block, high], axis=dim)
    return block


def kept_lon_basis(lon_count):
    wave = np.arange(2 * MODES)
    is_cosine = wave < MODES
    number = np.where(is_cosine, wave, wave - MODES + 1).astype(np.float32)
    cells = np.arange(lon_count).astype(np.float32)
    angle = np.float32(2.0 * math.pi) * number[:, None] * cells[None, :] / np.float32(lon_count)
    scale = np.where(number == 0.0, math.sqrt(1.0 / lon_count), math.sqrt(2.0 / lon_count)).astype(
        np.float32
    )
    table = np.where(is_cosine[:, None], np.cos(angle), np.sin(angle)) * scale[:, None]
    return table.astype(np.float32), number


def lat_table():
    order = np.arange(MODES).astype(np.float32)
    cells = np.arange(LAT).astype(np.float32)
    scale = np.where(order == 0.0, math.sqrt(1.0 / LAT), math.sqrt(2.0 / LAT)).astype(np.float32)
    angle = np.float32(math.pi) * (cells[None, :] + np.float32(0.5)) * order[:, None]
    return (np.cos(angle / np.float32(LAT)) * scale[:, None]).astype(np.float32)


def row_weights():
    rows = np.arange(LAT).astype(np.float32)
    return np.cos(
        np.float32(math.pi) * ((rows + np.float32(0.5)) / np.float32(LAT) - np.float32(0.5))
    ).astype(np.float32)


def donor_lookup(partner, donors):
    lon_count = partner.shape[-1]
    cells = jnp.arange(lon_count, dtype=jnp.int32)[None, :]
    offsets = jnp.mod(donors - cells, lon_count)
    result = jnp.zeros_like(partner)
    for shift_by in (-1, 0, 1, 2, 3, 4):
        moved = jnp.roll(partner, -shift_by, axis=-1)
        result = result + jnp.where(offsets == shift_by % lon_count, moved, 0.0)
    return result


def remote(src, dst, send_sem, recv_sem, device):
    return pltpu.make_async_remote_copy(
        src_ref=src,
        dst_ref=dst,
        send_sem=send_sem,
        recv_sem=recv_sem,
        device_id=device,
        device_id_type=MESH,
    )


def here():
    return lax.axis_index("member"), lax.axis_index("comp"), lax.axis_index("tile")


def greet(targets, count):
    barrier = pltpu.get_barrier_semaphore()
    for condition, device in targets:

        @pl.when(condition)
        def _():
            pl.semaphore_signal(barrier, inc=1, device_id=device, device_id_type=MESH)

    @pl.when(count > 0)
    def _():
        pl.semaphore_wait(barrier, count)


def differs(a, b):
    return jnp.logical_or(a[0] != b[0], jnp.logical_or(a[1] != b[1], a[2] != b[2]))


def shores(y, t, tiles):
    return jnp.logical_and(y == 1, t > 0), jnp.logical_and(y == 1, t < tiles - 1)


def edge_copies(edge_ref, low_ref, high_ref, esend, erecv, m, y, t):
    up = remote(edge_ref.at[:, :, 0], high_ref, esend.at[0], erecv.at[0], (m, y, t - 1))
    down = remote(edge_ref.at[:, :, 1], low_ref, esend.at[1], erecv.at[1], (m, y, t + 1))
    return up, down


def couple_kernel(
    sizes,
    field_ref,
    donors_ref,
    blend_ref,
    rate_ref,
    edge_ref,
    partner_ref,
    odonors_ref,
    oblend_ref,
    orate_ref,
    low_ref,
    high_ref,
    send,
    recv,
    esend,
    erecv,
):
    members, comps, fields, tiles, rows = sizes
    m, y, t = here()
    other = (m, 1 - y, t)
    north, south = shores(y, t, tiles)
    targets = [(m >= 0, other), (north, (m, y, t - 1)), (south, (m, y, t + 1))]
    greet(targets, 1 + north.astype(jnp.int32) + south.astype(jnp.int32))
    slots = partner_ref.shape[0]
    pairs = [(field_ref.at[s, 0, 0], partner_ref.at[s]) for s in range(slots)]
    pairs += [(donors_ref, odonors_ref), (blend_ref, oblend_ref), (rate_ref, orate_ref)]
    copies = [remote(a, b, send.at[k], recv.at[k], other) for k, (a, b) in enumerate(pairs)]
    up, down = edge_copies(edge_ref, low_ref, high_ref, esend, erecv, m, y, t)
    for copy in copies:
        copy.start()
    pl.when(north)(up.start)
    pl.when(south)(down.start)
    for copy in copies:
        copy.wait()
    pl.when(north)(up.wait_send)
    pl.when(south)(down.wait_send)
    pl.when(south)(up.wait_recv)
    pl.when(north)(down.wait_recv)


def spread_kernel(
    sizes,
    c_ref,
    r_ref,
    edge_ref,
    u_ref,
    ru_ref,
    h_ref,
    low_ref,
    high_ref,
    send,
    hsend,
    hrecv,
    rsend,
    recv,
    rrecv,
    loc,
    esend,
    erecv,
):
    members, comps, fields, tiles, rows = sizes
    me = m, y, t = here()
    per = c_ref.shape[2] // members
    unit_m, unit_f = t // fields, t % fields
    has_surface = jnp.logical_and(m == 0, unit_f == 0)
    north, south = shores(y, t, tiles)
    targets = [(y == 1, (m, 0, t)), (north, (m, y, t - 1)), (south, (m, y, t + 1))]
    up, down = edge_copies(edge_ref, low_ref, high_ref, esend, erecv, m, y, t)
    for j in range(tiles):
        source = (unit_m, y, j)
        targets.append((differs(source, me), source))
    for j in range(tiles):
        source = (unit_m, 1, j)
        targets.append((jnp.logical_and(has_surface, differs(source, me)), source))
    self_unit = (unit_m == m).astype(jnp.int32)
    self_surface = jnp.logical_and(has_surface, unit_m == m).astype(jnp.int32)
    count = members * fields - self_unit + jnp.where(y == 0, 1, comps - self_surface)
    greet(targets, count + north.astype(jnp.int32) + south.astype(jnp.int32))
    pl.when(north)(up.start)
    pl.when(south)(down.start)

    def rows_of(j):
        return pl.ds(pl.multiple_of(j * rows, 8), rows)

    pieces = [(f, c) for f in range(fields) for c in range(members)]

    def place(k):
        f, c = pieces[k]
        return lax.rem(f + t, fields), c

    def piece(k, ref):
        f, c = place(k)
        device = (c, y, m * fields + f)
        src = ref.at[f, pl.ds(c * per, per)]
        dst = u_ref.at[:, rows_of(t), :]
        copy = remote(src, dst, send.at[k], recv.at[t], device)
        return differs(device, me), copy, pltpu.make_async_copy(src, dst, loc.at[0])

    def hop(k):
        f, c = place(k)
        part = (f, pl.ds(c * per, per))
        return remote(
            c_ref.at[(1,) + part], h_ref.at[part], hsend.at[k], hrecv.at[k], (m, 1 - y, t)
        )

    def surface(s):
        device = (0, s, m * fields)
        dst = ru_ref.at[rows_of(t), :]
        copy = remote(r_ref.at[s], dst, rsend.at[s], rrecv.at[t], device)
        return differs(device, me), copy, pltpu.make_async_copy(r_ref.at[s], dst, loc.at[1])

    def begin(parts):
        away, copy, local = parts
        pl.when(away)(copy.start)
        pl.when(jnp.logical_not(away))(local.start)

    def end(parts):
        away, copy, local = parts
        pl.when(away)(copy.wait_send)
        pl.when(jnp.logical_not(away))(local.wait)

    @pl.when(y == 0)
    def _():
        for k in range(len(pieces)):
            hop(k).start()
            begin(piece(k, c_ref.at[0]))

    @pl.when(y == 1)
    def _():
        for s in range(comps):
            begin(surface(s))
        for k in range(len(pieces)):
            hop(k).wait_recv()
            begin(piece(k, h_ref))

    for j in range(tiles):
        away = differs((unit_m, y, j), me)
        part = u_ref.at[:, rows_of(j), :]
        arrival = remote(part, part, send.at[0], recv.at[j], me)
        pl.when(away)(arrival.wait_recv)
        late = remote(
            ru_ref.at[rows_of(j), :], ru_ref.at[rows_of(j), :], rsend.at[0], rrecv.at[j], me
        )
        away = jnp.logical_and(has_surface, differs((unit_m, 1, j), me))
        pl.when(away)(late.wait_recv)

    @pl.when(y == 0)
    def _():
        for k in range(len(pieces)):
            hop(k).wait_send()
            end(piece(k, c_ref.at[0]))

    @pl.when(y == 1)
    def _():
        for s in range(comps):
            end(surface(s))
        for k in range(len(pieces)):
            end(piece(k, h_ref))

    pl.when(north)(up.wait_send)
    pl.when(south)(down.wait_send)
    pl.when(south)(up.wait_recv)
    pl.when(north)(down.wait_recv)


def swap_kernel(sizes, x_ref, xo_ref, sa_ref, send, recv, ssend, srecv, loc):
    members, comps, fields, tiles, rows = sizes
    me = m, y, t = here()
    unit_m, unit_f = t // fields, t % fields
    has_surface = jnp.logical_and(m == 0, unit_f == 0)
    other = (1 - m, y, t)
    targets = [(m >= 0, other)]
    for s in range(comps):
        source = (0, s, m * fields)
        targets.append((jnp.logical_and(y == 1, differs(source, me)), source))
    own_surface = jnp.logical_and(has_surface, jnp.logical_and(y == 1, unit_m == m))
    count = 1 + jnp.where(has_surface, tiles - own_surface.astype(jnp.int32), 0)
    greet(targets, count)

    def surface(j):
        device = (unit_m, 1, j)
        part = x_ref.at[0, pl.ds(j * rows, rows), :]
        copy = remote(part, sa_ref.at[y], ssend.at[j], srecv.at[y], device)
        return device, copy, pltpu.make_async_copy(part, sa_ref.at[y], loc.at[0])

    @pl.when(has_surface)
    def _():
        for j in range(tiles):
            device, copy, local = surface(j)
            away = differs(device, me)
            pl.when(away)(copy.start)
            pl.when(jnp.logical_not(away))(local.start)

    across = remote(x_ref, xo_ref, send.at[0], recv.at[0], other)
    across.start()
    across.wait()

    @pl.when(has_surface)
    def _():
        for j in range(tiles):
            device, copy, local = surface(j)
            away = differs(device, me)
            pl.when(away)(copy.wait_send)
            pl.when(jnp.logical_not(away))(local.wait)

    for s in range(comps):
        away = jnp.logical_and(y == 1, differs((0, s, m * fields), me))
        arrival = remote(sa_ref.at[s], sa_ref.at[s], ssend.at[0], srecv.at[s], me)
        pl.when(away)(arrival.wait_recv)


def return_kernel(
    sizes,
    f_ref,
    p_ref,
    o_ref,
    q_ref,
    own_ref,
    far_ref,
    score_ref,
    faro_ref,
    part_ref,
    send,
    recv,
    fsend,
    frecv,
    psend,
    precv,
    loc,
    osend,
    orecv,
    qsend,
    qrecv,
):
    members, comps, fields, tiles, rows = sizes
    me = m, y, t = here()
    per = f_ref.shape[0]
    unit_m, unit_f = t // fields, t % fields
    has_surface = jnp.logical_and(m == 0, unit_f == 0)
    other = (1 - m, y, t)
    pieces = [(s, f, c) for s in range(comps) for f in range(fields) for c in range(members)]
    targets = [(m >= 0, other)]
    for j in range(tiles):
        targets.append((jnp.logical_and(y == 1, j != t), (m, y, j)))
    for s, f, c in pieces:
        source = (c, s, m * fields + f)
        targets.append((jnp.logical_and(y == 0, differs(source, me)), source))
    own_unit = jnp.logical_and(y == 0, unit_m == m).astype(jnp.int32)
    greet(targets, tiles - own_unit + jnp.where(y == 0, 1, tiles))
    across = remote(o_ref, faro_ref, osend.at[0], orecv.at[0], other)
    keep = pltpu.make_async_copy(q_ref, part_ref.at[t], loc.at[2])

    def share(j):
        return remote(q_ref, part_ref.at[t], qsend.at[j], qrecv.at[t], (m, y, j))

    def band(j):
        device = (unit_m, 0, j)
        src = f_ref.at[:, pl.ds(j * rows, rows), :]
        dst = own_ref.at[y, unit_f, pl.ds(m * per, per)]
        slot = (y * fields + unit_f) * members + m
        return (
            device,
            remote(src, dst, send.at[j], recv.at[slot], device),
            pltpu.make_async_copy(src, dst, loc.at[0]),
            remote(p_ref, score_ref.at[y], psend.at[j], precv.at[y], device),
            pltpu.make_async_copy(p_ref, score_ref.at[y], loc.at[1]),
        )

    for j in range(tiles):
        device, copy, local, point, local_point = band(j)
        away = differs(device, me)
        pl.when(away)(copy.start)
        pl.when(jnp.logical_not(away))(local.start)
        pl.when(jnp.logical_and(has_surface, away))(point.start)
        pl.when(jnp.logical_and(has_surface, jnp.logical_not(away)))(local_point.start)

    @pl.when(y == 1)
    def _():
        across.start()
        keep.start()
        for j in range(tiles):
            pl.when(j != t)(share(j).start)

    def forward(k):
        s, f, c = pieces[k]
        part = (s, f, pl.ds(c * per, per))
        return remote(own_ref.at[part], far_ref.at[part], fsend.at[k], frecv.at[k], other)

    @pl.when(y == 0)
    def _():
        for k, (s, f, c) in enumerate(pieces):
            part = own_ref.at[s, f, pl.ds(c * per, per)]
            away = differs((c, s, m * fields + f), me)
            arrival = remote(part, part, send.at[0], recv.at[k], me)
            pl.when(away)(arrival.wait_recv)
            own = pltpu.make_async_copy(part, part, loc.at[0])
            pl.when(jnp.logical_not(away))(own.wait)
            forward(k).start()
        for s in range(comps):
            away = differs((0, s, m * fields), me)
            arrival = remote(score_ref.at[s], score_ref.at[s], psend.at[0], precv.at[s], me)
            pl.when(away)(arrival.wait_recv)
            own = pltpu.make_async_copy(p_ref, score_ref.at[s], loc.at[1])
            pl.when(jnp.logical_not(away))(own.wait)
        for k in range(len(pieces)):
            forward(k).wait()

    for j in range(tiles):
        device, copy, local, point, local_point = band(j)
        away = differs(device, me)
        pl.when(away)(copy.wait_send)
        pl.when(jnp.logical_and(has_surface, away))(point.wait_send)

    @pl.when(y == 1)
    def _():
        keep.wait()
        for j in range(tiles):
            arrival = remote(part_ref.at[j], part_ref.at[j], qsend.at[0], qrecv.at[j], me)
            pl.when(j != t)(arrival.wait_recv)
            pl.when(j != t)(share(j).wait_send)
        across.wait()


def call(kernel, collective_id, outs, sems, *args):
    return pl.pallas_call(
        kernel,
        out_shape=[
            jax.ShapeDtypeStruct(out.shape, out.dtype)
            if hasattr(out, "dtype")
            else jax.ShapeDtypeStruct(out, jnp.float32)
            for out in outs
        ],
        in_specs=[pl.BlockSpec(memory_space=pl.ANY)] * len(args),
        out_specs=[pl.BlockSpec(memory_space=pl.ANY)] * len(outs),
        scratch_shapes=[pltpu.SemaphoreType.DMA((n,)) for n in sems],
        compiler_params=pltpu.CompilerParams(collective_id=collective_id, has_side_effects=True),
    )(*args)


def matmul(a, b):
    return jnp.dot(a, b, precision=precise, preferred_element_type=jnp.float32)


def split(value):
    high = value.astype(jnp.bfloat16)
    return high, (value - high.astype(jnp.float32)).astype(jnp.bfloat16)


def split_table(table):
    high = table.astype(jnp.bfloat16)
    low = (table - high.astype(np.float32)).astype(jnp.bfloat16)
    return jnp.asarray(high), jnp.asarray(low)


def dot3(value, high_ref, low_ref):
    high, low = split(value)
    total = jnp.dot(high, low_ref[...], preferred_element_type=jnp.float32)
    total = total + jnp.dot(low, high_ref[...], preferred_element_type=jnp.float32)
    return total + jnp.dot(high, high_ref[...], preferred_element_type=jnp.float32)


def lookup(surface, donors):
    lon_count = surface.shape[-1]
    offset = donors - lax.broadcasted_iota(jnp.int32, donors.shape, 1)
    offset = jnp.where(offset > lon_count // 2, offset - lon_count, offset)
    offset = jnp.where(offset < -(lon_count // 2), offset + lon_count, offset)
    result = surface
    for shift in (-1, 1, 2, 3, 4):
        moved = pltpu.roll(surface, (-shift) % lon_count, 1)
        result = jnp.where(offset == shift, moved, result)
    return result


def mixed_level(blend_ref, field_ref, u):
    levels = field_ref.shape[2]
    total = blend_ref[u, 0] * field_ref[0, 0, 0]
    for v in range(1, levels):
        total = total + blend_ref[u, v] * field_ref[0, 0, v]
    return forcing_rate * jnp.tanh(total)


def air_kernel(field_ref, partner_ref, donors_ref, blend_ref, high_ref, low_ref, out_ref, forced):
    levels, rows = field_ref.shape[2:4]
    for u in range(levels):
        forced[u * rows : (u + 1) * rows] = field_ref[0, 0, u] + mixed_level(blend_ref, field_ref, u)

    @pl.when(pl.program_id(1) == 0)
    def _():
        received = lookup(partner_ref[0], donors_ref[...])
        forced[:rows] += coupling_rate * (received - field_ref[0, 0, 0])

    out_ref[0, 0] = dot3(forced[...], high_ref, low_ref).reshape(out_ref.shape[2:])


def sea_kernel(
    field_ref,
    low_ref,
    high_ref,
    partner_ref,
    donors_ref,
    next_ref,
    land_ref,
    weight_ref,
    blend_ref,
    rate_ref,
    out_ref,
    look_ref,
    edge_ref,
    sum_ref,
):
    levels, rows, lon_count = field_ref.shape[2:]
    rate = rate_ref[pl.program_id(1)]
    sea = land_ref[...] == 1
    first = pl.program_id(1) == 0
    row = lax.broadcasted_iota(jnp.int32, (rows, lon_count), 0)
    for u in range(levels):
        value = field_ref[0, 0, u]
        forced = value + mixed_level(blend_ref, field_ref, u)
        north = jnp.where(row == 0, low_ref[0, 0, u : u + 1], pltpu.roll(value, 1, 0))
        south = jnp.where(row == rows - 1, high_ref[0, 0, u : u + 1], pltpu.roll(value, rows - 1, 0))
        laplacian = (
            south
            + north
            + pltpu.roll(value, 1, 1)
            + pltpu.roll(value, lon_count - 1, 1)
            - 4.0 * value
        )
        if u == 0:
            received = lookup(partner_ref[0], donors_ref[...])
            extra = coupling_rate * (received - value)
            forced = forced + jnp.where(first, extra, 0.0)
        result = jnp.where(sea, forced + rate * laplacian, value)
        out_ref[0, 0, u] = result
        edge_ref[0, 0, 0, u : u + 1] = result[:1]
        edge_ref[0, 0, 1, u : u + 1] = result[rows - 1 :]

    @pl.when(first)
    def _():
        look_ref[0] = lookup(out_ref[0, 0, 0], next_ref[...])
        total = jnp.sum(out_ref[0, 0, 0] * weight_ref[...], axis=0, keepdims=True)
        total = jnp.sum(total, axis=1, keepdims=True) / lon_count
        sum_ref[0] = jnp.broadcast_to(total, sum_ref.shape[1:])


def whole_spec(array):
    zeros = (0,) * array.ndim
    return pl.BlockSpec(array.shape, lambda *_: zeros)


def scalar_spec():
    return pl.BlockSpec(memory_space=pltpu.SMEM)


def state_spec(shape):
    zeros = (0,) * (len(shape) - 2)
    return pl.BlockSpec((1, 1) + tuple(shape[2:]), lambda s, f, *_: (s, f) + zeros)


def surface_spec(shape):
    return pl.BlockSpec((1,) + tuple(shape[1:]), lambda s, f, *_: (s, 0, 0))


large = pltpu.CompilerParams(vmem_limit_bytes=40 * 1024 * 1024)


def air_forward(field, partner, donors, blend, table):
    slots, fields, levels, rows, lon_count = field.shape
    high, low = split_table(table)
    shape = field.shape[:-1] + (table.shape[1],)
    return pl.pallas_call(
        air_kernel,
        grid=(slots, fields),
        out_shape=jax.ShapeDtypeStruct(shape, jnp.float32),
        in_specs=[
            state_spec(field.shape),
            surface_spec(partner.shape),
            whole_spec(donors),
            scalar_spec(),
            whole_spec(high),
            whole_spec(low),
        ],
        out_specs=state_spec(shape),
        scratch_shapes=[pltpu.VMEM((levels * rows, lon_count), jnp.float32)],
        compiler_params=large,
    )(field, partner, donors, blend, high, low)


def sea_step(field, low, high, partner, donors, following, land_sea, weights, blend, rate):
    slots, fields, levels, rows, lon_count = field.shape
    edge = (slots, fields, 2, levels, lon_count)
    return pl.pallas_call(
        sea_kernel,
        grid=field.shape[:2],
        out_shape=[
            jax.ShapeDtypeStruct(field.shape, jnp.float32),
            jax.ShapeDtypeStruct(partner.shape, jnp.float32),
            jax.ShapeDtypeStruct(edge, jnp.float32),
            jax.ShapeDtypeStruct((slots, 8, 128), jnp.float32),
        ],
        in_specs=[
            state_spec(field.shape),
            state_spec(low.shape),
            state_spec(high.shape),
            surface_spec(partner.shape),
            whole_spec(donors),
            whole_spec(following),
            whole_spec(land_sea),
            whole_spec(weights),
            scalar_spec(),
            scalar_spec(),
        ],
        out_specs=[
            state_spec(field.shape),
            surface_spec(partner.shape),
            state_spec(edge),
            surface_spec((slots, 8, 128)),
        ],
        compiler_params=large,
    )(field, low, high, partner, donors, following, land_sea, weights, blend, rate)


def air_last_kernel(inside_ref, near_ref, own_ref, far_ref, high_ref, low_ref, out_ref):
    near = near_ref[pl.program_id(0)] == 1
    levels, rows, waves = own_ref.shape[2:]
    coefs = jnp.where(near, own_ref[0, 0], far_ref[0, 0]).reshape(levels * rows, waves)
    out_ref[0, 0] = dot3(coefs, high_ref, low_ref).reshape(out_ref.shape[2:])


def sea_last_kernel(inside_ref, near_ref, own_ref, far_ref, out_ref):
    near = near_ref[pl.program_id(0)] == 1
    out_ref[0, 0] = jnp.where(near, own_ref[0, 0], far_ref[0, 0])


def resampled(kernel, inside, near, own, far, tables, lon_count):
    shape = own.shape[:-1] + (lon_count,)

    def parent(s, f, inside_ref, near_ref):
        return (inside_ref[s], f, 0, 0, 0)

    parent_spec = pl.BlockSpec((1, 1) + own.shape[2:], parent)
    return pl.pallas_call(
        kernel,
        grid_spec=pltpu.PrefetchScalarGridSpec(
            num_scalar_prefetch=2,
            grid=own.shape[:2],
            in_specs=[parent_spec, parent_spec] + [whole_spec(table) for table in tables],
            out_specs=state_spec(shape),
        ),
        out_shape=jax.ShapeDtypeStruct(shape, jnp.float32),
        compiler_params=large,
    )(inside, near, own, far, *tables)


def left3(high_ref, low_ref, value):
    high, low = split(value)
    total = jnp.dot(low_ref[...], high, preferred_element_type=jnp.float32)
    total = total + jnp.dot(high_ref[...], low, preferred_element_type=jnp.float32)
    return total + jnp.dot(high_ref[...], high, preferred_element_type=jnp.float32)


def filtered(value, squares_ref, rate_ref, forward, inverse):
    spectrum = left3(*forward, value) / (1.0 + rate_ref[0] * squares_ref[...])
    return left3(*inverse, spectrum)


def to_grid_kernel(x_ref, sq_ref, rate_ref, fh, fl, ih, il, gh, gl, out_ref):
    coefs = filtered(x_ref[0], sq_ref, rate_ref, (fh, fl), (ih, il))
    out_ref[0] = dot3(coefs, gh, gl)


def to_coefs_kernel(
    x_ref,
    o_ref,
    sst_ref,
    here_ref,
    there_ref,
    flag_ref,
    w_ref,
    sq_ref,
    rate_ref,
    fh,
    fl,
    ih,
    il,
    gh,
    gl,
    out_ref,
    sum_ref,
    forced,
):
    per = x_ref.shape[0]
    u = pl.program_id(0)
    mixing = here_ref[u, 0] * x_ref[0] + there_ref[u, 0] * o_ref[0]
    for v in range(1, per):
        mixing = mixing + here_ref[u, v] * x_ref[v] + there_ref[u, v] * o_ref[v]
    forced[...] = x_ref[u] + forcing_rate * jnp.tanh(mixing)

    @pl.when(jnp.logical_and(u == 0, flag_ref[0] == 1))
    def _():
        forced[...] += coupling_rate * (sst_ref[...] - x_ref[0])

    coefs = dot3(forced[...], gh, gl)
    result = filtered(coefs, sq_ref, rate_ref, (fh, fl), (ih, il))
    out_ref[0] = result

    @pl.when(u == 0)
    def _():
        total = jnp.sum(result[:, : w_ref.shape[1]] * w_ref[...], axis=0, keepdims=True)
        total = jnp.sum(total, axis=1, keepdims=True)
        sum_ref[...] = jnp.broadcast_to(total, sum_ref.shape)


def level_spec(shape):
    return pl.BlockSpec((1,) + tuple(shape[1:]), lambda u: (u, 0, 0))


def to_grid(value, squares, rate, tables, lon_count):
    shape = value.shape[:2] + (lon_count,)
    return pl.pallas_call(
        to_grid_kernel,
        grid=value.shape[:1],
        out_shape=jax.ShapeDtypeStruct(shape, jnp.float32),
        in_specs=[level_spec(value.shape), whole_spec(squares), scalar_spec()]
        + [whole_spec(table) for table in tables],
        out_specs=level_spec(shape),
        compiler_params=large,
    )(value, squares, rate, *tables)


def to_coefs(state, other, sst, mine, theirs, flag, weights, squares, rate, tables):
    shape = state.shape[:2] + (squares.shape[1],)
    return pl.pallas_call(
        to_coefs_kernel,
        grid=state.shape[:1],
        out_shape=[
            jax.ShapeDtypeStruct(shape, jnp.float32),
            jax.ShapeDtypeStruct((8, 128), jnp.float32),
        ],
        in_specs=[whole_spec(state), whole_spec(other), whole_spec(sst)]
        + [scalar_spec()] * 3
        + [whole_spec(weights), whole_spec(squares), scalar_spec()]
        + [whole_spec(table) for table in tables],
        out_specs=[level_spec(shape), pl.BlockSpec((8, 128), lambda u: (0, 0))],
        scratch_shapes=[pltpu.VMEM(state.shape[1:], jnp.float32)],
        compiler_params=large,
    )(state, other, sst, mine, theirs, flag, weights, squares, rate, *tables)


def by_units(
    member_state,
    layer_blend_operator,
    coefficient,
    interpolation_donor_meridians,
    land_sea,
    ancestry,
):
    member, component, tile = here()
    members, comps, tiles = (lax.axis_size(name) for name in ("member", "comp", "tile"))
    field = member_state[:, 0]
    slots, fields, levels, rows, lon_count = field.shape
    per = levels // members
    sizes = (members, comps, fields, tiles, rows)
    lon_basis, number = kept_lon_basis(lon_count)
    waves = lon_basis.shape[0]
    lon_columns = np.ascontiguousarray(lon_basis.T)
    lat_basis = lat_table()
    lat_tables = split_table(lat_basis) + split_table(np.ascontiguousarray(lat_basis.T))
    weights = row_weights()
    weight_total = float(weights.sum())
    order = np.arange(MODES).astype(np.float32)
    squares = order[:, None] ** 2 + number[None, :] ** 2
    squares = jnp.asarray((squares / np.float32(MODES * MODES)).astype(np.float32))
    air_weights = np.zeros((LAT, 128), np.float32)
    air_weights[:, 0] = weights * lon_basis[0, 0] / weight_total
    my_weights = lax.dynamic_slice_in_dim(jnp.asarray(weights[:, None]), tile * rows, rows)

    is_air = component == 0
    blend = layer_blend_operator[0]
    rate = coefficient[0]
    donors = interpolation_donor_meridians[0]
    edge_shape = (slots, fields, 2, levels, lon_count)
    halo_shape = (slots, fields, levels, lon_count)
    edge = jnp.stack([field[:, :, :, 0], field[:, :, :, -1]], axis=2)

    def within(low, high):
        return jnp.where(tile == 0, 0.0, low), jnp.where(tile == tiles - 1, 0.0, high)

    partner, other_donors, other_blend, other_rate, low, high = call(
        functools.partial(couple_kernel, sizes),
        4,
        [(slots, rows, lon_count), donors, blend, coefficient, halo_shape, halo_shape],
        (slots + 3, slots + 3, 2, 2),
        field,
        donors,
        blend,
        coefficient,
        edge,
    )
    low, high = within(low, high)
    air_blend = jnp.where(is_air, blend, other_blend)
    air_rate = jnp.where(is_air, rate, other_rate[0])

    def air_first(_):
        fourier = air_forward(field, partner, donors, blend, lon_columns)
        return (
            fourier,
            jnp.zeros((slots, rows, lon_count), jnp.float32),
            jnp.zeros(field.shape, jnp.float32),
            jnp.zeros(edge_shape, jnp.float32),
        )

    def sea_first(_):
        new, looked, edge, _ = sea_step(
            field, low, high, partner, donors, other_donors, land_sea, my_weights, blend, rate
        )
        return jnp.zeros((slots, fields, levels, rows, waves), jnp.float32), looked, new, edge

    fourier, looked, ocean, edge = lax.cond(is_air, air_first, sea_first, 0)
    gathered, sst, _, low, high = call(
        functools.partial(spread_kernel, sizes),
        0,
        [(per, LAT, waves), (LAT, lon_count), (fields, levels, rows, waves)] + [halo_shape] * 2,
        (members * fields,) * 3 + (comps, tiles, tiles, 2, 2, 2),
        fourier,
        looked,
        edge,
    )
    low, high = within(low, high)
    unit_field = tile % fields
    unit_rate = lax.dynamic_slice_in_dim(air_rate, unit_field, 1)
    state = to_grid(
        gathered, squares, unit_rate, lat_tables + split_table(lon_basis), lon_count
    )
    other_state, flux = call(
        functools.partial(swap_kernel, sizes),
        1,
        [(per, LAT, lon_count), (slots, rows, lon_count)],
        (1, 1, tiles, comps, 1),
        state,
    )
    mine = lax.dynamic_slice_in_dim(air_blend, member * per, per)
    mine_own = lax.dynamic_slice_in_dim(mine, member * per, per, axis=1)
    mine_other = lax.dynamic_slice_in_dim(mine, (1 - member) * per, per, axis=1)
    flag = jnp.logical_and(member == 0, unit_field == 0).astype(jnp.int32).reshape(1)
    back, air_point = to_coefs(
        state,
        other_state,
        sst,
        mine_own,
        mine_other,
        flag,
        jnp.asarray(air_weights),
        squares,
        unit_rate,
        lat_tables + split_table(lon_columns),
    )

    def sea_second(_):
        new, _, _, sums = sea_step(
            ocean, low, high, flux, donors, donors, land_sea, my_weights, blend, rate
        )
        return new, sums

    def air_second(_):
        return ocean, jnp.zeros((slots, 8, 128), jnp.float32)

    ocean, sums = lax.cond(is_air, air_second, sea_second, 0)
    own, far, air_scores, far_ocean, sea_parts = call(
        functools.partial(return_kernel, sizes),
        2,
        [(slots, fields, levels, rows, waves)] * 2
        + [(slots, 8, 128), field, (tiles, slots, 8, 128)],
        (tiles, slots * fields * members, slots * fields * members)
        + (slots * fields * members, tiles, comps, 3, 1, 1, tiles, tiles),
        back,
        air_point,
        ocean,
        sums,
    )
    parents = lax.dynamic_slice_in_dim(ancestry, member * slots, slots)

    inside = parents % slots
    near = (parents // slots == member).astype(jnp.int32)

    def air_last(_):
        grid = resampled(
            air_last_kernel, inside, near, own, far, split_table(lon_basis), lon_count
        )
        return grid.reshape(member_state.shape), air_scores[:, 0, :1]

    def sea_last(_):
        score = jnp.sum(sea_parts[:, :, 0, :1], axis=0) / weight_total
        states = resampled(sea_last_kernel, inside, near, ocean, far_ocean, (), lon_count)
        return states.reshape(member_state.shape), score

    return lax.cond(is_air, air_last, sea_last, 0)


def by_bands(
    member_state,
    layer_blend_operator,
    coefficient,
    interpolation_donor_meridians,
    land_sea,
    ancestry,
):
    slot_count = member_state.shape[0]
    component = lax.axis_index("comp")
    tile_index = lax.axis_index("tile")
    tile_count = lax.axis_size("tile")
    row_count = member_state.shape[4]
    lon_count = member_state.shape[5]
    lon_table, number = kept_lon_basis(lon_count)
    lon_basis = jnp.asarray(lon_table)
    local_modes = lon_table.shape[0] // tile_count
    my_numbers = lax.dynamic_slice_in_dim(jnp.asarray(number), tile_index * local_modes, local_modes)
    lat_basis = jnp.asarray(lat_table())
    order = jnp.arange(MODES, dtype=jnp.int32).astype(jnp.float32)
    sea_cells = land_sea[None, None] == 1
    diffusivity = coefficient[0][:, None, None, None]
    weights = row_weights()
    my_weights = lax.dynamic_slice_in_dim(jnp.asarray(weights), tile_index * row_count, row_count)
    weight_total = float(weights.sum())
    stepped_list = []
    partial_list = []
    for slot in range(slot_count):
        field = member_state[slot, 0]
        for _ in range(STEPS):
            surface = field[0, 0]
            partner = partner_2(surface, "comp", 0)
            received = donor_lookup(partner, interpolation_donor_meridians[0])
            mixing = jnp.einsum("uv,fvjx->fujx", layer_blend_operator[0], field, precision=precise)
            forced = field + forcing_rate * jnp.tanh(mixing)
            forced = forced.at[0, 0].add(coupling_rate * (received - surface))
            spectral_gain = 1.0 / (
                1.0
                + coefficient[0][:, None, None]
                * (order[None, None, :] ** 2 + my_numbers[None, :, None] ** 2)
                / (MODES * MODES)
            )
            fourier = jnp.einsum("fvjx,qx->fvjq", forced, lon_basis, precision=precise)
            spectrum = jnp.einsum(
                "lj,fkjq->fkql",
                lat_basis,
                lax.all_to_all(fourier, "tile", split_axis=3, concat_axis=2, tiled=True),
                precision=precise,
            )
            spectrum = spectrum * spectral_gain[:, None]
            returned = jnp.einsum("lj,fkql->fkjq", lat_basis, spectrum, precision=precise)
            filtered = lax.all_to_all(returned, "tile", split_axis=2, concat_axis=3, tiled=True)
            block_atm = jnp.einsum("fvjq,qx->fvjx", filtered, lon_basis, precision=precise)
            padded = padded_2(field, (("tile", 2),), 1)
            laplacian = (
                padded[:, :, 2:]
                + padded[:, :, :-2]
                + jnp.roll(field, 1, axis=3)
                + jnp.roll(field, -1, axis=3)
                - 4.0 * field
            )
            new_ocn = jnp.where(sea_cells, forced + diffusivity * laplacian, field)
            field = jnp.where(component == 0, block_atm, new_ocn)
        stepped_list.append(field)
        partial_list.append(jnp.sum(jnp.mean(field[0, 0], axis=1) * my_weights))
    local_states = jnp.stack(stepped_list)
    region_sums = lax.psum(jnp.stack(partial_list), "tile")
    region_score = (region_sums / weight_total).reshape(slot_count, 1)
    member_index = lax.axis_index("member")
    my_parents = lax.dynamic_slice_in_dim(ancestry, member_index * slot_count, slot_count)
    gathered = lax.all_gather(local_states, "member", axis=0, tiled=True)
    chosen = jnp.take(gathered, my_parents, axis=0)
    return (chosen[:, None], region_score)


def local(member_state, *others):
    members, comps, tiles = (lax.axis_size(name) for name in ("member", "comp", "tile"))
    slots, _, fields, levels, rows, _ = member_state.shape
    fits = members == 2 and comps == 2 and slots == comps and tiles == members * fields
    if fits and levels % members == 0 and rows % 8 == 0:
        return by_units(member_state, *others)
    return by_bands(member_state, *others)


def solution(mesh):
    return jax.shard_map(
        local,
        mesh=mesh,
        in_specs=(
            P("member", "comp", None, None, "tile", None),
            P("comp", None, None),
            P("comp", None),
            P("comp", "tile", None),
            P("tile", None),
            P(),
        ),
        out_specs=(P("member", "comp", None, None, "tile", None), P("member", "comp")),
        check_vma=False,
    )
```

```python
import functools
import math

import jax
import jax.numpy as jnp
import numpy as np
from jax import lax
from jax.experimental import pallas as pl
from jax.experimental.pallas import tpu as pltpu
from jax.sharding import PartitionSpec as P

LAT = 384
MODES = 256
STEPS = 2
MESH = pl.DeviceIdType.MESH


coupling_rate = 0.5
forcing_rate = 0.5
precise = lax.Precision.HIGH


def partner_2(value, axis, distance):
    mask = 2**distance
    pairs = [(source, source ^ mask) for source in range(lax.axis_size(axis))]
    return lax.ppermute(value, axis, pairs)


def padded_2(block, sides, width):
    for axis, dim in sides:
        count = lax.axis_size(axis)
        forward = [(i, i + 1) for i in range(count - 1)]
        backward = [(target, source) for source, target in forward]
        low = lax.ppermute(
            lax.slice_in_dim(block, block.shape[dim] - width, None, axis=dim), axis, forward
        )
        high = lax.ppermute(lax.slice_in_dim(block, 0, width, axis=dim), axis, backward)
        block = jnp.concatenate([low, block, high], axis=dim)
    return block


def kept_lon_basis(lon_count):
    wave = np.arange(2 * MODES)
    is_cosine = wave < MODES
    number = np.where(is_cosine, wave, wave - MODES + 1).astype(np.float32)
    cells = np.arange(lon_count).astype(np.float32)
    angle = np.float32(2.0 * math.pi) * number[:, None] * cells[None, :] / np.float32(lon_count)
    scale = np.where(number == 0.0, math.sqrt(1.0 / lon_count), math.sqrt(2.0 / lon_count)).astype(
        np.float32
    )
    table = np.where(is_cosine[:, None], np.cos(angle), np.sin(angle)) * scale[:, None]
    return table.astype(np.float32), number


def lat_table():
    order = np.arange(MODES).astype(np.float32)
    cells = np.arange(LAT).astype(np.float32)
    scale = np.where(order == 0.0, math.sqrt(1.0 / LAT), math.sqrt(2.0 / LAT)).astype(np.float32)
    angle = np.float32(math.pi) * (cells[None, :] + np.float32(0.5)) * order[:, None]
    return (np.cos(angle / np.float32(LAT)) * scale[:, None]).astype(np.float32)


def row_weights():
    rows = np.arange(LAT).astype(np.float32)
    return np.cos(
        np.float32(math.pi) * ((rows + np.float32(0.5)) / np.float32(LAT) - np.float32(0.5))
    ).astype(np.float32)


def donor_lookup(partner, donors):
    lon_count = partner.shape[-1]
    cells = jnp.arange(lon_count, dtype=jnp.int32)[None, :]
    offsets = jnp.mod(donors - cells, lon_count)
    result = jnp.zeros_like(partner)
    for shift_by in (-1, 0, 1, 2, 3, 4):
        moved = jnp.roll(partner, -shift_by, axis=-1)
        result = result + jnp.where(offsets == shift_by % lon_count, moved, 0.0)
    return result


def remote(src, dst, send_sem, recv_sem, device):
    return pltpu.make_async_remote_copy(
        src_ref=src,
        dst_ref=dst,
        send_sem=send_sem,
        recv_sem=recv_sem,
        device_id=device,
        device_id_type=MESH,
    )


def here():
    return lax.axis_index("member"), lax.axis_index("comp"), lax.axis_index("tile")


def greet(targets, count):
    barrier = pltpu.get_barrier_semaphore()
    for condition, device in targets:

        @pl.when(condition)
        def _():
            pl.semaphore_signal(barrier, inc=1, device_id=device, device_id_type=MESH)

    @pl.when(count > 0)
    def _():
        pl.semaphore_wait(barrier, count)


def differs(a, b):
    return jnp.logical_or(a[0] != b[0], jnp.logical_or(a[1] != b[1], a[2] != b[2]))


def shores(y, t, tiles):
    return jnp.logical_and(y == 1, t > 0), jnp.logical_and(y == 1, t < tiles - 1)


def edge_copies(edge_ref, low_ref, high_ref, esend, erecv, m, y, t):
    up = remote(edge_ref.at[:, :, 0], high_ref, esend.at[0], erecv.at[0], (m, y, t - 1))
    down = remote(edge_ref.at[:, :, 1], low_ref, esend.at[1], erecv.at[1], (m, y, t + 1))
    return up, down


def couple_kernel(
    sizes,
    field_ref,
    donors_ref,
    blend_ref,
    rate_ref,
    edge_ref,
    partner_ref,
    odonors_ref,
    oblend_ref,
    orate_ref,
    low_ref,
    high_ref,
    send,
    recv,
    esend,
    erecv,
):
    members, comps, fields, tiles, rows = sizes
    m, y, t = here()
    other = (m, 1 - y, t)
    north, south = shores(y, t, tiles)
    targets = [(m >= 0, other), (north, (m, y, t - 1)), (south, (m, y, t + 1))]
    greet(targets, 1 + north.astype(jnp.int32) + south.astype(jnp.int32))
    slots = partner_ref.shape[0]
    pairs = [(field_ref.at[s, 0, 0], partner_ref.at[s]) for s in range(slots)]
    pairs += [(donors_ref, odonors_ref), (blend_ref, oblend_ref), (rate_ref, orate_ref)]
    copies = [remote(a, b, send.at[k], recv.at[k], other) for k, (a, b) in enumerate(pairs)]
    up, down = edge_copies(edge_ref, low_ref, high_ref, esend, erecv, m, y, t)
    for copy in copies:
        copy.start()
    pl.when(north)(up.start)
    pl.when(south)(down.start)
    for copy in copies:
        copy.wait()
    pl.when(north)(up.wait_send)
    pl.when(south)(down.wait_send)
    pl.when(south)(up.wait_recv)
    pl.when(north)(down.wait_recv)


def spread_kernel(
    sizes,
    c_ref,
    r_ref,
    edge_ref,
    u_ref,
    ru_ref,
    h_ref,
    low_ref,
    high_ref,
    send,
    hsend,
    hrecv,
    rsend,
    recv,
    rrecv,
    loc,
    esend,
    erecv,
):
    members, comps, fields, tiles, rows = sizes
    me = m, y, t = here()
    per = c_ref.shape[2] // members
    unit_m, unit_f = t // fields, t % fields
    has_surface = jnp.logical_and(m == 0, unit_f == 0)
    north, south = shores(y, t, tiles)
    targets = [(y == 1, (m, 0, t)), (north, (m, y, t - 1)), (south, (m, y, t + 1))]
    up, down = edge_copies(edge_ref, low_ref, high_ref, esend, erecv, m, y, t)
    for j in range(tiles):
        source = (unit_m, y, j)
        targets.append((differs(source, me), source))
    for j in range(tiles):
        source = (unit_m, 1, j)
        targets.append((jnp.logical_and(has_surface, differs(source, me)), source))
    self_unit = (unit_m == m).astype(jnp.int32)
    self_surface = jnp.logical_and(has_surface, unit_m == m).astype(jnp.int32)
    count = members * fields - self_unit + jnp.where(y == 0, 1, comps - self_surface)
    greet(targets, count + north.astype(jnp.int32) + south.astype(jnp.int32))
    pl.when(north)(up.start)
    pl.when(south)(down.start)

    def rows_of(j):
        return pl.ds(pl.multiple_of(j * rows, 8), rows)

    pieces = [(f, c) for f in range(fields) for c in range(members)]

    def place(k):
        f, c = pieces[k]
        return lax.rem(f + t, fields), c

    def piece(k, ref):
        f, c = place(k)
        device = (c, y, m * fields + f)
        src = ref.at[f, pl.ds(c * per, per)]
        dst = u_ref.at[:, rows_of(t), :]
        copy = remote(src, dst, send.at[k], recv.at[t], device)
        return differs(device, me), copy, pltpu.make_async_copy(src, dst, loc.at[0])

    def hop(k):
        f, c = place(k)
        part = (f, pl.ds(c * per, per))
        return remote(
            c_ref.at[(1,) + part], h_ref.at[part], hsend.at[k], hrecv.at[k], (m, 1 - y, t)
        )

    def surface(s):
        device = (0, s, m * fields)
        dst = ru_ref.at[rows_of(t), :]
        copy = remote(r_ref.at[s], dst, rsend.at[s], rrecv.at[t], device)
        return differs(device, me), copy, pltpu.make_async_copy(r_ref.at[s], dst, loc.at[1])

    def begin(parts):
        away, copy, local = parts
        pl.when(away)(copy.start)
        pl.when(jnp.logical_not(away))(local.start)

    def end(parts):
        away, copy, local = parts
        pl.when(away)(copy.wait_send)
        pl.when(jnp.logical_not(away))(local.wait)

    @pl.when(y == 0)
    def _():
        for k in range(len(pieces)):
            hop(k).start()
            begin(piece(k, c_ref.at[0]))

    @pl.when(y == 1)
    def _():
        for s in range(comps):
            begin(surface(s))
        for k in range(len(pieces)):
            hop(k).wait_recv()
            begin(piece(k, h_ref))

    for j in range(tiles):
        away = differs((unit_m, y, j), me)
        part = u_ref.at[:, rows_of(j), :]
        arrival = remote(part, part, send.at[0], recv.at[j], me)
        pl.when(away)(arrival.wait_recv)
        late = remote(
            ru_ref.at[rows_of(j), :], ru_ref.at[rows_of(j), :], rsend.at[0], rrecv.at[j], me
        )
        away = jnp.logical_and(has_surface, differs((unit_m, 1, j), me))
        pl.when(away)(late.wait_recv)

    @pl.when(y == 0)
    def _():
        for k in range(len(pieces)):
            hop(k).wait_send()
            end(piece(k, c_ref.at[0]))

    @pl.when(y == 1)
    def _():
        for s in range(comps):
            end(surface(s))
        for k in range(len(pieces)):
            end(piece(k, h_ref))

    pl.when(north)(up.wait_send)
    pl.when(south)(down.wait_send)
    pl.when(south)(up.wait_recv)
    pl.when(north)(down.wait_recv)


def swap_kernel(sizes, x_ref, xo_ref, send, recv):
    m, y, t = here()
    other = (1 - m, y, t)
    greet([(m >= 0, other)], 1)
    across = remote(x_ref, xo_ref, send.at[0], recv.at[0], other)
    across.start()
    across.wait()


def return_kernel(
    sizes,
    f_ref,
    p_ref,
    x_ref,
    o_ref,
    low_ref,
    high_ref,
    donors_ref,
    land_ref,
    weight_ref,
    blend_ref,
    rate_ref,
    own_ref,
    far_ref,
    score_ref,
    new_ref,
    faro_ref,
    part_ref,
    before,
    after,
    flux,
    sums,
    send,
    recv,
    fsend,
    frecv,
    psend,
    precv,
    loc,
    osend,
    orecv,
    keep,
    qsend,
    qrecv,
    ssend,
    srecv,
):
    members, comps, fields, tiles, rows = sizes
    me = m, y, t = here()
    per = f_ref.shape[0]
    unit_m, unit_f = t // fields, t % fields
    has_surface = jnp.logical_and(m == 0, unit_f == 0)
    other = (1 - m, y, t)
    pieces = [(s, f, c) for s in range(comps) for f in range(fields) for c in range(members)]
    targets = [(m >= 0, other)]
    for j in range(tiles):
        targets.append((jnp.logical_and(y == 1, j != t), (m, y, j)))
    for s in range(comps):
        source = (0, s, m * fields)
        targets.append((jnp.logical_and(y == 1, differs(source, me)), source))
    for s, f, c in pieces:
        source = (c, s, m * fields + f)
        targets.append((jnp.logical_and(y == 0, differs(source, me)), source))
    own_unit = jnp.logical_and(y == 0, unit_m == m).astype(jnp.int32)
    own_surface = jnp.logical_and(has_surface, jnp.logical_and(y == 1, unit_m == m))
    count = tiles - own_unit + jnp.where(y == 0, 1, tiles)
    greet(targets, count + jnp.where(has_surface, tiles - own_surface.astype(jnp.int32), 0))
    load = pltpu.make_async_copy(o_ref, before, loc.at[2])
    pl.when(y == 1)(load.start)

    def share(j):
        return remote(sums, part_ref.at[t], qsend.at[j], qrecv.at[t], (m, y, j))

    def surface(j):
        device = (unit_m, 1, j)
        part = x_ref.at[0, pl.ds(j * rows, rows), :]
        copy = remote(part, flux.at[y], ssend.at[j], srecv.at[y], device)
        return differs(device, me), copy, pltpu.make_async_copy(part, flux.at[y], loc.at[3])

    @pl.when(has_surface)
    def _():
        for j in range(tiles):
            away, copy, local = surface(j)
            pl.when(away)(copy.start)
            pl.when(jnp.logical_not(away))(local.start)

    def band(j):
        device = (unit_m, 0, j)
        src = f_ref.at[:, pl.ds(j * rows, rows), :]
        dst = own_ref.at[y, unit_f, pl.ds(m * per, per)]
        slot = (y * fields + unit_f) * members + m
        return (
            device,
            remote(src, dst, send.at[j], recv.at[slot], device),
            pltpu.make_async_copy(src, dst, loc.at[0]),
            remote(p_ref, score_ref.at[y], psend.at[j], precv.at[y], device),
            pltpu.make_async_copy(p_ref, score_ref.at[y], loc.at[1]),
        )

    for j in range(tiles):
        device, copy, local, point, local_point = band(j)
        away = differs(device, me)
        pl.when(away)(copy.start)
        pl.when(jnp.logical_not(away))(local.start)
        pl.when(jnp.logical_and(has_surface, away))(point.start)
        pl.when(jnp.logical_and(has_surface, jnp.logical_not(away)))(local_point.start)

    def forward(k):
        s, f, c = pieces[k]
        part = (s, f, pl.ds(c * per, per))
        return remote(own_ref.at[part], far_ref.at[part], fsend.at[k], frecv.at[k], other)

    @pl.when(y == 0)
    def _():
        for k, (s, f, c) in enumerate(pieces):
            part = own_ref.at[s, f, pl.ds(c * per, per)]
            away = differs((c, s, m * fields + f), me)
            arrival = remote(part, part, send.at[0], recv.at[k], me)
            pl.when(away)(arrival.wait_recv)
            own = pltpu.make_async_copy(part, part, loc.at[0])
            pl.when(jnp.logical_not(away))(own.wait)
            forward(k).start()
        for s in range(comps):
            away = differs((0, s, m * fields), me)
            arrival = remote(score_ref.at[s], score_ref.at[s], psend.at[0], precv.at[s], me)
            pl.when(away)(arrival.wait_recv)
            own = pltpu.make_async_copy(p_ref, score_ref.at[s], loc.at[1])
            pl.when(jnp.logical_not(away))(own.wait)
        for k in range(len(pieces)):
            forward(k).wait()

    for j in range(tiles):
        device, copy, local, point, local_point = band(j)
        away = differs(device, me)
        pl.when(away)(copy.wait_send)
        pl.when(jnp.logical_and(has_surface, away))(point.wait_send)

    def clone(s, f):
        i = s * fields + f
        part = (s, f)
        return (
            remote(after.at[part], faro_ref.at[part], osend.at[i], orecv.at[i], other),
            pltpu.make_async_copy(after.at[part], new_ref.at[part], keep.at[i]),
        )

    @pl.when(y == 1)
    def _():
        load.wait()
        for s in range(comps):
            away = differs((0, s, m * fields), me)
            arrival = remote(flux.at[s], flux.at[s], ssend.at[0], srecv.at[s], me)
            pl.when(away)(arrival.wait_recv)
            own = pltpu.make_async_copy(x_ref.at[0, pl.ds(0, rows), :], flux.at[s], loc.at[3])
            pl.when(jnp.logical_not(away))(own.wait)
        sea = land_ref[...] == 1

        def step(i, _):
            s, f = lax.div(i, fields), lax.rem(i, fields)
            levels = before.shape[2]
            for u in range(levels):
                mixing = blend_ref[u, 0] * before[s, f, 0]
                for v in range(1, levels):
                    mixing = mixing + blend_ref[u, v] * before[s, f, v]
                value = before[s, f, u]
                forced = value + forcing_rate * jnp.tanh(mixing)
                ends = (low_ref[s, f, u : u + 1], high_ref[s, f, u : u + 1])
                forced = forced + rate_ref[f] * laplacian_of(value, *ends)
                after[s, f, u] = jnp.where(sea, forced, value)

            @pl.when(f == 0)
            def _():
                value = before[s, 0, 0]
                extra = coupling_rate * (lookup(flux[s], donors_ref[...]) - value)
                result = after[s, 0, 0] + jnp.where(sea, extra, 0.0)
                after[s, 0, 0] = result
                sums[s] = weighted_sum(result, weight_ref[...], sums.shape[1:])

            across, own = clone(s, f)
            across.start()
            own.start()
            return 0

        lax.fori_loop(0, comps * fields, step, 0)
        mine = pltpu.make_async_copy(sums, part_ref.at[t], loc.at[4])
        mine.start()
        for j in range(tiles):
            pl.when(j != t)(share(j).start)
        mine.wait()
        for j in range(tiles):
            arrival = remote(part_ref.at[j], part_ref.at[j], qsend.at[0], qrecv.at[j], me)
            pl.when(j != t)(arrival.wait_recv)
            pl.when(j != t)(share(j).wait_send)
        for s in range(comps):
            for f in range(fields):
                across, own = clone(s, f)
                across.wait()
                own.wait()

    @pl.when(has_surface)
    def _():
        for j in range(tiles):
            away, copy, local = surface(j)
            pl.when(away)(copy.wait_send)


def laplacian_of(value, low, high):
    rows, lon_count = value.shape
    row = lax.broadcasted_iota(jnp.int32, (rows, lon_count), 0)
    north = jnp.where(row == 0, low, pltpu.roll(value, 1, 0))
    south = jnp.where(row == rows - 1, high, pltpu.roll(value, rows - 1, 0))
    east, west = pltpu.roll(value, 1, 1), pltpu.roll(value, lon_count - 1, 1)
    return south + north + east + west - 4.0 * value


def weighted_sum(value, weights, shape):
    total = jnp.sum(value * weights, axis=0, keepdims=True)
    total = jnp.sum(total, axis=1, keepdims=True) / value.shape[1]
    return jnp.broadcast_to(total, shape)


def call(kernel, collective_id, outs, sems, *args):
    return pl.pallas_call(
        kernel,
        out_shape=[
            jax.ShapeDtypeStruct(out.shape, out.dtype)
            if hasattr(out, "dtype")
            else jax.ShapeDtypeStruct(out, jnp.float32)
            for out in outs
        ],
        in_specs=[pl.BlockSpec(memory_space=pl.ANY)] * len(args),
        out_specs=[pl.BlockSpec(memory_space=pl.ANY)] * len(outs),
        scratch_shapes=[pltpu.SemaphoreType.DMA((n,)) for n in sems],
        compiler_params=pltpu.CompilerParams(collective_id=collective_id, has_side_effects=True),
    )(*args)


def matmul(a, b):
    return jnp.dot(a, b, precision=precise, preferred_element_type=jnp.float32)


def split(value):
    high = value.astype(jnp.bfloat16)
    return high, (value - high.astype(jnp.float32)).astype(jnp.bfloat16)


def split_table(table):
    high = table.astype(jnp.bfloat16)
    low = (table - high.astype(np.float32)).astype(jnp.bfloat16)
    return jnp.asarray(high), jnp.asarray(low)


def dot3(value, high_ref, low_ref):
    high, low = split(value)
    total = jnp.dot(high, low_ref[...], preferred_element_type=jnp.float32)
    total = total + jnp.dot(low, high_ref[...], preferred_element_type=jnp.float32)
    return total + jnp.dot(high, high_ref[...], preferred_element_type=jnp.float32)


def lookup(surface, donors):
    lon_count = surface.shape[-1]
    offset = donors - lax.broadcasted_iota(jnp.int32, donors.shape, 1)
    offset = jnp.where(offset > lon_count // 2, offset - lon_count, offset)
    offset = jnp.where(offset < -(lon_count // 2), offset + lon_count, offset)
    result = surface
    for shift in (-1, 1, 2, 3, 4):
        moved = pltpu.roll(surface, (-shift) % lon_count, 1)
        result = jnp.where(offset == shift, moved, result)
    return result


def mixed_level(blend_ref, field_ref, u):
    levels = field_ref.shape[2]
    total = blend_ref[u, 0] * field_ref[0, 0, 0]
    for v in range(1, levels):
        total = total + blend_ref[u, v] * field_ref[0, 0, v]
    return forcing_rate * jnp.tanh(total)


def air_kernel(field_ref, partner_ref, donors_ref, blend_ref, high_ref, low_ref, out_ref, forced):
    levels, rows = field_ref.shape[2:4]
    for u in range(levels):
        forced[u * rows : (u + 1) * rows] = field_ref[0, 0, u] + mixed_level(blend_ref, field_ref, u)

    @pl.when(pl.program_id(1) == 0)
    def _():
        received = lookup(partner_ref[0], donors_ref[...])
        forced[:rows] += coupling_rate * (received - field_ref[0, 0, 0])

    out_ref[0, 0] = dot3(forced[...], high_ref, low_ref).reshape(out_ref.shape[2:])


def sea_kernel(
    field_ref,
    low_ref,
    high_ref,
    partner_ref,
    donors_ref,
    next_ref,
    land_ref,
    blend_ref,
    rate_ref,
    out_ref,
    look_ref,
    edge_ref,
):
    levels, rows, lon_count = field_ref.shape[2:]
    rate = rate_ref[pl.program_id(1)]
    sea = land_ref[...] == 1
    first = pl.program_id(1) == 0
    for u in range(levels):
        value = field_ref[0, 0, u]
        forced = value + mixed_level(blend_ref, field_ref, u)
        ends = (low_ref[0, 0, u : u + 1], high_ref[0, 0, u : u + 1])
        laplacian = laplacian_of(value, *ends)
        if u == 0:
            received = lookup(partner_ref[0], donors_ref[...])
            extra = coupling_rate * (received - value)
            forced = forced + jnp.where(first, extra, 0.0)
        result = jnp.where(sea, forced + rate * laplacian, value)
        out_ref[0, 0, u] = result
        edge_ref[0, 0, 0, u : u + 1] = result[:1]
        edge_ref[0, 0, 1, u : u + 1] = result[rows - 1 :]

    @pl.when(first)
    def _():
        look_ref[0] = lookup(out_ref[0, 0, 0], next_ref[...])


def whole_spec(array):
    zeros = (0,) * array.ndim
    return pl.BlockSpec(array.shape, lambda *_: zeros)


def scalar_spec():
    return pl.BlockSpec(memory_space=pltpu.SMEM)


def state_spec(shape):
    zeros = (0,) * (len(shape) - 2)
    return pl.BlockSpec((1, 1) + tuple(shape[2:]), lambda s, f, *_: (s, f) + zeros)


def surface_spec(shape):
    return pl.BlockSpec((1,) + tuple(shape[1:]), lambda s, f, *_: (s, 0, 0))


large = pltpu.CompilerParams(vmem_limit_bytes=40 * 1024 * 1024)


def air_forward(field, partner, donors, blend, table):
    slots, fields, levels, rows, lon_count = field.shape
    high, low = split_table(table)
    shape = field.shape[:-1] + (table.shape[1],)
    return pl.pallas_call(
        air_kernel,
        grid=(slots, fields),
        out_shape=jax.ShapeDtypeStruct(shape, jnp.float32),
        in_specs=[
            state_spec(field.shape),
            surface_spec(partner.shape),
            whole_spec(donors),
            scalar_spec(),
            whole_spec(high),
            whole_spec(low),
        ],
        out_specs=state_spec(shape),
        scratch_shapes=[pltpu.VMEM((levels * rows, lon_count), jnp.float32)],
        compiler_params=large,
    )(field, partner, donors, blend, high, low)


def sea_step(field, low, high, partner, donors, following, land_sea, blend, rate):
    slots, fields, levels, rows, lon_count = field.shape
    edge = (slots, fields, 2, levels, lon_count)
    return pl.pallas_call(
        sea_kernel,
        grid=field.shape[:2],
        out_shape=[
            jax.ShapeDtypeStruct(field.shape, jnp.float32),
            jax.ShapeDtypeStruct(partner.shape, jnp.float32),
            jax.ShapeDtypeStruct(edge, jnp.float32),
        ],
        in_specs=[
            state_spec(field.shape),
            state_spec(low.shape),
            state_spec(high.shape),
            surface_spec(partner.shape),
            whole_spec(donors),
            whole_spec(following),
            whole_spec(land_sea),
            scalar_spec(),
            scalar_spec(),
        ],
        out_specs=[
            state_spec(field.shape),
            surface_spec(partner.shape),
            state_spec(edge),
        ],
        compiler_params=large,
    )(field, low, high, partner, donors, following, land_sea, blend, rate)


def air_last_kernel(inside_ref, near_ref, own_ref, far_ref, high_ref, low_ref, out_ref):
    near = near_ref[pl.program_id(0)] == 1
    levels, rows, waves = own_ref.shape[2:]
    coefs = jnp.where(near, own_ref[0, 0], far_ref[0, 0]).reshape(levels * rows, waves)
    out_ref[0, 0] = dot3(coefs, high_ref, low_ref).reshape(out_ref.shape[2:])


def sea_last_kernel(inside_ref, near_ref, own_ref, far_ref, out_ref):
    near = near_ref[pl.program_id(0)] == 1
    out_ref[0, 0] = jnp.where(near, own_ref[0, 0], far_ref[0, 0])


def resampled(kernel, inside, near, own, far, tables, lon_count):
    shape = own.shape[:-1] + (lon_count,)

    def parent(s, f, inside_ref, near_ref):
        return (inside_ref[s], f, 0, 0, 0)

    parent_spec = pl.BlockSpec((1, 1) + own.shape[2:], parent)
    return pl.pallas_call(
        kernel,
        grid_spec=pltpu.PrefetchScalarGridSpec(
            num_scalar_prefetch=2,
            grid=own.shape[:2],
            in_specs=[parent_spec, parent_spec] + [whole_spec(table) for table in tables],
            out_specs=state_spec(shape),
        ),
        out_shape=jax.ShapeDtypeStruct(shape, jnp.float32),
        compiler_params=large,
    )(inside, near, own, far, *tables)


def edge_kernel(top_ref, bottom_ref, edge_ref):
    for u in range(top_ref.shape[2]):
        edge_ref[0, 0, 0, u : u + 1] = top_ref[0, 0, u, :1]
        edge_ref[0, 0, 1, u : u + 1] = bottom_ref[0, 0, u, 7:]


def edge_rows(field):
    slots, fields, levels, rows, lon_count = field.shape
    edge = (slots, fields, 2, levels, lon_count)
    block = (1, 1, levels, 8, lon_count)
    last = rows // 8 - 1
    return pl.pallas_call(
        edge_kernel,
        grid=(slots, fields),
        out_shape=jax.ShapeDtypeStruct(edge, jnp.float32),
        in_specs=[
            pl.BlockSpec(block, lambda s, f: (s, f, 0, 0, 0)),
            pl.BlockSpec(block, lambda s, f: (s, f, 0, last, 0)),
        ],
        out_specs=state_spec(edge),
    )(field, field)


def left3(high_ref, low_ref, value):
    high, low = split(value)
    total = jnp.dot(low_ref[...], high, preferred_element_type=jnp.float32)
    total = total + jnp.dot(high_ref[...], low, preferred_element_type=jnp.float32)
    return total + jnp.dot(high_ref[...], high, preferred_element_type=jnp.float32)


def filtered(value, squares_ref, rate_ref, forward, inverse):
    spectrum = left3(*forward, value) / (1.0 + rate_ref[0] * squares_ref[...])
    return left3(*inverse, spectrum)


def to_grid_kernel(x_ref, sq_ref, rate_ref, fh, fl, ih, il, gh, gl, out_ref):
    coefs = filtered(x_ref[0], sq_ref, rate_ref, (fh, fl), (ih, il))
    out_ref[0] = dot3(coefs, gh, gl)


def to_coefs_kernel(
    x_ref,
    o_ref,
    sst_ref,
    here_ref,
    there_ref,
    flag_ref,
    w_ref,
    sq_ref,
    rate_ref,
    fh,
    fl,
    ih,
    il,
    gh,
    gl,
    out_ref,
    sum_ref,
    forced,
):
    per = x_ref.shape[0]
    u = pl.program_id(0)
    mixing = here_ref[u, 0] * x_ref[0] + there_ref[u, 0] * o_ref[0]
    for v in range(1, per):
        mixing = mixing + here_ref[u, v] * x_ref[v] + there_ref[u, v] * o_ref[v]
    forced[...] = x_ref[u] + forcing_rate * jnp.tanh(mixing)

    @pl.when(jnp.logical_and(u == 0, flag_ref[0] == 1))
    def _():
        forced[...] += coupling_rate * (sst_ref[...] - x_ref[0])

    coefs = dot3(forced[...], gh, gl)
    result = filtered(coefs, sq_ref, rate_ref, (fh, fl), (ih, il))
    out_ref[0] = result

    @pl.when(u == 0)
    def _():
        total = jnp.sum(result[:, : w_ref.shape[1]] * w_ref[...], axis=0, keepdims=True)
        total = jnp.sum(total, axis=1, keepdims=True)
        sum_ref[...] = jnp.broadcast_to(total, sum_ref.shape)


def level_spec(shape):
    return pl.BlockSpec((1,) + tuple(shape[1:]), lambda u: (u, 0, 0))


def to_grid(value, squares, rate, tables, lon_count):
    shape = value.shape[:2] + (lon_count,)
    return pl.pallas_call(
        to_grid_kernel,
        grid=value.shape[:1],
        out_shape=jax.ShapeDtypeStruct(shape, jnp.float32),
        in_specs=[level_spec(value.shape), whole_spec(squares), scalar_spec()]
        + [whole_spec(table) for table in tables],
        out_specs=level_spec(shape),
        compiler_params=large,
    )(value, squares, rate, *tables)


def to_coefs(state, other, sst, mine, theirs, flag, weights, squares, rate, tables):
    shape = state.shape[:2] + (squares.shape[1],)
    return pl.pallas_call(
        to_coefs_kernel,
        grid=state.shape[:1],
        out_shape=[
            jax.ShapeDtypeStruct(shape, jnp.float32),
            jax.ShapeDtypeStruct((8, 128), jnp.float32),
        ],
        in_specs=[whole_spec(state), whole_spec(other), whole_spec(sst)]
        + [scalar_spec()] * 3
        + [whole_spec(weights), whole_spec(squares), scalar_spec()]
        + [whole_spec(table) for table in tables],
        out_specs=[level_spec(shape), pl.BlockSpec((8, 128), lambda u: (0, 0))],
        scratch_shapes=[pltpu.VMEM(state.shape[1:], jnp.float32)],
        compiler_params=large,
    )(state, other, sst, mine, theirs, flag, weights, squares, rate, *tables)


def by_units(
    member_state,
    layer_blend_operator,
    coefficient,
    interpolation_donor_meridians,
    land_sea,
    ancestry,
):
    member, component, tile = here()
    members, comps, tiles = (lax.axis_size(name) for name in ("member", "comp", "tile"))
    field = member_state[:, 0]
    slots, fields, levels, rows, lon_count = field.shape
    per = levels // members
    sizes = (members, comps, fields, tiles, rows)
    lon_basis, number = kept_lon_basis(lon_count)
    waves = lon_basis.shape[0]
    lon_columns = np.ascontiguousarray(lon_basis.T)
    lat_basis = lat_table()
    lat_tables = split_table(lat_basis) + split_table(np.ascontiguousarray(lat_basis.T))
    weights = row_weights()
    weight_total = float(weights.sum())
    order = np.arange(MODES).astype(np.float32)
    squares = order[:, None] ** 2 + number[None, :] ** 2
    squares = jnp.asarray((squares / np.float32(MODES * MODES)).astype(np.float32))
    air_weights = np.zeros((LAT, 128), np.float32)
    air_weights[:, 0] = weights * lon_basis[0, 0] / weight_total
    my_weights = lax.dynamic_slice_in_dim(jnp.asarray(weights[:, None]), tile * rows, rows)

    is_air = component == 0
    blend = layer_blend_operator[0]
    rate = coefficient[0]
    donors = interpolation_donor_meridians[0]
    edge_shape = (slots, fields, 2, levels, lon_count)
    halo_shape = (slots, fields, levels, lon_count)
    edge = edge_rows(field)

    def within(low, high):
        return jnp.where(tile == 0, 0.0, low), jnp.where(tile == tiles - 1, 0.0, high)

    partner, other_donors, other_blend, other_rate, low, high = call(
        functools.partial(couple_kernel, sizes),
        4,
        [(slots, rows, lon_count), donors, blend, coefficient, halo_shape, halo_shape],
        (slots + 3, slots + 3, 2, 2),
        field,
        donors,
        blend,
        coefficient,
        edge,
    )
    low, high = within(low, high)
    air_blend = jnp.where(is_air, blend, other_blend)
    air_rate = jnp.where(is_air, rate, other_rate[0])

    def air_first(_):
        fourier = air_forward(field, partner, donors, blend, lon_columns)
        return (
            fourier,
            jnp.zeros((slots, rows, lon_count), jnp.float32),
            jnp.zeros(field.shape, jnp.float32),
            jnp.zeros(edge_shape, jnp.float32),
        )

    def sea_first(_):
        new, looked, edge = sea_step(
            field, low, high, partner, donors, other_donors, land_sea, blend, rate
        )
        return jnp.zeros((slots, fields, levels, rows, waves), jnp.float32), looked, new, edge

    fourier, looked, ocean, edge = lax.cond(is_air, air_first, sea_first, 0)
    gathered, sst, _, low, high = call(
        functools.partial(spread_kernel, sizes),
        0,
        [(per, LAT, waves), (LAT, lon_count), (fields, levels, rows, waves)] + [halo_shape] * 2,
        (members * fields,) * 3 + (comps, tiles, tiles, 2, 2, 2),
        fourier,
        looked,
        edge,
    )
    low, high = within(low, high)
    unit_field = tile % fields
    unit_rate = lax.dynamic_slice_in_dim(air_rate, unit_field, 1)
    state = to_grid(
        gathered, squares, unit_rate, lat_tables + split_table(lon_basis), lon_count
    )
    (other_state,) = call(
        functools.partial(swap_kernel, sizes), 1, [(per, LAT, lon_count)], (1, 1), state
    )
    mine = lax.dynamic_slice_in_dim(air_blend, member * per, per)
    mine_own = lax.dynamic_slice_in_dim(mine, member * per, per, axis=1)
    mine_other = lax.dynamic_slice_in_dim(mine, (1 - member) * per, per, axis=1)
    flag = jnp.logical_and(member == 0, unit_field == 0).astype(jnp.int32).reshape(1)
    back, air_point = to_coefs(
        state,
        other_state,
        sst,
        mine_own,
        mine_other,
        flag,
        jnp.asarray(air_weights),
        squares,
        unit_rate,
        lat_tables + split_table(lon_columns),
    )

    count = slots * fields * members
    anywhere = pl.BlockSpec(memory_space=pl.ANY)
    inside = pl.BlockSpec(memory_space=pltpu.VMEM)
    coefs_shape = (slots, fields, levels, rows, waves)
    out_shapes = [coefs_shape, coefs_shape, (slots, 8, 128)]
    out_shapes += [field.shape, field.shape, (tiles, slots, 8, 128)]
    scratch = [field.shape, field.shape, (slots, rows, lon_count), (slots, 8, 128)]
    sems = (tiles, count, count, count, tiles, comps, 5)
    sems += (slots * fields,) * 3 + (tiles, tiles, tiles, comps)
    own, far, air_scores, ocean, far_ocean, sea_parts = pl.pallas_call(
        functools.partial(return_kernel, sizes),
        out_shape=[jax.ShapeDtypeStruct(shape, jnp.float32) for shape in out_shapes],
        in_specs=[anywhere] * 4 + [inside] * 5 + [scalar_spec()] * 2,
        out_specs=[anywhere] * len(out_shapes),
        scratch_shapes=[pltpu.VMEM(shape, jnp.float32) for shape in scratch]
        + [pltpu.SemaphoreType.DMA((n,)) for n in sems],
        compiler_params=pltpu.CompilerParams(
            collective_id=2, has_side_effects=True, vmem_limit_bytes=40 * 1024 * 1024
        ),
    )(back, air_point, state, ocean, low, high, donors, land_sea, my_weights, blend, rate)
    parents = lax.dynamic_slice_in_dim(ancestry, member * slots, slots)

    inside = parents % slots
    near = (parents // slots == member).astype(jnp.int32)

    def air_last(_):
        grid = resampled(
            air_last_kernel, inside, near, own, far, split_table(lon_basis), lon_count
        )
        return grid.reshape(member_state.shape), air_scores[:, 0, :1]

    def sea_last(_):
        score = jnp.sum(sea_parts[:, :, 0, :1], axis=0) / weight_total
        states = resampled(sea_last_kernel, inside, near, ocean, far_ocean, (), lon_count)
        return states.reshape(member_state.shape), score

    return lax.cond(is_air, air_last, sea_last, 0)


def by_bands(
    member_state,
    layer_blend_operator,
    coefficient,
    interpolation_donor_meridians,
    land_sea,
    ancestry,
):
    slot_count = member_state.shape[0]
    component = lax.axis_index("comp")
    tile_index = lax.axis_index("tile")
    tile_count = lax.axis_size("tile")
    row_count = member_state.shape[4]
    lon_count = member_state.shape[5]
    lon_table, number = kept_lon_basis(lon_count)
    lon_basis = jnp.asarray(lon_table)
    local_modes = lon_table.shape[0] // tile_count
    my_numbers = lax.dynamic_slice_in_dim(jnp.asarray(number), tile_index * local_modes, local_modes)
    lat_basis = jnp.asarray(lat_table())
    order = jnp.arange(MODES, dtype=jnp.int32).astype(jnp.float32)
    sea_cells = land_sea[None, None] == 1
    diffusivity = coefficient[0][:, None, None, None]
    weights = row_weights()
    my_weights = lax.dynamic_slice_in_dim(jnp.asarray(weights), tile_index * row_count, row_count)
    weight_total = float(weights.sum())
    stepped_list = []
    partial_list = []
    for slot in range(slot_count):
        field = member_state[slot, 0]
        for _ in range(STEPS):
            surface = field[0, 0]
            partner = partner_2(surface, "comp", 0)
            received = donor_lookup(partner, interpolation_donor_meridians[0])
            mixing = jnp.einsum("uv,fvjx->fujx", layer_blend_operator[0], field, precision=precise)
            forced = field + forcing_rate * jnp.tanh(mixing)
            forced = forced.at[0, 0].add(coupling_rate * (received - surface))
            spectral_gain = 1.0 / (
                1.0
                + coefficient[0][:, None, None]
                * (order[None, None, :] ** 2 + my_numbers[None, :, None] ** 2)
                / (MODES * MODES)
            )
            fourier = jnp.einsum("fvjx,qx->fvjq", forced, lon_basis, precision=precise)
            spectrum = jnp.einsum(
                "lj,fkjq->fkql",
                lat_basis,
                lax.all_to_all(fourier, "tile", split_axis=3, concat_axis=2, tiled=True),
                precision=precise,
            )
            spectrum = spectrum * spectral_gain[:, None]
            returned = jnp.einsum("lj,fkql->fkjq", lat_basis, spectrum, precision=precise)
            filtered = lax.all_to_all(returned, "tile", split_axis=2, concat_axis=3, tiled=True)
            block_atm = jnp.einsum("fvjq,qx->fvjx", filtered, lon_basis, precision=precise)
            padded = padded_2(field, (("tile", 2),), 1)
            laplacian = (
                padded[:, :, 2:]
                + padded[:, :, :-2]
                + jnp.roll(field, 1, axis=3)
                + jnp.roll(field, -1, axis=3)
                - 4.0 * field
            )
            new_ocn = jnp.where(sea_cells, forced + diffusivity * laplacian, field)
            field = jnp.where(component == 0, block_atm, new_ocn)
        stepped_list.append(field)
        partial_list.append(jnp.sum(jnp.mean(field[0, 0], axis=1) * my_weights))
    local_states = jnp.stack(stepped_list)
    region_sums = lax.psum(jnp.stack(partial_list), "tile")
    region_score = (region_sums / weight_total).reshape(slot_count, 1)
    member_index = lax.axis_index("member")
    my_parents = lax.dynamic_slice_in_dim(ancestry, member_index * slot_count, slot_count)
    gathered = lax.all_gather(local_states, "member", axis=0, tiled=True)
    chosen = jnp.take(gathered, my_parents, axis=0)
    return (chosen[:, None], region_score)


def local(member_state, *others):
    members, comps, tiles = (lax.axis_size(name) for name in ("member", "comp", "tile"))
    slots, _, fields, levels, rows, _ = member_state.shape
    fits = members == 2 and comps == 2 and slots == comps and tiles == members * fields
    if fits and levels % members == 0 and rows % 8 == 0:
        return by_units(member_state, *others)
    return by_bands(member_state, *others)


def solution(mesh):
    return jax.shard_map(
        local,
        mesh=mesh,
        in_specs=(
            P("member", "comp", None, None, "tile", None),
            P("comp", None, None),
            P("comp", None),
            P("comp", "tile", None),
            P("tile", None),
            P(),
        ),
        out_specs=(P("member", "comp", None, None, "tile", None), P("member", "comp")),
        check_vma=False,
    )
```

```python
import functools
import math

import jax
import jax.numpy as jnp
import numpy as np
from jax import lax
from jax.experimental import pallas as pl
from jax.experimental.pallas import tpu as pltpu
from jax.sharding import PartitionSpec as P

LAT = 384
MODES = 256
STEPS = 2
MESH = pl.DeviceIdType.MESH


coupling_rate = 0.5
forcing_rate = 0.5
precise = lax.Precision.HIGH


def partner_2(value, axis, distance):
    mask = 2**distance
    pairs = [(source, source ^ mask) for source in range(lax.axis_size(axis))]
    return lax.ppermute(value, axis, pairs)


def padded_2(block, sides, width):
    for axis, dim in sides:
        count = lax.axis_size(axis)
        forward = [(i, i + 1) for i in range(count - 1)]
        backward = [(target, source) for source, target in forward]
        low = lax.ppermute(
            lax.slice_in_dim(block, block.shape[dim] - width, None, axis=dim), axis, forward
        )
        high = lax.ppermute(lax.slice_in_dim(block, 0, width, axis=dim), axis, backward)
        block = jnp.concatenate([low, block, high], axis=dim)
    return block


def kept_lon_basis(lon_count):
    wave = np.arange(2 * MODES)
    is_cosine = wave < MODES
    number = np.where(is_cosine, wave, wave - MODES + 1).astype(np.float32)
    cells = np.arange(lon_count).astype(np.float32)
    angle = np.float32(2.0 * math.pi) * number[:, None] * cells[None, :] / np.float32(lon_count)
    scale = np.where(number == 0.0, math.sqrt(1.0 / lon_count), math.sqrt(2.0 / lon_count)).astype(
        np.float32
    )
    table = np.where(is_cosine[:, None], np.cos(angle), np.sin(angle)) * scale[:, None]
    return table.astype(np.float32), number


def lat_table():
    order = np.arange(MODES).astype(np.float32)
    cells = np.arange(LAT).astype(np.float32)
    scale = np.where(order == 0.0, math.sqrt(1.0 / LAT), math.sqrt(2.0 / LAT)).astype(np.float32)
    angle = np.float32(math.pi) * (cells[None, :] + np.float32(0.5)) * order[:, None]
    return (np.cos(angle / np.float32(LAT)) * scale[:, None]).astype(np.float32)


def row_weights():
    rows = np.arange(LAT).astype(np.float32)
    return np.cos(
        np.float32(math.pi) * ((rows + np.float32(0.5)) / np.float32(LAT) - np.float32(0.5))
    ).astype(np.float32)


def donor_lookup(partner, donors):
    lon_count = partner.shape[-1]
    cells = jnp.arange(lon_count, dtype=jnp.int32)[None, :]
    offsets = jnp.mod(donors - cells, lon_count)
    result = jnp.zeros_like(partner)
    for shift_by in (-1, 0, 1, 2, 3, 4):
        moved = jnp.roll(partner, -shift_by, axis=-1)
        result = result + jnp.where(offsets == shift_by % lon_count, moved, 0.0)
    return result


def remote(src, dst, send_sem, recv_sem, device):
    return pltpu.make_async_remote_copy(
        src_ref=src,
        dst_ref=dst,
        send_sem=send_sem,
        recv_sem=recv_sem,
        device_id=device,
        device_id_type=MESH,
    )


def here():
    return lax.axis_index("member"), lax.axis_index("comp"), lax.axis_index("tile")


def greet(targets, count):
    barrier = pltpu.get_barrier_semaphore()
    for condition, device in targets:

        @pl.when(condition)
        def _():
            pl.semaphore_signal(barrier, inc=1, device_id=device, device_id_type=MESH)

    @pl.when(count > 0)
    def _():
        pl.semaphore_wait(barrier, count)


def differs(a, b):
    return jnp.logical_or(a[0] != b[0], jnp.logical_or(a[1] != b[1], a[2] != b[2]))


def shores(y, t, tiles):
    return jnp.logical_and(y == 1, t > 0), jnp.logical_and(y == 1, t < tiles - 1)


def edge_copies(edge_ref, low_ref, high_ref, esend, erecv, m, y, t):
    up = remote(edge_ref.at[:, :, 0], high_ref, esend.at[0], erecv.at[0], (m, y, t - 1))
    down = remote(edge_ref.at[:, :, 1], low_ref, esend.at[1], erecv.at[1], (m, y, t + 1))
    return up, down


def first_kernel(
    sizes,
    field_ref,
    donors_ref,
    land_ref,
    blend_ref,
    rate_ref,
    blend_any,
    rate_any,
    table_high,
    table_low,
    u_ref,
    ru_ref,
    new_ref,
    low_out,
    high_out,
    oblend_ref,
    orate_ref,
    before,
    after,
    coefs,
    hops,
    forced,
    partner,
    odonors,
    looked,
    edge,
    low,
    high,
    load,
    psend,
    precv,
    esend,
    erecv,
    send,
    hsend,
    hrecv,
    rsend,
    recv,
    rrecv,
    loc,
    esend_2,
    erecv_2,
):
    members, comps, fields, tiles, rows = sizes
    me = m, y, t = here()
    slots, _, levels = before.shape[:3]
    per = levels // members
    unit_m, unit_f = t // fields, t % fields
    has_surface = jnp.logical_and(m == 0, unit_f == 0)
    across = (m, 1 - y, t)
    north, south = shores(y, t, tiles)
    targets = [(m >= 0, across), (north, (m, y, t - 1)), (south, (m, y, t + 1))]
    for j in range(tiles):
        source = (unit_m, y, j)
        targets.append((differs(source, me), source))
    for j in range(tiles):
        source = (unit_m, 1, j)
        targets.append((jnp.logical_and(has_surface, differs(source, me)), source))
    self_unit = (unit_m == m).astype(jnp.int32)
    self_surface = jnp.logical_and(has_surface, unit_m == m).astype(jnp.int32)
    count = 1 + members * fields - self_unit + jnp.where(y == 0, 0, comps - self_surface)
    loading = pltpu.make_async_copy(field_ref, before, load.at[0])
    loading.start()
    greet(targets, count + north.astype(jnp.int32) + south.astype(jnp.int32))

    pairs = [(field_ref.at[s, 0, 0], partner.at[s]) for s in range(slots)]
    pairs += [(donors_ref, odonors), (blend_any, oblend_ref), (rate_any, orate_ref)]
    copies = [remote(p, q, psend.at[k], precv.at[k], across) for k, (p, q) in enumerate(pairs)]
    up, down = edge_copies(edge.at[0], low, high, esend, erecv, m, y, t)
    up_2, down_2 = edge_copies(edge.at[1], low_out, high_out, esend_2, erecv_2, m, y, t)

    def rows_of(j):
        return pl.ds(pl.multiple_of(j * rows, 8), rows)

    def begin(parts):
        away, copy, local = parts
        pl.when(away)(copy.start)
        pl.when(jnp.logical_not(away))(local.start)

    def end(parts):
        away, copy, local = parts
        pl.when(away)(copy.wait_send)
        pl.when(jnp.logical_not(away))(local.wait)

    def piece(f, c, ref):
        device = (c, y, m * fields + f)
        src = ref.at[f, pl.ds(c * per, per)]
        dst = u_ref.at[:, rows_of(t), :]
        copy = remote(src, dst, send.at[f * members + c], recv.at[t], device)
        return differs(device, me), copy, pltpu.make_async_copy(src, dst, loc.at[0])

    def hop(f, c):
        part = (f, pl.ds(c * per, per))
        k = f * members + c
        return remote(coefs.at[(1,) + part], hops.at[part], hsend.at[k], hrecv.at[k], across)

    def surface(s):
        device = (0, s, m * fields)
        dst = ru_ref.at[rows_of(t), :]
        copy = remote(looked.at[s], dst, rsend.at[s], rrecv.at[t], device)
        return differs(device, me), copy, pltpu.make_async_copy(looked.at[s], dst, loc.at[1])

    def field_at(j):
        return jnp.where(j < fields - 1, 1 + lax.rem(j + t, fields - 1), 0)

    def mixed(s, f, u):
        total = blend_ref[u, 0] * before[s, f, 0]
        for v in range(1, levels):
            total = total + blend_ref[u, v] * before[s, f, v]
        return forcing_rate * jnp.tanh(total)

    def added(s):
        received = lookup(partner[s], donors_ref[...])
        return coupling_rate * (received - before[s, 0, 0])

    def partner_arrives():
        for copy in copies[:slots]:
            copy.wait_recv()

    for copy in copies:
        copy.start()
    loading.wait()
    keep = pltpu.make_async_copy(after, new_ref, load.at[1])

    @pl.when(y == 0)
    def _():
        def step(i, _):
            j = lax.div(i, slots)
            s, f = slots - 1 - lax.rem(i, slots), field_at(j)
            for u in range(levels):
                forced[u * rows : (u + 1) * rows] = before[s, f, u] + mixed(s, f, u)

            pl.when(i == slots * (fields - 1))(partner_arrives)

            @pl.when(j == fields - 1)
            def _():
                forced[:rows] += added(s)

            result = dot3(forced[...], table_high, table_low)
            coefs[s, f] = result.reshape(levels, rows, coefs.shape[-1])

            @pl.when(s == 1)
            def _():
                for c in range(members):
                    hop(f, c).start()

            @pl.when(s == 0)
            def _():
                for c in range(members):
                    begin(piece(f, c, coefs.at[0]))

            return 0

        lax.fori_loop(0, slots * fields, step, 0)

    @pl.when(y == 1)
    def _():
        pl.when(t == 0)(lambda: zero(low))
        pl.when(t == tiles - 1)(lambda: zero(high))

        def gather(i, _):
            s, f = lax.div(i, fields), lax.rem(i, fields)
            for u in range(levels):
                edge[0, s, f, 0, u : u + 1] = before[s, f, u, :1]
                edge[0, s, f, 1, u : u + 1] = before[s, f, u, rows - 1 :]
            return 0

        lax.fori_loop(0, slots * fields, gather, 0)
        pl.when(north)(up.start)
        pl.when(south)(down.start)
        pl.when(south)(up.wait_recv)
        pl.when(north)(down.wait_recv)
        sea = land_ref[...] == 1

        def step(j, _):
            f = field_at(j)

            pl.when(j == fields - 1)(partner_arrives)

            def one(s, _):
                for u in range(levels):
                    value = before[s, f, u]
                    total = value + mixed(s, f, u)
                    ends = (low[s, f, u : u + 1], high[s, f, u : u + 1])
                    total = total + rate_ref[0, f] * laplacian_of(value, *ends)
                    after[s, f, u] = jnp.where(sea, total, value)

                @pl.when(j == fields - 1)
                def _():
                    after[s, 0, 0] = after[s, 0, 0] + jnp.where(sea, added(s), 0.0)

                for u in range(levels):
                    edge[1, s, f, 0, u : u + 1] = after[s, f, u, :1]
                    edge[1, s, f, 1, u : u + 1] = after[s, f, u, rows - 1 :]
                return 0

            lax.fori_loop(0, slots, one, 0)

            @pl.when(j == fields - 1)
            def _():
                copies[slots].wait_recv()
                for s in range(slots):
                    looked[s] = lookup(after[s, 0, 0], odonors[...])
                    begin(surface(s))
                pl.when(north)(up_2.start)
                pl.when(south)(down_2.start)
                keep.start()

            for c in range(members):
                hop(f, c).wait_recv()
                begin(piece(f, c, hops))
            return 0

        lax.fori_loop(0, fields, step, 0)

    for j in range(tiles):
        away = differs((unit_m, y, j), me)
        part = u_ref.at[:, rows_of(j), :]
        arrival = remote(part, part, send.at[0], recv.at[j], me)
        pl.when(away)(arrival.wait_recv)
        late = remote(
            ru_ref.at[rows_of(j), :], ru_ref.at[rows_of(j), :], rsend.at[0], rrecv.at[j], me
        )
        away = jnp.logical_and(has_surface, differs((unit_m, 1, j), me))
        pl.when(away)(late.wait_recv)

    @pl.when(y == 0)
    def _():
        copies[slots].wait_recv()
        for f in range(fields):
            for c in range(members):
                hop(f, c).wait_send()
                end(piece(f, c, coefs.at[0]))

    @pl.when(y == 1)
    def _():
        for s in range(comps):
            end(surface(s))
        for f in range(fields):
            for c in range(members):
                end(piece(f, c, hops))
        keep.wait()

    for copy in copies:
        copy.wait_send()
    for copy in copies[slots + 1 :]:
        copy.wait_recv()
    for first, last in ((up, down), (up_2, down_2)):
        pl.when(north)(first.wait_send)
        pl.when(south)(last.wait_send)
    pl.when(south)(up_2.wait_recv)
    pl.when(north)(down_2.wait_recv)


def zero(ref):
    ref[...] = jnp.zeros(ref.shape, ref.dtype)


def swap_kernel(sizes, x_ref, xo_ref, send, recv):
    m, y, t = here()
    other = (1 - m, y, t)
    greet([(m >= 0, other)], 1)
    across = remote(x_ref, xo_ref, send.at[0], recv.at[0], other)
    across.start()
    across.wait()


def return_kernel(
    sizes,
    f_ref,
    p_ref,
    x_ref,
    o_ref,
    low_ref,
    high_ref,
    donors_ref,
    land_ref,
    weight_ref,
    blend_ref,
    rate_ref,
    own_ref,
    far_ref,
    score_ref,
    new_ref,
    faro_ref,
    part_ref,
    before,
    after,
    flux,
    sums,
    send,
    recv,
    fsend,
    frecv,
    psend,
    precv,
    loc,
    osend,
    orecv,
    keep,
    qsend,
    qrecv,
    ssend,
    srecv,
):
    members, comps, fields, tiles, rows = sizes
    me = m, y, t = here()
    per = f_ref.shape[0]
    unit_m, unit_f = t // fields, t % fields
    has_surface = jnp.logical_and(m == 0, unit_f == 0)
    other = (1 - m, y, t)
    pieces = [(s, f, c) for s in range(comps) for f in range(fields) for c in range(members)]
    targets = [(m >= 0, other)]
    for j in range(tiles):
        targets.append((jnp.logical_and(y == 1, j != t), (m, y, j)))
    for s in range(comps):
        source = (0, s, m * fields)
        targets.append((jnp.logical_and(y == 1, differs(source, me)), source))
    for s, f, c in pieces:
        source = (c, s, m * fields + f)
        targets.append((jnp.logical_and(y == 0, differs(source, me)), source))
    own_unit = jnp.logical_and(y == 0, unit_m == m).astype(jnp.int32)
    own_surface = jnp.logical_and(has_surface, jnp.logical_and(y == 1, unit_m == m))
    count = tiles - own_unit + jnp.where(y == 0, 1, tiles)
    greet(targets, count + jnp.where(has_surface, tiles - own_surface.astype(jnp.int32), 0))
    load = pltpu.make_async_copy(o_ref, before, loc.at[2])
    pl.when(y == 1)(load.start)

    def share(j):
        return remote(sums, part_ref.at[t], qsend.at[j], qrecv.at[t], (m, y, j))

    def surface(j):
        device = (unit_m, 1, j)
        part = x_ref.at[0, pl.ds(j * rows, rows), :]
        copy = remote(part, flux.at[y], ssend.at[j], srecv.at[y], device)
        return differs(device, me), copy, pltpu.make_async_copy(part, flux.at[y], loc.at[3])

    @pl.when(has_surface)
    def _():
        for j in range(tiles):
            away, copy, local = surface(j)
            pl.when(away)(copy.start)
            pl.when(jnp.logical_not(away))(local.start)

    def band(j):
        device = (unit_m, 0, j)
        src = f_ref.at[:, pl.ds(j * rows, rows), :]
        dst = own_ref.at[y, unit_f, pl.ds(m * per, per)]
        slot = (y * fields + unit_f) * members + m
        return (
            device,
            remote(src, dst, send.at[j], recv.at[slot], device),
            pltpu.make_async_copy(src, dst, loc.at[0]),
            remote(p_ref, score_ref.at[y], psend.at[j], precv.at[y], device),
            pltpu.make_async_copy(p_ref, score_ref.at[y], loc.at[1]),
        )

    for j in range(tiles):
        device, copy, local, point, local_point = band(j)
        away = differs(device, me)
        pl.when(away)(copy.start)
        pl.when(jnp.logical_not(away))(local.start)
        pl.when(jnp.logical_and(has_surface, away))(point.start)
        pl.when(jnp.logical_and(has_surface, jnp.logical_not(away)))(local_point.start)

    def forward(k):
        s, f, c = pieces[k]
        part = (s, f, pl.ds(c * per, per))
        return remote(own_ref.at[part], far_ref.at[part], fsend.at[k], frecv.at[k], other)

    @pl.when(y == 0)
    def _():
        for k, (s, f, c) in enumerate(pieces):
            part = own_ref.at[s, f, pl.ds(c * per, per)]
            away = differs((c, s, m * fields + f), me)
            arrival = remote(part, part, send.at[0], recv.at[k], me)
            pl.when(away)(arrival.wait_recv)
            own = pltpu.make_async_copy(part, part, loc.at[0])
            pl.when(jnp.logical_not(away))(own.wait)
            forward(k).start()
        for s in range(comps):
            away = differs((0, s, m * fields), me)
            arrival = remote(score_ref.at[s], score_ref.at[s], psend.at[0], precv.at[s], me)
            pl.when(away)(arrival.wait_recv)
            own = pltpu.make_async_copy(p_ref, score_ref.at[s], loc.at[1])
            pl.when(jnp.logical_not(away))(own.wait)
        for k in range(len(pieces)):
            forward(k).wait()

    for j in range(tiles):
        device, copy, local, point, local_point = band(j)
        away = differs(device, me)
        pl.when(away)(copy.wait_send)
        pl.when(jnp.logical_and(has_surface, away))(point.wait_send)

    def clone(s, f):
        i = s * fields + f
        part = (s, f)
        return (
            remote(after.at[part], faro_ref.at[part], osend.at[i], orecv.at[i], other),
            pltpu.make_async_copy(after.at[part], new_ref.at[part], keep.at[i]),
        )

    @pl.when(y == 1)
    def _():
        load.wait()
        for s in range(comps):
            away = differs((0, s, m * fields), me)
            arrival = remote(flux.at[s], flux.at[s], ssend.at[0], srecv.at[s], me)
            pl.when(away)(arrival.wait_recv)
            own = pltpu.make_async_copy(x_ref.at[0, pl.ds(0, rows), :], flux.at[s], loc.at[3])
            pl.when(jnp.logical_not(away))(own.wait)
        sea = land_ref[...] == 1

        def step(i, _):
            s, f = lax.div(i, fields), lax.rem(i, fields)
            levels = before.shape[2]
            for u in range(levels):
                mixing = blend_ref[u, 0] * before[s, f, 0]
                for v in range(1, levels):
                    mixing = mixing + blend_ref[u, v] * before[s, f, v]
                value = before[s, f, u]
                forced = value + forcing_rate * jnp.tanh(mixing)
                ends = (
                    jnp.where(t == 0, 0.0, low_ref[s, f, u : u + 1]),
                    jnp.where(t == tiles - 1, 0.0, high_ref[s, f, u : u + 1]),
                )
                forced = forced + rate_ref[f] * laplacian_of(value, *ends)
                after[s, f, u] = jnp.where(sea, forced, value)

            @pl.when(f == 0)
            def _():
                value = before[s, 0, 0]
                extra = coupling_rate * (lookup(flux[s], donors_ref[...]) - value)
                result = after[s, 0, 0] + jnp.where(sea, extra, 0.0)
                after[s, 0, 0] = result
                sums[s] = weighted_sum(result, weight_ref[...], sums.shape[1:])

            across, own = clone(s, f)
            across.start()
            own.start()
            return 0

        lax.fori_loop(0, comps * fields, step, 0)
        mine = pltpu.make_async_copy(sums, part_ref.at[t], loc.at[4])
        mine.start()
        for j in range(tiles):
            pl.when(j != t)(share(j).start)
        mine.wait()
        for j in range(tiles):
            arrival = remote(part_ref.at[j], part_ref.at[j], qsend.at[0], qrecv.at[j], me)
            pl.when(j != t)(arrival.wait_recv)
            pl.when(j != t)(share(j).wait_send)
        for s in range(comps):
            for f in range(fields):
                across, own = clone(s, f)
                across.wait()
                own.wait()

    @pl.when(has_surface)
    def _():
        for j in range(tiles):
            away, copy, local = surface(j)
            pl.when(away)(copy.wait_send)


def laplacian_of(value, low, high):
    rows, lon_count = value.shape
    row = lax.broadcasted_iota(jnp.int32, (rows, lon_count), 0)
    north = jnp.where(row == 0, low, pltpu.roll(value, 1, 0))
    south = jnp.where(row == rows - 1, high, pltpu.roll(value, rows - 1, 0))
    east, west = pltpu.roll(value, 1, 1), pltpu.roll(value, lon_count - 1, 1)
    return south + north + east + west - 4.0 * value


def weighted_sum(value, weights, shape):
    total = jnp.sum(value * weights, axis=0, keepdims=True)
    total = jnp.sum(total, axis=1, keepdims=True) / value.shape[1]
    return jnp.broadcast_to(total, shape)


def call(kernel, collective_id, outs, sems, *args):
    return pl.pallas_call(
        kernel,
        out_shape=[
            jax.ShapeDtypeStruct(out.shape, out.dtype)
            if hasattr(out, "dtype")
            else jax.ShapeDtypeStruct(out, jnp.float32)
            for out in outs
        ],
        in_specs=[pl.BlockSpec(memory_space=pl.ANY)] * len(args),
        out_specs=[pl.BlockSpec(memory_space=pl.ANY)] * len(outs),
        scratch_shapes=[pltpu.SemaphoreType.DMA((n,)) for n in sems],
        compiler_params=pltpu.CompilerParams(collective_id=collective_id, has_side_effects=True),
    )(*args)


def matmul(a, b):
    return jnp.dot(a, b, precision=precise, preferred_element_type=jnp.float32)


def split(value):
    high = value.astype(jnp.bfloat16)
    return high, (value - high.astype(jnp.float32)).astype(jnp.bfloat16)


def split_table(table):
    high = table.astype(jnp.bfloat16)
    low = (table - high.astype(np.float32)).astype(jnp.bfloat16)
    return jnp.asarray(high), jnp.asarray(low)


def dot3(value, high_ref, low_ref):
    high, low = split(value)
    total = jnp.dot(high, low_ref[...], preferred_element_type=jnp.float32)
    total = total + jnp.dot(low, high_ref[...], preferred_element_type=jnp.float32)
    return total + jnp.dot(high, high_ref[...], preferred_element_type=jnp.float32)


def lookup(surface, donors):
    lon_count = surface.shape[-1]
    offset = donors - lax.broadcasted_iota(jnp.int32, donors.shape, 1)
    offset = jnp.where(offset > lon_count // 2, offset - lon_count, offset)
    offset = jnp.where(offset < -(lon_count // 2), offset + lon_count, offset)
    result = surface
    for shift in (-1, 1, 2, 3, 4):
        moved = pltpu.roll(surface, (-shift) % lon_count, 1)
        result = jnp.where(offset == shift, moved, result)
    return result


def whole_spec(array):
    zeros = (0,) * array.ndim
    return pl.BlockSpec(array.shape, lambda *_: zeros)


def scalar_spec():
    return pl.BlockSpec(memory_space=pltpu.SMEM)


def state_spec(shape):
    zeros = (0,) * (len(shape) - 2)
    return pl.BlockSpec((1, 1) + tuple(shape[2:]), lambda s, f, *_: (s, f) + zeros)


large = pltpu.CompilerParams(vmem_limit_bytes=40 * 1024 * 1024)


def air_last_kernel(inside_ref, near_ref, own_ref, far_ref, high_ref, low_ref, out_ref):
    near = near_ref[pl.program_id(0)] == 1
    levels, rows, waves = own_ref.shape[2:]
    coefs = jnp.where(near, own_ref[0, 0], far_ref[0, 0]).reshape(levels * rows, waves)
    out_ref[0, 0] = dot3(coefs, high_ref, low_ref).reshape(out_ref.shape[2:])


def sea_last_kernel(inside_ref, near_ref, own_ref, far_ref, out_ref):
    near = near_ref[pl.program_id(0)] == 1
    out_ref[0, 0] = jnp.where(near, own_ref[0, 0], far_ref[0, 0])


def resampled(kernel, inside, near, own, far, tables, lon_count):
    shape = own.shape[:-1] + (lon_count,)

    def parent(s, f, inside_ref, near_ref):
        return (inside_ref[s], f, 0, 0, 0)

    parent_spec = pl.BlockSpec((1, 1) + own.shape[2:], parent)
    return pl.pallas_call(
        kernel,
        grid_spec=pltpu.PrefetchScalarGridSpec(
            num_scalar_prefetch=2,
            grid=own.shape[:2],
            in_specs=[parent_spec, parent_spec] + [whole_spec(table) for table in tables],
            out_specs=state_spec(shape),
        ),
        out_shape=jax.ShapeDtypeStruct(shape, jnp.float32),
        compiler_params=large,
    )(inside, near, own, far, *tables)


def left3(high_ref, low_ref, value):
    high, low = split(value)
    total = jnp.dot(low_ref[...], high, preferred_element_type=jnp.float32)
    total = total + jnp.dot(high_ref[...], low, preferred_element_type=jnp.float32)
    return total + jnp.dot(high_ref[...], high, preferred_element_type=jnp.float32)


def filtered(value, squares_ref, rate_ref, forward, inverse):
    spectrum = left3(*forward, value) / (1.0 + rate_ref[0] * squares_ref[...])
    return left3(*inverse, spectrum)


def to_grid_kernel(x_ref, sq_ref, rate_ref, fh, fl, ih, il, gh, gl, out_ref):
    coefs = filtered(x_ref[0], sq_ref, rate_ref, (fh, fl), (ih, il))
    out_ref[0] = dot3(coefs, gh, gl)


def to_coefs_kernel(
    x_ref,
    o_ref,
    sst_ref,
    here_ref,
    there_ref,
    flag_ref,
    w_ref,
    sq_ref,
    rate_ref,
    fh,
    fl,
    ih,
    il,
    gh,
    gl,
    out_ref,
    sum_ref,
    forced,
):
    per = x_ref.shape[0]
    u = pl.program_id(0)
    mixing = here_ref[u, 0] * x_ref[0] + there_ref[u, 0] * o_ref[0]
    for v in range(1, per):
        mixing = mixing + here_ref[u, v] * x_ref[v] + there_ref[u, v] * o_ref[v]
    forced[...] = x_ref[u] + forcing_rate * jnp.tanh(mixing)

    @pl.when(jnp.logical_and(u == 0, flag_ref[0] == 1))
    def _():
        forced[...] += coupling_rate * (sst_ref[...] - x_ref[0])

    coefs = dot3(forced[...], gh, gl)
    result = filtered(coefs, sq_ref, rate_ref, (fh, fl), (ih, il))
    out_ref[0] = result

    @pl.when(u == 0)
    def _():
        total = jnp.sum(result[:, : w_ref.shape[1]] * w_ref[...], axis=0, keepdims=True)
        total = jnp.sum(total, axis=1, keepdims=True)
        sum_ref[...] = jnp.broadcast_to(total, sum_ref.shape)


def level_spec(shape):
    return pl.BlockSpec((1,) + tuple(shape[1:]), lambda u: (u, 0, 0))


def to_grid(value, squares, rate, tables, lon_count):
    shape = value.shape[:2] + (lon_count,)
    return pl.pallas_call(
        to_grid_kernel,
        grid=value.shape[:1],
        out_shape=jax.ShapeDtypeStruct(shape, jnp.float32),
        in_specs=[level_spec(value.shape), whole_spec(squares), scalar_spec()]
        + [whole_spec(table) for table in tables],
        out_specs=level_spec(shape),
        compiler_params=large,
    )(value, squares, rate, *tables)


def to_coefs(state, other, sst, mine, theirs, flag, weights, squares, rate, tables):
    shape = state.shape[:2] + (squares.shape[1],)
    return pl.pallas_call(
        to_coefs_kernel,
        grid=state.shape[:1],
        out_shape=[
            jax.ShapeDtypeStruct(shape, jnp.float32),
            jax.ShapeDtypeStruct((8, 128), jnp.float32),
        ],
        in_specs=[whole_spec(state), whole_spec(other), whole_spec(sst)]
        + [scalar_spec()] * 3
        + [whole_spec(weights), whole_spec(squares), scalar_spec()]
        + [whole_spec(table) for table in tables],
        out_specs=[level_spec(shape), pl.BlockSpec((8, 128), lambda u: (0, 0))],
        scratch_shapes=[pltpu.VMEM(state.shape[1:], jnp.float32)],
        compiler_params=large,
    )(state, other, sst, mine, theirs, flag, weights, squares, rate, *tables)


def by_units(
    member_state,
    layer_blend_operator,
    coefficient,
    interpolation_donor_meridians,
    land_sea,
    ancestry,
):
    member, component, tile = here()
    members, comps, tiles = (lax.axis_size(name) for name in ("member", "comp", "tile"))
    field = member_state[:, 0]
    slots, fields, levels, rows, lon_count = field.shape
    per = levels // members
    sizes = (members, comps, fields, tiles, rows)
    lon_basis, number = kept_lon_basis(lon_count)
    waves = lon_basis.shape[0]
    lon_columns = np.ascontiguousarray(lon_basis.T)
    lat_basis = lat_table()
    lat_tables = split_table(lat_basis) + split_table(np.ascontiguousarray(lat_basis.T))
    weights = row_weights()
    weight_total = float(weights.sum())
    order = np.arange(MODES).astype(np.float32)
    squares = order[:, None] ** 2 + number[None, :] ** 2
    squares = jnp.asarray((squares / np.float32(MODES * MODES)).astype(np.float32))
    air_weights = np.zeros((LAT, 128), np.float32)
    air_weights[:, 0] = weights * lon_basis[0, 0] / weight_total
    my_weights = lax.dynamic_slice_in_dim(jnp.asarray(weights[:, None]), tile * rows, rows)

    is_air = component == 0
    blend = layer_blend_operator[0]
    rate = coefficient[0]
    donors = interpolation_donor_meridians[0]
    anywhere = pl.BlockSpec(memory_space=pl.ANY)
    inside = pl.BlockSpec(memory_space=pltpu.VMEM)
    halo = (slots, fields, levels, lon_count)
    surface = (slots, rows, lon_count)
    coefs_shape = (slots, fields, levels, rows, waves)
    out_shapes = [(per, LAT, waves), (LAT, lon_count), field.shape, halo, halo]
    out_shapes += [blend.shape, coefficient.shape]
    scratch = [field.shape, field.shape, coefs_shape, coefs_shape[1:]]
    scratch += [(levels * rows, lon_count), surface]
    later = [surface, (2, slots, fields, 2, levels, lon_count), halo, halo]
    pieces = members * fields
    sems = (2, slots + 3, slots + 3, 2, 2, pieces, pieces, pieces, comps, tiles, tiles, 2, 2, 2)
    gathered, sst, ocean, low, high, other_blend, other_rate = pl.pallas_call(
        functools.partial(first_kernel, sizes),
        out_shape=[jax.ShapeDtypeStruct(shape, jnp.float32) for shape in out_shapes],
        in_specs=[anywhere, inside, inside]
        + [scalar_spec()] * 2
        + [anywhere] * 2
        + [inside] * 2,
        out_specs=[anywhere] * len(out_shapes),
        scratch_shapes=[pltpu.VMEM(shape, jnp.float32) for shape in scratch]
        + [pltpu.VMEM(donors.shape, jnp.int32)]
        + [pltpu.VMEM(shape, jnp.float32) for shape in later]
        + [pltpu.SemaphoreType.DMA((n,)) for n in sems],
        compiler_params=pltpu.CompilerParams(
            collective_id=0, has_side_effects=True, vmem_limit_bytes=48 * 1024 * 1024
        ),
    )(
        field,
        donors,
        land_sea,
        blend,
        coefficient,
        blend,
        coefficient,
        *split_table(lon_columns),
    )
    air_blend = jnp.where(is_air, blend, other_blend)
    air_rate = jnp.where(is_air, rate, other_rate[0])
    unit_field = tile % fields
    unit_rate = lax.dynamic_slice_in_dim(air_rate, unit_field, 1)
    state = to_grid(
        gathered, squares, unit_rate, lat_tables + split_table(lon_basis), lon_count
    )
    (other_state,) = call(
        functools.partial(swap_kernel, sizes), 1, [(per, LAT, lon_count)], (1, 1), state
    )
    mine = lax.dynamic_slice_in_dim(air_blend, member * per, per)
    mine_own = lax.dynamic_slice_in_dim(mine, member * per, per, axis=1)
    mine_other = lax.dynamic_slice_in_dim(mine, (1 - member) * per, per, axis=1)
    flag = jnp.logical_and(member == 0, unit_field == 0).astype(jnp.int32).reshape(1)
    back, air_point = to_coefs(
        state,
        other_state,
        sst,
        mine_own,
        mine_other,
        flag,
        jnp.asarray(air_weights),
        squares,
        unit_rate,
        lat_tables + split_table(lon_columns),
    )

    count = slots * fields * members
    out_shapes = [coefs_shape, coefs_shape, (slots, 8, 128)]
    out_shapes += [field.shape, field.shape, (tiles, slots, 8, 128)]
    scratch = [field.shape, field.shape, (slots, rows, lon_count), (slots, 8, 128)]
    sems = (tiles, count, count, count, tiles, comps, 5)
    sems += (slots * fields,) * 3 + (tiles, tiles, tiles, comps)
    own, far, air_scores, ocean, far_ocean, sea_parts = pl.pallas_call(
        functools.partial(return_kernel, sizes),
        out_shape=[jax.ShapeDtypeStruct(shape, jnp.float32) for shape in out_shapes],
        in_specs=[anywhere] * 4 + [inside] * 5 + [scalar_spec()] * 2,
        out_specs=[anywhere] * len(out_shapes),
        scratch_shapes=[pltpu.VMEM(shape, jnp.float32) for shape in scratch]
        + [pltpu.SemaphoreType.DMA((n,)) for n in sems],
        compiler_params=pltpu.CompilerParams(
            collective_id=2, has_side_effects=True, vmem_limit_bytes=40 * 1024 * 1024
        ),
    )(back, air_point, state, ocean, low, high, donors, land_sea, my_weights, blend, rate)
    parents = lax.dynamic_slice_in_dim(ancestry, member * slots, slots)

    inside = parents % slots
    near = (parents // slots == member).astype(jnp.int32)

    def air_last(_):
        grid = resampled(
            air_last_kernel, inside, near, own, far, split_table(lon_basis), lon_count
        )
        return grid.reshape(member_state.shape), air_scores[:, 0, :1]

    def sea_last(_):
        score = jnp.sum(sea_parts[:, :, 0, :1], axis=0) / weight_total
        states = resampled(sea_last_kernel, inside, near, ocean, far_ocean, (), lon_count)
        return states.reshape(member_state.shape), score

    return lax.cond(is_air, air_last, sea_last, 0)


def by_bands(
    member_state,
    layer_blend_operator,
    coefficient,
    interpolation_donor_meridians,
    land_sea,
    ancestry,
):
    slot_count = member_state.shape[0]
    component = lax.axis_index("comp")
    tile_index = lax.axis_index("tile")
    tile_count = lax.axis_size("tile")
    row_count = member_state.shape[4]
    lon_count = member_state.shape[5]
    lon_table, number = kept_lon_basis(lon_count)
    lon_basis = jnp.asarray(lon_table)
    local_modes = lon_table.shape[0] // tile_count
    my_numbers = lax.dynamic_slice_in_dim(jnp.asarray(number), tile_index * local_modes, local_modes)
    lat_basis = jnp.asarray(lat_table())
    order = jnp.arange(MODES, dtype=jnp.int32).astype(jnp.float32)
    sea_cells = land_sea[None, None] == 1
    diffusivity = coefficient[0][:, None, None, None]
    weights = row_weights()
    my_weights = lax.dynamic_slice_in_dim(jnp.asarray(weights), tile_index * row_count, row_count)
    weight_total = float(weights.sum())
    stepped_list = []
    partial_list = []
    for slot in range(slot_count):
        field = member_state[slot, 0]
        for _ in range(STEPS):
            surface = field[0, 0]
            partner = partner_2(surface, "comp", 0)
            received = donor_lookup(partner, interpolation_donor_meridians[0])
            mixing = jnp.einsum("uv,fvjx->fujx", layer_blend_operator[0], field, precision=precise)
            forced = field + forcing_rate * jnp.tanh(mixing)
            forced = forced.at[0, 0].add(coupling_rate * (received - surface))
            spectral_gain = 1.0 / (
                1.0
                + coefficient[0][:, None, None]
                * (order[None, None, :] ** 2 + my_numbers[None, :, None] ** 2)
                / (MODES * MODES)
            )
            fourier = jnp.einsum("fvjx,qx->fvjq", forced, lon_basis, precision=precise)
            spectrum = jnp.einsum(
                "lj,fkjq->fkql",
                lat_basis,
                lax.all_to_all(fourier, "tile", split_axis=3, concat_axis=2, tiled=True),
                precision=precise,
            )
            spectrum = spectrum * spectral_gain[:, None]
            returned = jnp.einsum("lj,fkql->fkjq", lat_basis, spectrum, precision=precise)
            filtered = lax.all_to_all(returned, "tile", split_axis=2, concat_axis=3, tiled=True)
            block_atm = jnp.einsum("fvjq,qx->fvjx", filtered, lon_basis, precision=precise)
            padded = padded_2(field, (("tile", 2),), 1)
            laplacian = (
                padded[:, :, 2:]
                + padded[:, :, :-2]
                + jnp.roll(field, 1, axis=3)
                + jnp.roll(field, -1, axis=3)
                - 4.0 * field
            )
            new_ocn = jnp.where(sea_cells, forced + diffusivity * laplacian, field)
            field = jnp.where(component == 0, block_atm, new_ocn)
        stepped_list.append(field)
        partial_list.append(jnp.sum(jnp.mean(field[0, 0], axis=1) * my_weights))
    local_states = jnp.stack(stepped_list)
    region_sums = lax.psum(jnp.stack(partial_list), "tile")
    region_score = (region_sums / weight_total).reshape(slot_count, 1)
    member_index = lax.axis_index("member")
    my_parents = lax.dynamic_slice_in_dim(ancestry, member_index * slot_count, slot_count)
    gathered = lax.all_gather(local_states, "member", axis=0, tiled=True)
    chosen = jnp.take(gathered, my_parents, axis=0)
    return (chosen[:, None], region_score)


def local(member_state, *others):
    members, comps, tiles = (lax.axis_size(name) for name in ("member", "comp", "tile"))
    slots, _, fields, levels, rows, _ = member_state.shape
    fits = members == 2 and comps == 2 and slots == comps and tiles == members * fields
    if fits and levels % members == 0 and rows % 8 == 0:
        return by_units(member_state, *others)
    return by_bands(member_state, *others)


def solution(mesh):
    return jax.shard_map(
        local,
        mesh=mesh,
        in_specs=(
            P("member", "comp", None, None, "tile", None),
            P("comp", None, None),
            P("comp", None),
            P("comp", "tile", None),
            P("tile", None),
            P(),
        ),
        out_specs=(P("member", "comp", None, None, "tile", None), P("member", "comp")),
        check_vma=False,
    )
```

```python
import functools
import math

import jax
import jax.numpy as jnp
import numpy as np
from jax import lax
from jax.experimental import pallas as pl
from jax.experimental.pallas import tpu as pltpu
from jax.sharding import PartitionSpec as P

LAT = 384
MODES = 256
STEPS = 2
MESH = pl.DeviceIdType.MESH


coupling_rate = 0.5
forcing_rate = 0.5
precise = lax.Precision.HIGH


def partner_2(value, axis, distance):
    mask = 2**distance
    pairs = [(source, source ^ mask) for source in range(lax.axis_size(axis))]
    return lax.ppermute(value, axis, pairs)


def padded_2(block, sides, width):
    for axis, dim in sides:
        count = lax.axis_size(axis)
        forward = [(i, i + 1) for i in range(count - 1)]
        backward = [(target, source) for source, target in forward]
        low = lax.ppermute(
            lax.slice_in_dim(block, block.shape[dim] - width, None, axis=dim), axis, forward
        )
        high = lax.ppermute(lax.slice_in_dim(block, 0, width, axis=dim), axis, backward)
        block = jnp.concatenate([low, block, high], axis=dim)
    return block


def kept_lon_basis(lon_count):
    wave = np.arange(2 * MODES)
    is_cosine = wave < MODES
    number = np.where(is_cosine, wave, wave - MODES + 1).astype(np.float32)
    cells = np.arange(lon_count).astype(np.float32)
    angle = np.float32(2.0 * math.pi) * number[:, None] * cells[None, :] / np.float32(lon_count)
    scale = np.where(number == 0.0, math.sqrt(1.0 / lon_count), math.sqrt(2.0 / lon_count)).astype(
        np.float32
    )
    table = np.where(is_cosine[:, None], np.cos(angle), np.sin(angle)) * scale[:, None]
    return table.astype(np.float32), number


def lat_table():
    order = np.arange(MODES).astype(np.float32)
    cells = np.arange(LAT).astype(np.float32)
    scale = np.where(order == 0.0, math.sqrt(1.0 / LAT), math.sqrt(2.0 / LAT)).astype(np.float32)
    angle = np.float32(math.pi) * (cells[None, :] + np.float32(0.5)) * order[:, None]
    return (np.cos(angle / np.float32(LAT)) * scale[:, None]).astype(np.float32)


def row_weights():
    rows = np.arange(LAT).astype(np.float32)
    return np.cos(
        np.float32(math.pi) * ((rows + np.float32(0.5)) / np.float32(LAT) - np.float32(0.5))
    ).astype(np.float32)


def donor_lookup(partner, donors):
    lon_count = partner.shape[-1]
    cells = jnp.arange(lon_count, dtype=jnp.int32)[None, :]
    offsets = jnp.mod(donors - cells, lon_count)
    result = jnp.zeros_like(partner)
    for shift_by in (-1, 0, 1, 2, 3, 4):
        moved = jnp.roll(partner, -shift_by, axis=-1)
        result = result + jnp.where(offsets == shift_by % lon_count, moved, 0.0)
    return result


def remote(src, dst, send_sem, recv_sem, device):
    return pltpu.make_async_remote_copy(
        src_ref=src,
        dst_ref=dst,
        send_sem=send_sem,
        recv_sem=recv_sem,
        device_id=device,
        device_id_type=MESH,
    )


def here():
    return lax.axis_index("member"), lax.axis_index("comp"), lax.axis_index("tile")


def greet(targets, count):
    barrier = pltpu.get_barrier_semaphore()
    for condition, device in targets:

        @pl.when(condition)
        def _():
            pl.semaphore_signal(barrier, inc=1, device_id=device, device_id_type=MESH)

    @pl.when(count > 0)
    def _():
        pl.semaphore_wait(barrier, count)


def differs(a, b):
    return jnp.logical_or(a[0] != b[0], jnp.logical_or(a[1] != b[1], a[2] != b[2]))


def shores(y, t, tiles):
    return jnp.logical_and(y == 1, t > 0), jnp.logical_and(y == 1, t < tiles - 1)


def edge_copies(edge_ref, low_ref, high_ref, esend, erecv, m, y, t):
    up = remote(edge_ref.at[:, :, 0], high_ref, esend.at[0], erecv.at[0], (m, y, t - 1))
    down = remote(edge_ref.at[:, :, 1], low_ref, esend.at[1], erecv.at[1], (m, y, t + 1))
    return up, down


def first_kernel(
    sizes,
    field_ref,
    donors_ref,
    land_ref,
    blend_ref,
    rate_ref,
    blend_any,
    rate_any,
    table_high,
    table_low,
    u_ref,
    ru_ref,
    new_ref,
    low_out,
    high_out,
    oblend_ref,
    orate_ref,
    before,
    after,
    coefs,
    hops,
    forced,
    partner,
    odonors,
    looked,
    edge,
    low,
    high,
    load,
    psend,
    precv,
    esend,
    erecv,
    send,
    hsend,
    hrecv,
    rsend,
    recv,
    rrecv,
    loc,
    esend_2,
    erecv_2,
):
    members, comps, fields, tiles, rows = sizes
    me = m, y, t = here()
    slots, _, levels = before.shape[:3]
    per = levels // members
    unit_m, unit_f = t // fields, t % fields
    has_surface = jnp.logical_and(m == 0, unit_f == 0)
    across = (m, 1 - y, t)
    north, south = shores(y, t, tiles)
    targets = [(m >= 0, across), (north, (m, y, t - 1)), (south, (m, y, t + 1))]
    for j in range(tiles):
        source = (unit_m, y, j)
        targets.append((differs(source, me), source))
    for j in range(tiles):
        source = (unit_m, 1, j)
        targets.append((jnp.logical_and(has_surface, differs(source, me)), source))
    self_unit = (unit_m == m).astype(jnp.int32)
    self_surface = jnp.logical_and(has_surface, unit_m == m).astype(jnp.int32)
    count = 1 + members * fields - self_unit + jnp.where(y == 0, 0, comps - self_surface)
    loading = pltpu.make_async_copy(field_ref, before, load.at[0])
    loading.start()
    greet(targets, count + north.astype(jnp.int32) + south.astype(jnp.int32))

    pairs = [(field_ref.at[s, 0, 0], partner.at[s]) for s in range(slots)]
    pairs += [(donors_ref, odonors), (blend_any, oblend_ref), (rate_any, orate_ref)]
    copies = [remote(p, q, psend.at[k], precv.at[k], across) for k, (p, q) in enumerate(pairs)]
    up, down = edge_copies(edge.at[0], low, high, esend, erecv, m, y, t)
    up_2, down_2 = edge_copies(edge.at[1], low_out, high_out, esend_2, erecv_2, m, y, t)

    def rows_of(j):
        return pl.ds(pl.multiple_of(j * rows, 8), rows)

    def begin(parts):
        away, copy, local = parts
        pl.when(away)(copy.start)
        pl.when(jnp.logical_not(away))(local.start)

    def end(parts):
        away, copy, local = parts
        pl.when(away)(copy.wait_send)
        pl.when(jnp.logical_not(away))(local.wait)

    def piece(f, c, ref):
        device = (c, y, m * fields + f)
        src = ref.at[f, pl.ds(c * per, per)]
        dst = u_ref.at[:, rows_of(t), :]
        copy = remote(src, dst, send.at[f * members + c], recv.at[t], device)
        return differs(device, me), copy, pltpu.make_async_copy(src, dst, loc.at[0])

    def hop(f, c):
        part = (f, pl.ds(c * per, per))
        k = f * members + c
        return remote(coefs.at[(1,) + part], hops.at[part], hsend.at[k], hrecv.at[k], across)

    def surface(s):
        device = (0, s, m * fields)
        dst = ru_ref.at[rows_of(t), :]
        copy = remote(looked.at[s], dst, rsend.at[s], rrecv.at[t], device)
        return differs(device, me), copy, pltpu.make_async_copy(looked.at[s], dst, loc.at[1])

    late = 1 + lax.rem(t, fields - 1)

    def field_at(j):
        at = jnp.where(j > late, j - 1, j)
        turn = lax.div(t, fields - 1) + t
        return jnp.where(j == late, 0, 1 + lax.rem(at + turn, fields - 1))

    def mixed(s, f, u):
        total = blend_ref[u, 0] * before[s, f, 0]
        for v in range(1, levels):
            total = total + blend_ref[u, v] * before[s, f, v]
        return forcing_rate * jnp.tanh(total)

    def added(s):
        received = lookup(partner[s], donors_ref[...])
        return coupling_rate * (received - before[s, 0, 0])

    def partner_arrives():
        for copy in copies[:slots]:
            copy.wait_recv()

    for copy in copies:
        copy.start()
    loading.wait()
    keep = pltpu.make_async_copy(after, new_ref, load.at[1])

    @pl.when(y == 0)
    def _():
        def step(i, _):
            s, j = slots - 1 - lax.div(i, fields), lax.rem(i, fields)
            f = field_at(j)
            for u in range(levels):
                forced[u * rows : (u + 1) * rows] = before[s, f, u] + mixed(s, f, u)

            pl.when(i == late)(partner_arrives)

            @pl.when(j == late)
            def _():
                forced[:rows] += added(s)

            result = dot3(forced[...], table_high, table_low)
            coefs[s, f] = result.reshape(levels, rows, coefs.shape[-1])

            @pl.when(s == 1)
            def _():
                for c in range(members):
                    hop(f, c).start()

            @pl.when(s == 0)
            def _():
                for c in range(members):
                    begin(piece(f, c, coefs.at[0]))

            return 0

        lax.fori_loop(0, slots * fields, step, 0)

    @pl.when(y == 1)
    def _():
        pl.when(t == 0)(lambda: zero(low))
        pl.when(t == tiles - 1)(lambda: zero(high))

        def gather(i, _):
            s, f = lax.div(i, fields), lax.rem(i, fields)
            for u in range(levels):
                edge[0, s, f, 0, u : u + 1] = before[s, f, u, :1]
                edge[0, s, f, 1, u : u + 1] = before[s, f, u, rows - 1 :]
            return 0

        lax.fori_loop(0, slots * fields, gather, 0)
        pl.when(north)(up.start)
        pl.when(south)(down.start)
        pl.when(south)(up.wait_recv)
        pl.when(north)(down.wait_recv)
        sea = land_ref[...] == 1

        def step(j, _):
            f = field_at(j)

            pl.when(j == late)(partner_arrives)

            def one(s, _):
                for u in range(levels):
                    value = before[s, f, u]
                    total = value + mixed(s, f, u)
                    ends = (low[s, f, u : u + 1], high[s, f, u : u + 1])
                    total = total + rate_ref[0, f] * laplacian_of(value, *ends)
                    after[s, f, u] = jnp.where(sea, total, value)

                @pl.when(j == late)
                def _():
                    after[s, 0, 0] = after[s, 0, 0] + jnp.where(sea, added(s), 0.0)

                for u in range(levels):
                    edge[1, s, f, 0, u : u + 1] = after[s, f, u, :1]
                    edge[1, s, f, 1, u : u + 1] = after[s, f, u, rows - 1 :]
                return 0

            lax.fori_loop(0, slots, one, 0)

            @pl.when(j == late)
            def _():
                copies[slots].wait_recv()
                for s in range(slots):
                    looked[s] = lookup(after[s, 0, 0], odonors[...])
                    begin(surface(s))

            @pl.when(j == fields - 1)
            def _():
                pl.when(north)(up_2.start)
                pl.when(south)(down_2.start)
                keep.start()

            for c in range(members):
                hop(f, c).wait_recv()
                begin(piece(f, c, hops))
            return 0

        lax.fori_loop(0, fields, step, 0)

    for j in range(tiles):
        away = differs((unit_m, y, j), me)
        part = u_ref.at[:, rows_of(j), :]
        arrival = remote(part, part, send.at[0], recv.at[j], me)
        pl.when(away)(arrival.wait_recv)
        arrival = remote(
            ru_ref.at[rows_of(j), :], ru_ref.at[rows_of(j), :], rsend.at[0], rrecv.at[j], me
        )
        away = jnp.logical_and(has_surface, differs((unit_m, 1, j), me))
        pl.when(away)(arrival.wait_recv)

    @pl.when(y == 0)
    def _():
        copies[slots].wait_recv()
        for f in range(fields):
            for c in range(members):
                hop(f, c).wait_send()
                end(piece(f, c, coefs.at[0]))

    @pl.when(y == 1)
    def _():
        for s in range(comps):
            end(surface(s))
        for f in range(fields):
            for c in range(members):
                end(piece(f, c, hops))
        keep.wait()

    for copy in copies:
        copy.wait_send()
    for copy in copies[slots + 1 :]:
        copy.wait_recv()
    for first, last in ((up, down), (up_2, down_2)):
        pl.when(north)(first.wait_send)
        pl.when(south)(last.wait_send)
    pl.when(south)(up_2.wait_recv)
    pl.when(north)(down_2.wait_recv)


def zero(ref):
    ref[...] = jnp.zeros(ref.shape, ref.dtype)


def swap_kernel(sizes, x_ref, xo_ref, send, recv):
    m, y, t = here()
    other = (1 - m, y, t)
    greet([(m >= 0, other)], 1)
    across = remote(x_ref, xo_ref, send.at[0], recv.at[0], other)
    across.start()
    across.wait()


def return_kernel(
    sizes,
    f_ref,
    p_ref,
    x_ref,
    o_ref,
    low_ref,
    high_ref,
    donors_ref,
    land_ref,
    weight_ref,
    blend_ref,
    rate_ref,
    own_ref,
    far_ref,
    score_ref,
    new_ref,
    faro_ref,
    part_ref,
    before,
    after,
    flux,
    sums,
    send,
    recv,
    fsend,
    frecv,
    psend,
    precv,
    loc,
    osend,
    orecv,
    keep,
    qsend,
    qrecv,
    ssend,
    srecv,
):
    members, comps, fields, tiles, rows = sizes
    me = m, y, t = here()
    per = f_ref.shape[0]
    unit_m, unit_f = t // fields, t % fields
    has_surface = jnp.logical_and(m == 0, unit_f == 0)
    other = (1 - m, y, t)
    pieces = [(s, f, c) for s in range(comps) for f in range(fields) for c in range(members)]
    targets = [(m >= 0, other)]
    for j in range(tiles):
        targets.append((jnp.logical_and(y == 1, j != t), (m, y, j)))
    for s in range(comps):
        source = (0, s, m * fields)
        targets.append((jnp.logical_and(y == 1, differs(source, me)), source))
    for s, f, c in pieces:
        source = (c, s, m * fields + f)
        targets.append((jnp.logical_and(y == 0, differs(source, me)), source))
    own_unit = jnp.logical_and(y == 0, unit_m == m).astype(jnp.int32)
    own_surface = jnp.logical_and(has_surface, jnp.logical_and(y == 1, unit_m == m))
    count = tiles - own_unit + jnp.where(y == 0, 1, tiles)
    greet(targets, count + jnp.where(has_surface, tiles - own_surface.astype(jnp.int32), 0))
    load = pltpu.make_async_copy(o_ref, before, loc.at[2])
    pl.when(y == 1)(load.start)

    def share(j):
        return remote(sums, part_ref.at[t], qsend.at[j], qrecv.at[t], (m, y, j))

    def surface(j):
        device = (unit_m, 1, j)
        part = x_ref.at[0, pl.ds(j * rows, rows), :]
        copy = remote(part, flux.at[y], ssend.at[j], srecv.at[y], device)
        return differs(device, me), copy, pltpu.make_async_copy(part, flux.at[y], loc.at[3])

    @pl.when(has_surface)
    def _():
        for j in range(tiles):
            away, copy, local = surface(j)
            pl.when(away)(copy.start)
            pl.when(jnp.logical_not(away))(local.start)

    def band(j):
        device = (unit_m, 0, j)
        src = f_ref.at[:, pl.ds(j * rows, rows), :]
        dst = own_ref.at[y, unit_f, pl.ds(m * per, per)]
        slot = (y * fields + unit_f) * members + m
        return (
            device,
            remote(src, dst, send.at[j], recv.at[slot], device),
            pltpu.make_async_copy(src, dst, loc.at[0]),
            remote(p_ref, score_ref.at[y], psend.at[j], precv.at[y], device),
            pltpu.make_async_copy(p_ref, score_ref.at[y], loc.at[1]),
        )

    for j in range(tiles):
        device, copy, local, point, local_point = band(j)
        away = differs(device, me)
        pl.when(away)(copy.start)
        pl.when(jnp.logical_not(away))(local.start)
        pl.when(jnp.logical_and(has_surface, away))(point.start)
        pl.when(jnp.logical_and(has_surface, jnp.logical_not(away)))(local_point.start)

    def forward(k):
        s, f, c = pieces[k]
        part = (s, f, pl.ds(c * per, per))
        return remote(own_ref.at[part], far_ref.at[part], fsend.at[k], frecv.at[k], other)

    @pl.when(y == 0)
    def _():
        for k, (s, f, c) in enumerate(pieces):
            part = own_ref.at[s, f, pl.ds(c * per, per)]
            away = differs((c, s, m * fields + f), me)
            arrival = remote(part, part, send.at[0], recv.at[k], me)
            pl.when(away)(arrival.wait_recv)
            own = pltpu.make_async_copy(part, part, loc.at[0])
            pl.when(jnp.logical_not(away))(own.wait)
            forward(k).start()
        for s in range(comps):
            away = differs((0, s, m * fields), me)
            arrival = remote(score_ref.at[s], score_ref.at[s], psend.at[0], precv.at[s], me)
            pl.when(away)(arrival.wait_recv)
            own = pltpu.make_async_copy(p_ref, score_ref.at[s], loc.at[1])
            pl.when(jnp.logical_not(away))(own.wait)
        for k in range(len(pieces)):
            forward(k).wait()

    for j in range(tiles):
        device, copy, local, point, local_point = band(j)
        away = differs(device, me)
        pl.when(away)(copy.wait_send)
        pl.when(jnp.logical_and(has_surface, away))(point.wait_send)

    def clone(s, f):
        i = s * fields + f
        part = (s, f)
        return (
            remote(after.at[part], faro_ref.at[part], osend.at[i], orecv.at[i], other),
            pltpu.make_async_copy(after.at[part], new_ref.at[part], keep.at[i]),
        )

    @pl.when(y == 1)
    def _():
        load.wait()
        sea = land_ref[...] == 1

        def flux_arrives():
            for s in range(comps):
                away = differs((0, s, m * fields), me)
                arrival = remote(flux.at[s], flux.at[s], ssend.at[0], srecv.at[s], me)
                pl.when(away)(arrival.wait_recv)
                part = x_ref.at[0, pl.ds(0, rows), :]
                own = pltpu.make_async_copy(part, flux.at[s], loc.at[3])
                pl.when(jnp.logical_not(away))(own.wait)

        def step(i, _):
            j, s = lax.div(i, comps), lax.rem(i, comps)
            f = lax.rem(j + 1, fields)
            pl.when(i == comps * (fields - 1))(flux_arrives)
            levels = before.shape[2]
            for u in range(levels):
                mixing = blend_ref[u, 0] * before[s, f, 0]
                for v in range(1, levels):
                    mixing = mixing + blend_ref[u, v] * before[s, f, v]
                value = before[s, f, u]
                forced = value + forcing_rate * jnp.tanh(mixing)
                ends = (
                    jnp.where(t == 0, 0.0, low_ref[s, f, u : u + 1]),
                    jnp.where(t == tiles - 1, 0.0, high_ref[s, f, u : u + 1]),
                )
                forced = forced + rate_ref[f] * laplacian_of(value, *ends)
                after[s, f, u] = jnp.where(sea, forced, value)

            @pl.when(f == 0)
            def _():
                value = before[s, 0, 0]
                extra = coupling_rate * (lookup(flux[s], donors_ref[...]) - value)
                result = after[s, 0, 0] + jnp.where(sea, extra, 0.0)
                after[s, 0, 0] = result
                sums[s] = weighted_sum(result, weight_ref[...], sums.shape[1:])

            across, own = clone(s, f)
            across.start()
            own.start()
            return 0

        lax.fori_loop(0, comps * fields, step, 0)
        mine = pltpu.make_async_copy(sums, part_ref.at[t], loc.at[4])
        mine.start()
        for j in range(tiles):
            pl.when(j != t)(share(j).start)
        mine.wait()
        for j in range(tiles):
            arrival = remote(part_ref.at[j], part_ref.at[j], qsend.at[0], qrecv.at[j], me)
            pl.when(j != t)(arrival.wait_recv)
            pl.when(j != t)(share(j).wait_send)
        for s in range(comps):
            for f in range(fields):
                across, own = clone(s, f)
                across.wait()
                own.wait()

    @pl.when(has_surface)
    def _():
        for j in range(tiles):
            away, copy, local = surface(j)
            pl.when(away)(copy.wait_send)


def laplacian_of(value, low, high):
    rows, lon_count = value.shape
    row = lax.broadcasted_iota(jnp.int32, (rows, lon_count), 0)
    north = jnp.where(row == 0, low, pltpu.roll(value, 1, 0))
    south = jnp.where(row == rows - 1, high, pltpu.roll(value, rows - 1, 0))
    east, west = pltpu.roll(value, 1, 1), pltpu.roll(value, lon_count - 1, 1)
    return south + north + east + west - 4.0 * value


def weighted_sum(value, weights, shape):
    total = jnp.sum(value * weights, axis=0, keepdims=True)
    total = jnp.sum(total, axis=1, keepdims=True) / value.shape[1]
    return jnp.broadcast_to(total, shape)


def call(kernel, collective_id, outs, sems, *args):
    return pl.pallas_call(
        kernel,
        out_shape=[
            jax.ShapeDtypeStruct(out.shape, out.dtype)
            if hasattr(out, "dtype")
            else jax.ShapeDtypeStruct(out, jnp.float32)
            for out in outs
        ],
        in_specs=[pl.BlockSpec(memory_space=pl.ANY)] * len(args),
        out_specs=[pl.BlockSpec(memory_space=pl.ANY)] * len(outs),
        scratch_shapes=[pltpu.SemaphoreType.DMA((n,)) for n in sems],
        compiler_params=pltpu.CompilerParams(collective_id=collective_id, has_side_effects=True),
    )(*args)


def matmul(a, b):
    return jnp.dot(a, b, precision=precise, preferred_element_type=jnp.float32)


def split(value):
    high = value.astype(jnp.bfloat16)
    return high, (value - high.astype(jnp.float32)).astype(jnp.bfloat16)


def split_table(table):
    high = table.astype(jnp.bfloat16)
    low = (table - high.astype(np.float32)).astype(jnp.bfloat16)
    return jnp.asarray(high), jnp.asarray(low)


def dot3(value, high_ref, low_ref):
    high, low = split(value)
    total = jnp.dot(high, low_ref[...], preferred_element_type=jnp.float32)
    total = total + jnp.dot(low, high_ref[...], preferred_element_type=jnp.float32)
    return total + jnp.dot(high, high_ref[...], preferred_element_type=jnp.float32)


def lookup(surface, donors):
    lon_count = surface.shape[-1]
    offset = donors - lax.broadcasted_iota(jnp.int32, donors.shape, 1)
    offset = jnp.where(offset > lon_count // 2, offset - lon_count, offset)
    offset = jnp.where(offset < -(lon_count // 2), offset + lon_count, offset)
    result = surface
    for shift in (-1, 1, 2, 3, 4):
        moved = pltpu.roll(surface, (-shift) % lon_count, 1)
        result = jnp.where(offset == shift, moved, result)
    return result


def whole_spec(array):
    zeros = (0,) * array.ndim
    return pl.BlockSpec(array.shape, lambda *_: zeros)


def scalar_spec():
    return pl.BlockSpec(memory_space=pltpu.SMEM)


def state_spec(shape):
    zeros = (0,) * (len(shape) - 2)
    return pl.BlockSpec((1, 1) + tuple(shape[2:]), lambda s, f, *_: (s, f) + zeros)


large = pltpu.CompilerParams(vmem_limit_bytes=24 * 1024 * 1024)


def air_last_kernel(inside_ref, near_ref, own_ref, far_ref, high_ref, low_ref, out_ref):
    near = near_ref[pl.program_id(0)] == 1
    levels, rows, waves = own_ref.shape[2:]
    coefs = jnp.where(near, own_ref[0, 0], far_ref[0, 0]).reshape(levels * rows, waves)
    out_ref[0, 0] = dot3(coefs, high_ref, low_ref).reshape(out_ref.shape[2:])


def sea_last_kernel(inside_ref, near_ref, own_ref, far_ref, out_ref):
    near = near_ref[pl.program_id(0)] == 1
    out_ref[0, 0] = jnp.where(near, own_ref[0, 0], far_ref[0, 0])


def resampled(kernel, inside, near, own, far, tables, lon_count):
    shape = own.shape[:-1] + (lon_count,)

    def parent(s, f, inside_ref, near_ref):
        return (inside_ref[s], f, 0, 0, 0)

    parent_spec = pl.BlockSpec((1, 1) + own.shape[2:], parent)
    return pl.pallas_call(
        kernel,
        grid_spec=pltpu.PrefetchScalarGridSpec(
            num_scalar_prefetch=2,
            grid=own.shape[:2],
            in_specs=[parent_spec, parent_spec] + [whole_spec(table) for table in tables],
            out_specs=state_spec(shape),
        ),
        out_shape=jax.ShapeDtypeStruct(shape, jnp.float32),
        compiler_params=large,
    )(inside, near, own, far, *tables)


def left3(high_ref, low_ref, value):
    high, low = split(value)
    total = jnp.dot(low_ref[...], high, preferred_element_type=jnp.float32)
    total = total + jnp.dot(high_ref[...], low, preferred_element_type=jnp.float32)
    return total + jnp.dot(high_ref[...], high, preferred_element_type=jnp.float32)


def filtered(value, squares_ref, rate_ref, forward, inverse):
    spectrum = left3(*forward, value) / (1.0 + rate_ref[0] * squares_ref[...])
    return left3(*inverse, spectrum)


def to_grid_kernel(x_ref, sq_ref, rate_ref, fh, fl, ih, il, gh, gl, out_ref):
    coefs = filtered(x_ref[0], sq_ref, rate_ref, (fh, fl), (ih, il))
    out_ref[0] = dot3(coefs, gh, gl)


def to_coefs_kernel(
    x_ref,
    o_ref,
    sst_ref,
    here_ref,
    there_ref,
    flag_ref,
    w_ref,
    sq_ref,
    rate_ref,
    fh,
    fl,
    ih,
    il,
    gh,
    gl,
    out_ref,
    sum_ref,
    forced,
):
    per = x_ref.shape[0]
    u = pl.program_id(0)
    mixing = here_ref[u, 0] * x_ref[0] + there_ref[u, 0] * o_ref[0]
    for v in range(1, per):
        mixing = mixing + here_ref[u, v] * x_ref[v] + there_ref[u, v] * o_ref[v]
    forced[...] = x_ref[u] + forcing_rate * jnp.tanh(mixing)

    @pl.when(jnp.logical_and(u == 0, flag_ref[0] == 1))
    def _():
        forced[...] += coupling_rate * (sst_ref[...] - x_ref[0])

    coefs = dot3(forced[...], gh, gl)
    result = filtered(coefs, sq_ref, rate_ref, (fh, fl), (ih, il))
    out_ref[0] = result

    @pl.when(u == 0)
    def _():
        total = jnp.sum(result[:, : w_ref.shape[1]] * w_ref[...], axis=0, keepdims=True)
        total = jnp.sum(total, axis=1, keepdims=True)
        sum_ref[...] = jnp.broadcast_to(total, sum_ref.shape)


def level_spec(shape):
    return pl.BlockSpec((1,) + tuple(shape[1:]), lambda u: (u, 0, 0))


def to_grid(value, squares, rate, tables, lon_count):
    shape = value.shape[:2] + (lon_count,)
    return pl.pallas_call(
        to_grid_kernel,
        grid=value.shape[:1],
        out_shape=jax.ShapeDtypeStruct(shape, jnp.float32),
        in_specs=[level_spec(value.shape), whole_spec(squares), scalar_spec()]
        + [whole_spec(table) for table in tables],
        out_specs=level_spec(shape),
        compiler_params=large,
    )(value, squares, rate, *tables)


def to_coefs(state, other, sst, mine, theirs, flag, weights, squares, rate, tables):
    shape = state.shape[:2] + (squares.shape[1],)
    return pl.pallas_call(
        to_coefs_kernel,
        grid=state.shape[:1],
        out_shape=[
            jax.ShapeDtypeStruct(shape, jnp.float32),
            jax.ShapeDtypeStruct((8, 128), jnp.float32),
        ],
        in_specs=[whole_spec(state), whole_spec(other), whole_spec(sst)]
        + [scalar_spec()] * 3
        + [whole_spec(weights), whole_spec(squares), scalar_spec()]
        + [whole_spec(table) for table in tables],
        out_specs=[level_spec(shape), pl.BlockSpec((8, 128), lambda u: (0, 0))],
        scratch_shapes=[pltpu.VMEM(state.shape[1:], jnp.float32)],
        compiler_params=large,
    )(state, other, sst, mine, theirs, flag, weights, squares, rate, *tables)


def by_units(
    member_state,
    layer_blend_operator,
    coefficient,
    interpolation_donor_meridians,
    land_sea,
    ancestry,
):
    member, component, tile = here()
    members, comps, tiles = (lax.axis_size(name) for name in ("member", "comp", "tile"))
    field = member_state[:, 0]
    slots, fields, levels, rows, lon_count = field.shape
    per = levels // members
    sizes = (members, comps, fields, tiles, rows)
    lon_basis, number = kept_lon_basis(lon_count)
    waves = lon_basis.shape[0]
    lon_columns = np.ascontiguousarray(lon_basis.T)
    lat_basis = lat_table()
    lat_tables = split_table(lat_basis) + split_table(np.ascontiguousarray(lat_basis.T))
    weights = row_weights()
    weight_total = float(weights.sum())
    order = np.arange(MODES).astype(np.float32)
    squares = order[:, None] ** 2 + number[None, :] ** 2
    squares = jnp.asarray((squares / np.float32(MODES * MODES)).astype(np.float32))
    air_weights = np.zeros((LAT, 128), np.float32)
    air_weights[:, 0] = weights * lon_basis[0, 0] / weight_total
    my_weights = lax.dynamic_slice_in_dim(jnp.asarray(weights[:, None]), tile * rows, rows)

    is_air = component == 0
    blend = layer_blend_operator[0]
    rate = coefficient[0]
    donors = interpolation_donor_meridians[0]
    anywhere = pl.BlockSpec(memory_space=pl.ANY)
    inside = pl.BlockSpec(memory_space=pltpu.VMEM)
    halo = (slots, fields, levels, lon_count)
    surface = (slots, rows, lon_count)
    coefs_shape = (slots, fields, levels, rows, waves)
    out_shapes = [(per, LAT, waves), (LAT, lon_count), field.shape, halo, halo]
    out_shapes += [blend.shape, coefficient.shape]
    scratch = [field.shape, field.shape, coefs_shape, coefs_shape[1:]]
    scratch += [(levels * rows, lon_count), surface]
    later = [surface, (2, slots, fields, 2, levels, lon_count), halo, halo]
    pieces = members * fields
    sems = (2, slots + 3, slots + 3, 2, 2, pieces, pieces, pieces, comps, tiles, tiles, 2, 2, 2)
    gathered, sst, ocean, low, high, other_blend, other_rate = pl.pallas_call(
        functools.partial(first_kernel, sizes),
        out_shape=[jax.ShapeDtypeStruct(shape, jnp.float32) for shape in out_shapes],
        in_specs=[anywhere, inside, inside]
        + [scalar_spec()] * 2
        + [anywhere] * 2
        + [inside] * 2,
        out_specs=[anywhere] * len(out_shapes),
        scratch_shapes=[pltpu.VMEM(shape, jnp.float32) for shape in scratch]
        + [pltpu.VMEM(donors.shape, jnp.int32)]
        + [pltpu.VMEM(shape, jnp.float32) for shape in later]
        + [pltpu.SemaphoreType.DMA((n,)) for n in sems],
        compiler_params=pltpu.CompilerParams(
            collective_id=0, has_side_effects=True, vmem_limit_bytes=26 * 1024 * 1024
        ),
    )(
        field,
        donors,
        land_sea,
        blend,
        coefficient,
        blend,
        coefficient,
        *split_table(lon_columns),
    )
    air_blend = jnp.where(is_air, blend, other_blend)
    air_rate = jnp.where(is_air, rate, other_rate[0])
    unit_field = tile % fields
    unit_rate = lax.dynamic_slice_in_dim(air_rate, unit_field, 1)
    state = to_grid(
        gathered, squares, unit_rate, lat_tables + split_table(lon_basis), lon_count
    )
    (other_state,) = call(
        functools.partial(swap_kernel, sizes), 1, [(per, LAT, lon_count)], (1, 1), state
    )
    mine = lax.dynamic_slice_in_dim(air_blend, member * per, per)
    mine_own = lax.dynamic_slice_in_dim(mine, member * per, per, axis=1)
    mine_other = lax.dynamic_slice_in_dim(mine, (1 - member) * per, per, axis=1)
    flag = jnp.logical_and(member == 0, unit_field == 0).astype(jnp.int32).reshape(1)
    back, air_point = to_coefs(
        state,
        other_state,
        sst,
        mine_own,
        mine_other,
        flag,
        jnp.asarray(air_weights),
        squares,
        unit_rate,
        lat_tables + split_table(lon_columns),
    )

    count = slots * fields * members
    out_shapes = [coefs_shape, coefs_shape, (slots, 8, 128)]
    out_shapes += [field.shape, field.shape, (tiles, slots, 8, 128)]
    scratch = [field.shape, field.shape, (slots, rows, lon_count), (slots, 8, 128)]
    sems = (tiles, count, count, count, tiles, comps, 5)
    sems += (slots * fields,) * 3 + (tiles, tiles, tiles, comps)
    own, far, air_scores, ocean, far_ocean, sea_parts = pl.pallas_call(
        functools.partial(return_kernel, sizes),
        out_shape=[jax.ShapeDtypeStruct(shape, jnp.float32) for shape in out_shapes],
        in_specs=[anywhere] * 4 + [inside] * 5 + [scalar_spec()] * 2,
        out_specs=[anywhere] * len(out_shapes),
        scratch_shapes=[pltpu.VMEM(shape, jnp.float32) for shape in scratch]
        + [pltpu.SemaphoreType.DMA((n,)) for n in sems],
        compiler_params=pltpu.CompilerParams(
            collective_id=2, has_side_effects=True, vmem_limit_bytes=18 * 1024 * 1024
        ),
    )(back, air_point, state, ocean, low, high, donors, land_sea, my_weights, blend, rate)
    parents = lax.dynamic_slice_in_dim(ancestry, member * slots, slots)

    inside = parents % slots
    near = (parents // slots == member).astype(jnp.int32)

    def air_last(_):
        grid = resampled(
            air_last_kernel, inside, near, own, far, split_table(lon_basis), lon_count
        )
        return grid.reshape(member_state.shape), air_scores[:, 0, :1]

    def sea_last(_):
        score = jnp.sum(sea_parts[:, :, 0, :1], axis=0) / weight_total
        states = resampled(sea_last_kernel, inside, near, ocean, far_ocean, (), lon_count)
        return states.reshape(member_state.shape), score

    return lax.cond(is_air, air_last, sea_last, 0)


def by_bands(
    member_state,
    layer_blend_operator,
    coefficient,
    interpolation_donor_meridians,
    land_sea,
    ancestry,
):
    slot_count = member_state.shape[0]
    component = lax.axis_index("comp")
    tile_index = lax.axis_index("tile")
    tile_count = lax.axis_size("tile")
    row_count = member_state.shape[4]
    lon_count = member_state.shape[5]
    lon_table, number = kept_lon_basis(lon_count)
    lon_basis = jnp.asarray(lon_table)
    local_modes = lon_table.shape[0] // tile_count
    my_numbers = lax.dynamic_slice_in_dim(jnp.asarray(number), tile_index * local_modes, local_modes)
    lat_basis = jnp.asarray(lat_table())
    order = jnp.arange(MODES, dtype=jnp.int32).astype(jnp.float32)
    sea_cells = land_sea[None, None] == 1
    diffusivity = coefficient[0][:, None, None, None]
    weights = row_weights()
    my_weights = lax.dynamic_slice_in_dim(jnp.asarray(weights), tile_index * row_count, row_count)
    weight_total = float(weights.sum())
    stepped_list = []
    partial_list = []
    for slot in range(slot_count):
        field = member_state[slot, 0]
        for _ in range(STEPS):
            surface = field[0, 0]
            partner = partner_2(surface, "comp", 0)
            received = donor_lookup(partner, interpolation_donor_meridians[0])
            mixing = jnp.einsum("uv,fvjx->fujx", layer_blend_operator[0], field, precision=precise)
            forced = field + forcing_rate * jnp.tanh(mixing)
            forced = forced.at[0, 0].add(coupling_rate * (received - surface))
            spectral_gain = 1.0 / (
                1.0
                + coefficient[0][:, None, None]
                * (order[None, None, :] ** 2 + my_numbers[None, :, None] ** 2)
                / (MODES * MODES)
            )
            fourier = jnp.einsum("fvjx,qx->fvjq", forced, lon_basis, precision=precise)
            spectrum = jnp.einsum(
                "lj,fkjq->fkql",
                lat_basis,
                lax.all_to_all(fourier, "tile", split_axis=3, concat_axis=2, tiled=True),
                precision=precise,
            )
            spectrum = spectrum * spectral_gain[:, None]
            returned = jnp.einsum("lj,fkql->fkjq", lat_basis, spectrum, precision=precise)
            filtered = lax.all_to_all(returned, "tile", split_axis=2, concat_axis=3, tiled=True)
            block_atm = jnp.einsum("fvjq,qx->fvjx", filtered, lon_basis, precision=precise)
            padded = padded_2(field, (("tile", 2),), 1)
            laplacian = (
                padded[:, :, 2:]
                + padded[:, :, :-2]
                + jnp.roll(field, 1, axis=3)
                + jnp.roll(field, -1, axis=3)
                - 4.0 * field
            )
            new_ocn = jnp.where(sea_cells, forced + diffusivity * laplacian, field)
            field = jnp.where(component == 0, block_atm, new_ocn)
        stepped_list.append(field)
        partial_list.append(jnp.sum(jnp.mean(field[0, 0], axis=1) * my_weights))
    local_states = jnp.stack(stepped_list)
    region_sums = lax.psum(jnp.stack(partial_list), "tile")
    region_score = (region_sums / weight_total).reshape(slot_count, 1)
    member_index = lax.axis_index("member")
    my_parents = lax.dynamic_slice_in_dim(ancestry, member_index * slot_count, slot_count)
    gathered = lax.all_gather(local_states, "member", axis=0, tiled=True)
    chosen = jnp.take(gathered, my_parents, axis=0)
    return (chosen[:, None], region_score)


def local(member_state, *others):
    members, comps, tiles = (lax.axis_size(name) for name in ("member", "comp", "tile"))
    slots, _, fields, levels, rows, _ = member_state.shape
    fits = members == 2 and comps == 2 and slots == comps and tiles == members * fields
    if fits and levels % members == 0 and rows % 8 == 0:
        return by_units(member_state, *others)
    return by_bands(member_state, *others)


def solution(mesh):
    return jax.shard_map(
        local,
        mesh=mesh,
        in_specs=(
            P("member", "comp", None, None, "tile", None),
            P("comp", None, None),
            P("comp", None),
            P("comp", "tile", None),
            P("tile", None),
            P(),
        ),
        out_specs=(P("member", "comp", None, None, "tile", None), P("member", "comp")),
        check_vma=False,
    )
```

```python
import functools
import math

import jax
import jax.numpy as jnp
import numpy as np
from jax import lax
from jax.experimental import pallas as pl
from jax.experimental.pallas import tpu as pltpu
from jax.sharding import PartitionSpec as P

LAT = 384
MODES = 256
STEPS = 2
MESH = pl.DeviceIdType.MESH


coupling_rate = 0.5
forcing_rate = 0.5
precise = lax.Precision.HIGH


def partner_2(value, axis, distance):
    mask = 2**distance
    pairs = [(source, source ^ mask) for source in range(lax.axis_size(axis))]
    return lax.ppermute(value, axis, pairs)


def padded_2(block, sides, width):
    for axis, dim in sides:
        count = lax.axis_size(axis)
        forward = [(i, i + 1) for i in range(count - 1)]
        backward = [(target, source) for source, target in forward]
        low = lax.ppermute(
            lax.slice_in_dim(block, block.shape[dim] - width, None, axis=dim), axis, forward
        )
        high = lax.ppermute(lax.slice_in_dim(block, 0, width, axis=dim), axis, backward)
        block = jnp.concatenate([low, block, high], axis=dim)
    return block


def kept_lon_basis(lon_count):
    wave = np.arange(2 * MODES)
    is_cosine = wave < MODES
    number = np.where(is_cosine, wave, wave - MODES + 1).astype(np.float32)
    cells = np.arange(lon_count).astype(np.float32)
    angle = np.float32(2.0 * math.pi) * number[:, None] * cells[None, :] / np.float32(lon_count)
    scale = np.where(number == 0.0, math.sqrt(1.0 / lon_count), math.sqrt(2.0 / lon_count)).astype(
        np.float32
    )
    table = np.where(is_cosine[:, None], np.cos(angle), np.sin(angle)) * scale[:, None]
    return table.astype(np.float32), number


def lat_table():
    order = np.arange(MODES).astype(np.float32)
    cells = np.arange(LAT).astype(np.float32)
    scale = np.where(order == 0.0, math.sqrt(1.0 / LAT), math.sqrt(2.0 / LAT)).astype(np.float32)
    angle = np.float32(math.pi) * (cells[None, :] + np.float32(0.5)) * order[:, None]
    return (np.cos(angle / np.float32(LAT)) * scale[:, None]).astype(np.float32)


def row_weights():
    rows = np.arange(LAT).astype(np.float32)
    return np.cos(
        np.float32(math.pi) * ((rows + np.float32(0.5)) / np.float32(LAT) - np.float32(0.5))
    ).astype(np.float32)


def donor_lookup(partner, donors):
    lon_count = partner.shape[-1]
    cells = jnp.arange(lon_count, dtype=jnp.int32)[None, :]
    offsets = jnp.mod(donors - cells, lon_count)
    result = jnp.zeros_like(partner)
    for shift_by in (-1, 0, 1, 2, 3, 4):
        moved = jnp.roll(partner, -shift_by, axis=-1)
        result = result + jnp.where(offsets == shift_by % lon_count, moved, 0.0)
    return result


def remote(src, dst, send_sem, recv_sem, device):
    return pltpu.make_async_remote_copy(
        src_ref=src,
        dst_ref=dst,
        send_sem=send_sem,
        recv_sem=recv_sem,
        device_id=device,
        device_id_type=MESH,
    )


def here():
    return lax.axis_index("member"), lax.axis_index("comp"), lax.axis_index("tile")


def greet(targets, count):
    barrier = pltpu.get_barrier_semaphore()
    for condition, device in targets:

        @pl.when(condition)
        def _():
            pl.semaphore_signal(barrier, inc=1, device_id=device, device_id_type=MESH)

    @pl.when(count > 0)
    def _():
        pl.semaphore_wait(barrier, count)


def differs(a, b):
    return jnp.logical_or(a[0] != b[0], jnp.logical_or(a[1] != b[1], a[2] != b[2]))


def shores(y, t, tiles):
    return jnp.logical_and(y == 1, t > 0), jnp.logical_and(y == 1, t < tiles - 1)


def edge_copies(edge_ref, low_ref, high_ref, esend, erecv, m, y, t):
    up = remote(edge_ref.at[:, :, 0], high_ref, esend.at[0], erecv.at[0], (m, y, t - 1))
    down = remote(edge_ref.at[:, :, 1], low_ref, esend.at[1], erecv.at[1], (m, y, t + 1))
    return up, down


def first_kernel(
    sizes,
    field_ref,
    donors_ref,
    land_ref,
    blend_ref,
    rate_ref,
    blend_any,
    rate_any,
    table_high,
    table_low,
    u_ref,
    ru_ref,
    new_ref,
    low_out,
    high_out,
    oblend_ref,
    orate_ref,
    before,
    after,
    coefs,
    hops,
    forced,
    partner,
    odonors,
    looked,
    edge,
    low,
    high,
    load,
    psend,
    precv,
    esend,
    erecv,
    send,
    hsend,
    hrecv,
    rsend,
    recv,
    rrecv,
    loc,
    esend_2,
    erecv_2,
):
    members, comps, fields, tiles, rows = sizes
    me = m, y, t = here()
    slots, _, levels = before.shape[:3]
    per = levels // members
    unit_m, unit_f = t // fields, t % fields
    has_surface = jnp.logical_and(m == 0, unit_f == 0)
    across = (m, 1 - y, t)
    north, south = shores(y, t, tiles)
    targets = [(m >= 0, across), (north, (m, y, t - 1)), (south, (m, y, t + 1))]
    for j in range(tiles):
        source = (unit_m, y, j)
        targets.append((differs(source, me), source))
    for j in range(tiles):
        source = (unit_m, 1, j)
        targets.append((jnp.logical_and(has_surface, differs(source, me)), source))
    self_unit = (unit_m == m).astype(jnp.int32)
    self_surface = jnp.logical_and(has_surface, unit_m == m).astype(jnp.int32)
    count = 1 + members * fields - self_unit + jnp.where(y == 0, 0, comps - self_surface)
    loading = pltpu.make_async_copy(field_ref, before, load.at[0])
    loading.start()
    greet(targets, count + north.astype(jnp.int32) + south.astype(jnp.int32))

    pairs = [(field_ref.at[s, 0, 0], partner.at[s]) for s in range(slots)]
    pairs += [(donors_ref, odonors), (blend_any, oblend_ref), (rate_any, orate_ref)]
    copies = [remote(p, q, psend.at[k], precv.at[k], across) for k, (p, q) in enumerate(pairs)]
    up, down = edge_copies(edge.at[0], low, high, esend, erecv, m, y, t)
    up_2, down_2 = edge_copies(edge.at[1], low_out, high_out, esend_2, erecv_2, m, y, t)

    def rows_of(j):
        return pl.ds(pl.multiple_of(j * rows, 8), rows)

    def begin(parts):
        away, copy, local = parts
        pl.when(away)(copy.start)
        pl.when(jnp.logical_not(away))(local.start)

    def end(parts):
        away, copy, local = parts
        pl.when(away)(copy.wait_send)
        pl.when(jnp.logical_not(away))(local.wait)

    def piece(f, c, ref):
        device = (c, y, m * fields + f)
        src = ref.at[f, pl.ds(c * per, per)]
        dst = u_ref.at[:, rows_of(t), :]
        copy = remote(src, dst, send.at[f * members + c], recv.at[t], device)
        return differs(device, me), copy, pltpu.make_async_copy(src, dst, loc.at[0])

    def hop(f, c):
        part = (f, pl.ds(c * per, per))
        k = f * members + c
        return remote(coefs.at[(1,) + part], hops.at[part], hsend.at[k], hrecv.at[k], across)

    def surface(s):
        device = (0, s, m * fields)
        dst = ru_ref.at[rows_of(t), :]
        copy = remote(looked.at[s], dst, rsend.at[s], rrecv.at[t], device)
        return differs(device, me), copy, pltpu.make_async_copy(looked.at[s], dst, loc.at[1])

    late = 1 + lax.rem(t, fields - 1)

    def field_at(j):
        at = jnp.where(j > late, j - 1, j)
        turn = lax.div(t, fields - 1) + t
        return jnp.where(j == late, 0, 1 + lax.rem(at + turn, fields - 1))

    def mixed(s, f, u):
        total = blend_ref[u, 0] * before[s, f, 0]
        for v in range(1, levels):
            total = total + blend_ref[u, v] * before[s, f, v]
        return forcing_rate * jnp.tanh(total)

    def added(s):
        received = lookup(partner[s], donors_ref[...])
        return coupling_rate * (received - before[s, 0, 0])

    def partner_arrives():
        for copy in copies[:slots]:
            copy.wait_recv()

    for copy in copies:
        copy.start()
    loading.wait()
    keep = pltpu.make_async_copy(after, new_ref, load.at[1])

    @pl.when(y == 0)
    def _():
        def step(i, _):
            s, j = slots - 1 - lax.div(i, fields), lax.rem(i, fields)
            f = field_at(j)
            for u in range(levels):
                forced[u * rows : (u + 1) * rows] = before[s, f, u] + mixed(s, f, u)

            pl.when(i == late)(partner_arrives)

            @pl.when(j == late)
            def _():
                forced[:rows] += added(s)

            result = dot3(forced[...], table_high, table_low)
            coefs[s, f] = result.reshape(levels, rows, coefs.shape[-1])

            @pl.when(s == 1)
            def _():
                for c in range(members):
                    hop(f, c).start()

            @pl.when(s == 0)
            def _():
                for c in range(members):
                    begin(piece(f, c, coefs.at[0]))

            return 0

        lax.fori_loop(0, slots * fields, step, 0)

    @pl.when(y == 1)
    def _():
        pl.when(t == 0)(lambda: zero(low))
        pl.when(t == tiles - 1)(lambda: zero(high))

        def gather(i, _):
            s, f = lax.div(i, fields), lax.rem(i, fields)
            for u in range(levels):
                edge[0, s, f, 0, u : u + 1] = before[s, f, u, :1]
                edge[0, s, f, 1, u : u + 1] = before[s, f, u, rows - 1 :]
            return 0

        lax.fori_loop(0, slots * fields, gather, 0)
        pl.when(north)(up.start)
        pl.when(south)(down.start)
        pl.when(south)(up.wait_recv)
        pl.when(north)(down.wait_recv)
        sea = land_ref[...] == 1

        def step(j, _):
            f = field_at(j)

            pl.when(j == late)(partner_arrives)

            def one(s, _):
                for u in range(levels):
                    value = before[s, f, u]
                    total = value + mixed(s, f, u)
                    ends = (low[s, f, u : u + 1], high[s, f, u : u + 1])
                    total = total + rate_ref[0, f] * laplacian_of(value, *ends)
                    after[s, f, u] = jnp.where(sea, total, value)

                @pl.when(j == late)
                def _():
                    after[s, 0, 0] = after[s, 0, 0] + jnp.where(sea, added(s), 0.0)

                for u in range(levels):
                    edge[1, s, f, 0, u : u + 1] = after[s, f, u, :1]
                    edge[1, s, f, 1, u : u + 1] = after[s, f, u, rows - 1 :]
                return 0

            lax.fori_loop(0, slots, one, 0)

            @pl.when(j == late)
            def _():
                copies[slots].wait_recv()
                for s in range(slots):
                    looked[s] = lookup(after[s, 0, 0], odonors[...])
                    begin(surface(s))

            @pl.when(j == fields - 1)
            def _():
                pl.when(north)(up_2.start)
                pl.when(south)(down_2.start)
                keep.start()

            for c in range(members):
                hop(f, c).wait_recv()
                begin(piece(f, c, hops))
            return 0

        lax.fori_loop(0, fields, step, 0)

    for j in range(tiles):
        away = differs((unit_m, y, j), me)
        part = u_ref.at[:, rows_of(j), :]
        arrival = remote(part, part, send.at[0], recv.at[j], me)
        pl.when(away)(arrival.wait_recv)
        arrival = remote(
            ru_ref.at[rows_of(j), :], ru_ref.at[rows_of(j), :], rsend.at[0], rrecv.at[j], me
        )
        away = jnp.logical_and(has_surface, differs((unit_m, 1, j), me))
        pl.when(away)(arrival.wait_recv)

    @pl.when(y == 0)
    def _():
        copies[slots].wait_recv()
        for f in range(fields):
            for c in range(members):
                hop(f, c).wait_send()
                end(piece(f, c, coefs.at[0]))

    @pl.when(y == 1)
    def _():
        for s in range(comps):
            end(surface(s))
        for f in range(fields):
            for c in range(members):
                end(piece(f, c, hops))
        keep.wait()

    for copy in copies:
        copy.wait_send()
    for copy in copies[slots + 1 :]:
        copy.wait_recv()
    for first, last in ((up, down), (up_2, down_2)):
        pl.when(north)(first.wait_send)
        pl.when(south)(last.wait_send)
    pl.when(south)(up_2.wait_recv)
    pl.when(north)(down_2.wait_recv)


def zero(ref):
    ref[...] = jnp.zeros(ref.shape, ref.dtype)


def swap_kernel(sizes, x_ref, xo_ref, send, recv):
    m, y, t = here()
    other = (1 - m, y, t)
    greet([(m >= 0, other)], 1)
    across = remote(x_ref, xo_ref, send.at[0], recv.at[0], other)
    across.start()
    across.wait()


def return_kernel(
    sizes,
    f_ref,
    p_ref,
    x_ref,
    o_ref,
    low_ref,
    high_ref,
    donors_ref,
    land_ref,
    weight_ref,
    blend_ref,
    rate_ref,
    own_ref,
    far_ref,
    score_ref,
    new_ref,
    faro_ref,
    part_ref,
    before,
    after,
    flux,
    sums,
    send,
    recv,
    fsend,
    frecv,
    psend,
    precv,
    loc,
    osend,
    orecv,
    keep,
    qsend,
    qrecv,
    ssend,
    srecv,
):
    members, comps, fields, tiles, rows = sizes
    me = m, y, t = here()
    per = f_ref.shape[0]
    unit_m, unit_f = t // fields, t % fields
    has_surface = jnp.logical_and(m == 0, unit_f == 0)
    other = (1 - m, y, t)
    pieces = [(s, f, c) for s in range(comps) for f in range(fields) for c in range(members)]
    targets = [(m >= 0, other)]
    for j in range(tiles):
        targets.append((jnp.logical_and(y == 1, j != t), (m, y, j)))
    for s in range(comps):
        source = (0, s, m * fields)
        targets.append((jnp.logical_and(y == 1, differs(source, me)), source))
    for s, f, c in pieces:
        source = (c, s, m * fields + f)
        targets.append((jnp.logical_and(y == 0, differs(source, me)), source))
    own_unit = jnp.logical_and(y == 0, unit_m == m).astype(jnp.int32)
    own_surface = jnp.logical_and(has_surface, jnp.logical_and(y == 1, unit_m == m))
    count = tiles - own_unit + jnp.where(y == 0, 1, tiles)
    greet(targets, count + jnp.where(has_surface, tiles - own_surface.astype(jnp.int32), 0))
    load = pltpu.make_async_copy(o_ref, before, loc.at[2])
    pl.when(y == 1)(load.start)

    def share(j):
        return remote(sums, part_ref.at[t], qsend.at[j], qrecv.at[t], (m, y, j))

    def surface(j):
        device = (unit_m, 1, j)
        part = x_ref.at[0, pl.ds(j * rows, rows), :]
        copy = remote(part, flux.at[y], ssend.at[j], srecv.at[y], device)
        return differs(device, me), copy, pltpu.make_async_copy(part, flux.at[y], loc.at[3])

    @pl.when(has_surface)
    def _():
        for j in range(tiles):
            away, copy, local = surface(j)
            pl.when(away)(copy.start)
            pl.when(jnp.logical_not(away))(local.start)

    def band(j):
        device = (unit_m, 0, j)
        src = f_ref.at[:, pl.ds(j * rows, rows), :]
        dst = own_ref.at[y, unit_f, pl.ds(m * per, per)]
        slot = (y * fields + unit_f) * members + m
        return (
            device,
            remote(src, dst, send.at[j], recv.at[slot], device),
            pltpu.make_async_copy(src, dst, loc.at[0]),
            remote(p_ref, score_ref.at[y], psend.at[j], precv.at[y], device),
            pltpu.make_async_copy(p_ref, score_ref.at[y], loc.at[1]),
        )

    for j in range(tiles):
        device, copy, local, point, local_point = band(j)
        away = differs(device, me)
        pl.when(away)(copy.start)
        pl.when(jnp.logical_not(away))(local.start)
        pl.when(jnp.logical_and(has_surface, away))(point.start)
        pl.when(jnp.logical_and(has_surface, jnp.logical_not(away)))(local_point.start)

    def forward(k):
        s, f, c = pieces[k]
        part = (s, f, pl.ds(c * per, per))
        return remote(own_ref.at[part], far_ref.at[part], fsend.at[k], frecv.at[k], other)

    @pl.when(y == 0)
    def _():
        for k, (s, f, c) in enumerate(pieces):
            part = own_ref.at[s, f, pl.ds(c * per, per)]
            away = differs((c, s, m * fields + f), me)
            arrival = remote(part, part, send.at[0], recv.at[k], me)
            pl.when(away)(arrival.wait_recv)
            own = pltpu.make_async_copy(part, part, loc.at[0])
            pl.when(jnp.logical_not(away))(own.wait)
            forward(k).start()
        for s in range(comps):
            away = differs((0, s, m * fields), me)
            arrival = remote(score_ref.at[s], score_ref.at[s], psend.at[0], precv.at[s], me)
            pl.when(away)(arrival.wait_recv)
            own = pltpu.make_async_copy(p_ref, score_ref.at[s], loc.at[1])
            pl.when(jnp.logical_not(away))(own.wait)
        for k in range(len(pieces)):
            forward(k).wait()

    for j in range(tiles):
        device, copy, local, point, local_point = band(j)
        away = differs(device, me)
        pl.when(away)(copy.wait_send)
        pl.when(jnp.logical_and(has_surface, away))(point.wait_send)

    def clone(s, f):
        i = s * fields + f
        part = (s, f)
        return (
            remote(after.at[part], faro_ref.at[part], osend.at[i], orecv.at[i], other),
            pltpu.make_async_copy(after.at[part], new_ref.at[part], keep.at[i]),
        )

    @pl.when(y == 1)
    def _():
        load.wait()
        sea = land_ref[...] == 1

        def flux_arrives():
            for s in range(comps):
                away = differs((0, s, m * fields), me)
                arrival = remote(flux.at[s], flux.at[s], ssend.at[0], srecv.at[s], me)
                pl.when(away)(arrival.wait_recv)
                part = x_ref.at[0, pl.ds(0, rows), :]
                own = pltpu.make_async_copy(part, flux.at[s], loc.at[3])
                pl.when(jnp.logical_not(away))(own.wait)

        def step(i, _):
            j, s = lax.div(i, comps), lax.rem(i, comps)
            f = lax.rem(j + 1, fields)
            pl.when(i == comps * (fields - 1))(flux_arrives)
            levels = before.shape[2]
            for u in range(levels):
                mixing = blend_ref[u, 0] * before[s, f, 0]
                for v in range(1, levels):
                    mixing = mixing + blend_ref[u, v] * before[s, f, v]
                value = before[s, f, u]
                forced = value + forcing_rate * jnp.tanh(mixing)
                ends = (
                    jnp.where(t == 0, 0.0, low_ref[s, f, u : u + 1]),
                    jnp.where(t == tiles - 1, 0.0, high_ref[s, f, u : u + 1]),
                )
                forced = forced + rate_ref[f] * laplacian_of(value, *ends)
                after[s, f, u] = jnp.where(sea, forced, value)

            @pl.when(f == 0)
            def _():
                value = before[s, 0, 0]
                extra = coupling_rate * (lookup(flux[s], donors_ref[...]) - value)
                result = after[s, 0, 0] + jnp.where(sea, extra, 0.0)
                after[s, 0, 0] = result
                sums[s] = weighted_sum(result, weight_ref[...], sums.shape[1:])

            across, own = clone(s, f)
            across.start()
            own.start()
            return 0

        lax.fori_loop(0, comps * fields, step, 0)
        mine = pltpu.make_async_copy(sums, part_ref.at[t], loc.at[4])
        mine.start()
        for j in range(tiles):
            pl.when(j != t)(share(j).start)
        mine.wait()
        for j in range(tiles):
            arrival = remote(part_ref.at[j], part_ref.at[j], qsend.at[0], qrecv.at[j], me)
            pl.when(j != t)(arrival.wait_recv)
            pl.when(j != t)(share(j).wait_send)
        for s in range(comps):
            for f in range(fields):
                across, own = clone(s, f)
                across.wait()
                own.wait()

    @pl.when(has_surface)
    def _():
        for j in range(tiles):
            away, copy, local = surface(j)
            pl.when(away)(copy.wait_send)


def laplacian_of(value, low, high):
    rows, lon_count = value.shape
    row = lax.broadcasted_iota(jnp.int32, (rows, lon_count), 0)
    north = jnp.where(row == 0, low, pltpu.roll(value, 1, 0))
    south = jnp.where(row == rows - 1, high, pltpu.roll(value, rows - 1, 0))
    east, west = pltpu.roll(value, 1, 1), pltpu.roll(value, lon_count - 1, 1)
    return south + north + east + west - 4.0 * value


def weighted_sum(value, weights, shape):
    total = jnp.sum(value * weights, axis=0, keepdims=True)
    total = jnp.sum(total, axis=1, keepdims=True) / value.shape[1]
    return jnp.broadcast_to(total, shape)


def call(kernel, collective_id, outs, sems, *args):
    return pl.pallas_call(
        kernel,
        out_shape=[
            jax.ShapeDtypeStruct(out.shape, out.dtype)
            if hasattr(out, "dtype")
            else jax.ShapeDtypeStruct(out, jnp.float32)
            for out in outs
        ],
        in_specs=[pl.BlockSpec(memory_space=pl.ANY)] * len(args),
        out_specs=[pl.BlockSpec(memory_space=pl.ANY)] * len(outs),
        scratch_shapes=[pltpu.SemaphoreType.DMA((n,)) for n in sems],
        compiler_params=pltpu.CompilerParams(collective_id=collective_id, has_side_effects=True),
    )(*args)


def matmul(a, b):
    return jnp.dot(a, b, precision=precise, preferred_element_type=jnp.float32)


def split(value):
    high = value.astype(jnp.bfloat16)
    return high, (value - high.astype(jnp.float32)).astype(jnp.bfloat16)


def split_table(table):
    high = table.astype(jnp.bfloat16)
    low = (table - high.astype(np.float32)).astype(jnp.bfloat16)
    return jnp.asarray(high), jnp.asarray(low)


def dot3(value, high_ref, low_ref):
    high, low = split(value)
    total = jnp.dot(high, low_ref[...], preferred_element_type=jnp.float32)
    total = total + jnp.dot(low, high_ref[...], preferred_element_type=jnp.float32)
    return total + jnp.dot(high, high_ref[...], preferred_element_type=jnp.float32)


def lookup(surface, donors):
    lon_count = surface.shape[-1]
    offset = donors - lax.broadcasted_iota(jnp.int32, donors.shape, 1)
    offset = jnp.where(offset > lon_count // 2, offset - lon_count, offset)
    offset = jnp.where(offset < -(lon_count // 2), offset + lon_count, offset)
    result = surface
    for shift in (-1, 1, 2, 3, 4):
        moved = pltpu.roll(surface, (-shift) % lon_count, 1)
        result = jnp.where(offset == shift, moved, result)
    return result


def whole_spec(array):
    zeros = (0,) * array.ndim
    return pl.BlockSpec(array.shape, lambda *_: zeros)


def scalar_spec():
    return pl.BlockSpec(memory_space=pltpu.SMEM)


def state_spec(shape):
    zeros = (0,) * (len(shape) - 2)
    return pl.BlockSpec((1, 1) + tuple(shape[2:]), lambda s, f, *_: (s, f) + zeros)


large = pltpu.CompilerParams(vmem_limit_bytes=60 * 1024 * 1024)


def air_last_kernel(inside_ref, near_ref, own_ref, far_ref, high_ref, low_ref, out_ref):
    near = near_ref[pl.program_id(0)] == 1
    levels, rows, waves = own_ref.shape[2:]
    coefs = jnp.where(near, own_ref[0, 0], far_ref[0, 0]).reshape(levels * rows, waves)
    out_ref[0, 0] = dot3(coefs, high_ref, low_ref).reshape(out_ref.shape[2:])


def sea_last_kernel(inside_ref, near_ref, own_ref, far_ref, out_ref):
    near = near_ref[pl.program_id(0)] == 1
    out_ref[0, 0] = jnp.where(near, own_ref[0, 0], far_ref[0, 0])


def resampled(kernel, inside, near, own, far, tables, lon_count):
    shape = own.shape[:-1] + (lon_count,)

    def parent(s, f, inside_ref, near_ref):
        return (inside_ref[s], f, 0, 0, 0)

    parent_spec = pl.BlockSpec((1, 1) + own.shape[2:], parent)
    return pl.pallas_call(
        kernel,
        grid_spec=pltpu.PrefetchScalarGridSpec(
            num_scalar_prefetch=2,
            grid=own.shape[:2],
            in_specs=[parent_spec, parent_spec] + [whole_spec(table) for table in tables],
            out_specs=state_spec(shape),
        ),
        out_shape=jax.ShapeDtypeStruct(shape, jnp.float32),
        compiler_params=large,
    )(inside, near, own, far, *tables)


def left3(high_ref, low_ref, value):
    high, low = split(value)
    total = jnp.dot(low_ref[...], high, preferred_element_type=jnp.float32)
    total = total + jnp.dot(high_ref[...], low, preferred_element_type=jnp.float32)
    return total + jnp.dot(high_ref[...], high, preferred_element_type=jnp.float32)


def filtered(value, squares_ref, rate_ref, forward, inverse):
    spectrum = left3(*forward, value) / (1.0 + rate_ref[0] * squares_ref[...])
    return left3(*inverse, spectrum)


def to_grid_kernel(x_ref, sq_ref, rate_ref, fh, fl, ih, il, gh, gl, out_ref):
    coefs = filtered(x_ref[0], sq_ref, rate_ref, (fh, fl), (ih, il))
    out_ref[0] = dot3(coefs, gh, gl)


def to_coefs_kernel(
    x_ref,
    o_ref,
    sst_ref,
    here_ref,
    there_ref,
    flag_ref,
    w_ref,
    sq_ref,
    rate_ref,
    fh,
    fl,
    ih,
    il,
    gh,
    gl,
    out_ref,
    sum_ref,
    forced,
):
    per = x_ref.shape[0]
    u = pl.program_id(0)
    mixing = here_ref[u, 0] * x_ref[0] + there_ref[u, 0] * o_ref[0]
    for v in range(1, per):
        mixing = mixing + here_ref[u, v] * x_ref[v] + there_ref[u, v] * o_ref[v]
    forced[...] = x_ref[u] + forcing_rate * jnp.tanh(mixing)

    @pl.when(jnp.logical_and(u == 0, flag_ref[0] == 1))
    def _():
        forced[...] += coupling_rate * (sst_ref[...] - x_ref[0])

    coefs = dot3(forced[...], gh, gl)
    result = filtered(coefs, sq_ref, rate_ref, (fh, fl), (ih, il))
    out_ref[0] = result

    @pl.when(u == 0)
    def _():
        total = jnp.sum(result[:, : w_ref.shape[1]] * w_ref[...], axis=0, keepdims=True)
        total = jnp.sum(total, axis=1, keepdims=True)
        sum_ref[...] = jnp.broadcast_to(total, sum_ref.shape)


def level_spec(shape):
    return pl.BlockSpec((1,) + tuple(shape[1:]), lambda u: (u, 0, 0))


def to_grid(value, squares, rate, tables, lon_count):
    shape = value.shape[:2] + (lon_count,)
    return pl.pallas_call(
        to_grid_kernel,
        grid=value.shape[:1],
        out_shape=jax.ShapeDtypeStruct(shape, jnp.float32),
        in_specs=[level_spec(value.shape), whole_spec(squares), scalar_spec()]
        + [whole_spec(table) for table in tables],
        out_specs=level_spec(shape),
        compiler_params=large,
    )(value, squares, rate, *tables)


def to_coefs(state, other, sst, mine, theirs, flag, weights, squares, rate, tables):
    shape = state.shape[:2] + (squares.shape[1],)
    return pl.pallas_call(
        to_coefs_kernel,
        grid=state.shape[:1],
        out_shape=[
            jax.ShapeDtypeStruct(shape, jnp.float32),
            jax.ShapeDtypeStruct((8, 128), jnp.float32),
        ],
        in_specs=[whole_spec(state), whole_spec(other), whole_spec(sst)]
        + [scalar_spec()] * 3
        + [whole_spec(weights), whole_spec(squares), scalar_spec()]
        + [whole_spec(table) for table in tables],
        out_specs=[level_spec(shape), pl.BlockSpec((8, 128), lambda u: (0, 0))],
        scratch_shapes=[pltpu.VMEM(state.shape[1:], jnp.float32)],
        compiler_params=large,
    )(state, other, sst, mine, theirs, flag, weights, squares, rate, *tables)


def by_units(
    member_state,
    layer_blend_operator,
    coefficient,
    interpolation_donor_meridians,
    land_sea,
    ancestry,
):
    member, component, tile = here()
    members, comps, tiles = (lax.axis_size(name) for name in ("member", "comp", "tile"))
    field = member_state[:, 0]
    slots, fields, levels, rows, lon_count = field.shape
    per = levels // members
    sizes = (members, comps, fields, tiles, rows)
    lon_basis, number = kept_lon_basis(lon_count)
    waves = lon_basis.shape[0]
    lon_columns = np.ascontiguousarray(lon_basis.T)
    lat_basis = lat_table()
    lat_tables = split_table(lat_basis) + split_table(np.ascontiguousarray(lat_basis.T))
    weights = row_weights()
    weight_total = float(weights.sum())
    order = np.arange(MODES).astype(np.float32)
    squares = order[:, None] ** 2 + number[None, :] ** 2
    squares = jnp.asarray((squares / np.float32(MODES * MODES)).astype(np.float32))
    air_weights = np.zeros((LAT, 128), np.float32)
    air_weights[:, 0] = weights * lon_basis[0, 0] / weight_total
    my_weights = lax.dynamic_slice_in_dim(jnp.asarray(weights[:, None]), tile * rows, rows)

    is_air = component == 0
    blend = layer_blend_operator[0]
    rate = coefficient[0]
    donors = interpolation_donor_meridians[0]
    anywhere = pl.BlockSpec(memory_space=pl.ANY)
    inside = pl.BlockSpec(memory_space=pltpu.VMEM)
    halo = (slots, fields, levels, lon_count)
    surface = (slots, rows, lon_count)
    coefs_shape = (slots, fields, levels, rows, waves)
    out_shapes = [(per, LAT, waves), (LAT, lon_count), field.shape, halo, halo]
    out_shapes += [blend.shape, coefficient.shape]
    scratch = [field.shape, field.shape, coefs_shape, coefs_shape[1:]]
    scratch += [(levels * rows, lon_count), surface]
    later = [surface, (2, slots, fields, 2, levels, lon_count), halo, halo]
    pieces = members * fields
    sems = (2, slots + 3, slots + 3, 2, 2, pieces, pieces, pieces, comps, tiles, tiles, 2, 2, 2)
    gathered, sst, ocean, low, high, other_blend, other_rate = pl.pallas_call(
        functools.partial(first_kernel, sizes),
        out_shape=[jax.ShapeDtypeStruct(shape, jnp.float32) for shape in out_shapes],
        in_specs=[anywhere, inside, inside]
        + [scalar_spec()] * 2
        + [anywhere] * 2
        + [inside] * 2,
        out_specs=[anywhere] * len(out_shapes),
        scratch_shapes=[pltpu.VMEM(shape, jnp.float32) for shape in scratch]
        + [pltpu.VMEM(donors.shape, jnp.int32)]
        + [pltpu.VMEM(shape, jnp.float32) for shape in later]
        + [pltpu.SemaphoreType.DMA((n,)) for n in sems],
        compiler_params=pltpu.CompilerParams(
            collective_id=0, has_side_effects=True, vmem_limit_bytes=60 * 1024 * 1024
        ),
    )(
        field,
        donors,
        land_sea,
        blend,
        coefficient,
        blend,
        coefficient,
        *split_table(lon_columns),
    )
    air_blend = jnp.where(is_air, blend, other_blend)
    air_rate = jnp.where(is_air, rate, other_rate[0])
    unit_field = tile % fields
    unit_rate = lax.dynamic_slice_in_dim(air_rate, unit_field, 1)
    state = to_grid(
        gathered, squares, unit_rate, lat_tables + split_table(lon_basis), lon_count
    )
    (other_state,) = call(
        functools.partial(swap_kernel, sizes), 1, [(per, LAT, lon_count)], (1, 1), state
    )
    mine = lax.dynamic_slice_in_dim(air_blend, member * per, per)
    mine_own = lax.dynamic_slice_in_dim(mine, member * per, per, axis=1)
    mine_other = lax.dynamic_slice_in_dim(mine, (1 - member) * per, per, axis=1)
    flag = jnp.logical_and(member == 0, unit_field == 0).astype(jnp.int32).reshape(1)
    back, air_point = to_coefs(
        state,
        other_state,
        sst,
        mine_own,
        mine_other,
        flag,
        jnp.asarray(air_weights),
        squares,
        unit_rate,
        lat_tables + split_table(lon_columns),
    )

    count = slots * fields * members
    out_shapes = [coefs_shape, coefs_shape, (slots, 8, 128)]
    out_shapes += [field.shape, field.shape, (tiles, slots, 8, 128)]
    scratch = [field.shape, field.shape, (slots, rows, lon_count), (slots, 8, 128)]
    sems = (tiles, count, count, count, tiles, comps, 5)
    sems += (slots * fields,) * 3 + (tiles, tiles, tiles, comps)
    own, far, air_scores, ocean, far_ocean, sea_parts = pl.pallas_call(
        functools.partial(return_kernel, sizes),
        out_shape=[jax.ShapeDtypeStruct(shape, jnp.float32) for shape in out_shapes],
        in_specs=[anywhere] * 4 + [inside] * 5 + [scalar_spec()] * 2,
        out_specs=[anywhere] * len(out_shapes),
        scratch_shapes=[pltpu.VMEM(shape, jnp.float32) for shape in scratch]
        + [pltpu.SemaphoreType.DMA((n,)) for n in sems],
        compiler_params=pltpu.CompilerParams(
            collective_id=2, has_side_effects=True, vmem_limit_bytes=60 * 1024 * 1024
        ),
    )(back, air_point, state, ocean, low, high, donors, land_sea, my_weights, blend, rate)
    parents = lax.dynamic_slice_in_dim(ancestry, member * slots, slots)

    inside = parents % slots
    near = (parents // slots == member).astype(jnp.int32)

    def air_last(_):
        grid = resampled(
            air_last_kernel, inside, near, own, far, split_table(lon_basis), lon_count
        )
        return grid.reshape(member_state.shape), air_scores[:, 0, :1]

    def sea_last(_):
        score = jnp.sum(sea_parts[:, :, 0, :1], axis=0) / weight_total
        states = resampled(sea_last_kernel, inside, near, ocean, far_ocean, (), lon_count)
        return states.reshape(member_state.shape), score

    return lax.cond(is_air, air_last, sea_last, 0)


def by_bands(
    member_state,
    layer_blend_operator,
    coefficient,
    interpolation_donor_meridians,
    land_sea,
    ancestry,
):
    slot_count = member_state.shape[0]
    component = lax.axis_index("comp")
    tile_index = lax.axis_index("tile")
    tile_count = lax.axis_size("tile")
    row_count = member_state.shape[4]
    lon_count = member_state.shape[5]
    lon_table, number = kept_lon_basis(lon_count)
    lon_basis = jnp.asarray(lon_table)
    local_modes = lon_table.shape[0] // tile_count
    my_numbers = lax.dynamic_slice_in_dim(jnp.asarray(number), tile_index * local_modes, local_modes)
    lat_basis = jnp.asarray(lat_table())
    order = jnp.arange(MODES, dtype=jnp.int32).astype(jnp.float32)
    sea_cells = land_sea[None, None] == 1
    diffusivity = coefficient[0][:, None, None, None]
    weights = row_weights()
    my_weights = lax.dynamic_slice_in_dim(jnp.asarray(weights), tile_index * row_count, row_count)
    weight_total = float(weights.sum())
    stepped_list = []
    partial_list = []
    for slot in range(slot_count):
        field = member_state[slot, 0]
        for _ in range(STEPS):
            surface = field[0, 0]
            partner = partner_2(surface, "comp", 0)
            received = donor_lookup(partner, interpolation_donor_meridians[0])
            mixing = jnp.einsum("uv,fvjx->fujx", layer_blend_operator[0], field, precision=precise)
            forced = field + forcing_rate * jnp.tanh(mixing)
            forced = forced.at[0, 0].add(coupling_rate * (received - surface))
            spectral_gain = 1.0 / (
                1.0
                + coefficient[0][:, None, None]
                * (order[None, None, :] ** 2 + my_numbers[None, :, None] ** 2)
                / (MODES * MODES)
            )
            fourier = jnp.einsum("fvjx,qx->fvjq", forced, lon_basis, precision=precise)
            spectrum = jnp.einsum(
                "lj,fkjq->fkql",
                lat_basis,
                lax.all_to_all(fourier, "tile", split_axis=3, concat_axis=2, tiled=True),
                precision=precise,
            )
            spectrum = spectrum * spectral_gain[:, None]
            returned = jnp.einsum("lj,fkql->fkjq", lat_basis, spectrum, precision=precise)
            filtered = lax.all_to_all(returned, "tile", split_axis=2, concat_axis=3, tiled=True)
            block_atm = jnp.einsum("fvjq,qx->fvjx", filtered, lon_basis, precision=precise)
            padded = padded_2(field, (("tile", 2),), 1)
            laplacian = (
                padded[:, :, 2:]
                + padded[:, :, :-2]
                + jnp.roll(field, 1, axis=3)
                + jnp.roll(field, -1, axis=3)
                - 4.0 * field
            )
            new_ocn = jnp.where(sea_cells, forced + diffusivity * laplacian, field)
            field = jnp.where(component == 0, block_atm, new_ocn)
        stepped_list.append(field)
        partial_list.append(jnp.sum(jnp.mean(field[0, 0], axis=1) * my_weights))
    local_states = jnp.stack(stepped_list)
    region_sums = lax.psum(jnp.stack(partial_list), "tile")
    region_score = (region_sums / weight_total).reshape(slot_count, 1)
    member_index = lax.axis_index("member")
    my_parents = lax.dynamic_slice_in_dim(ancestry, member_index * slot_count, slot_count)
    gathered = lax.all_gather(local_states, "member", axis=0, tiled=True)
    chosen = jnp.take(gathered, my_parents, axis=0)
    return (chosen[:, None], region_score)


def local(member_state, *others):
    members, comps, tiles = (lax.axis_size(name) for name in ("member", "comp", "tile"))
    slots, _, fields, levels, rows, _ = member_state.shape
    fits = members == 2 and comps == 2 and slots == comps and tiles == members * fields
    if fits and levels % members == 0 and rows % 8 == 0:
        return by_units(member_state, *others)
    return by_bands(member_state, *others)


def solution(mesh):
    return jax.shard_map(
        local,
        mesh=mesh,
        in_specs=(
            P("member", "comp", None, None, "tile", None),
            P("comp", None, None),
            P("comp", None),
            P("comp", "tile", None),
            P("tile", None),
            P(),
        ),
        out_specs=(P("member", "comp", None, None, "tile", None), P("member", "comp")),
        check_vma=False,
    )
```
